32 devices in a mesh: scene: 2 (over x), pulse: 16 (over z, y, core).
Axes of the slice: x: 2, y: 2, z: 4, core: 2. Of those that a mesh axis runs over, the one named last changes fastest.
Arguments:
- beams: bfloat16 [2, 2048, 4096], P(None, ('scene', 'pulse')), parts along dimension 1, may hold values from -6 to 6
- ukern: bfloat16 [2, 32], replicated, may hold values from -1 to 1
- rkern: float32 [16, 4], replicated, may hold values from -3 to 3
- angles: float32 [4, 2, 128], replicated, may hold values from -3.140625 to 3.140625
- taps: int32 [4, 2048], P(None, ('scene', 'pulse')), parts along dimension 1, may hold values from 0 to 15
- shifts: int32 [4, 16], replicated, may hold values from -48 to 48
- half_table: int32 [4, 16], replicated, may hold values from 0 to 1, as said below
Outputs:
- merged: bfloat16 [2, 2048, 4096], P(None, ('scene', 'pulse')), parts along dimension 1
The draws below stay inside these ranges and needn't reach their ends.
There are 2 independent parts, one for each index of `scene`. The reference program is written for one: setup_inputs(seed, part) draws one part's arguments, and reference() takes and returns one part's arrays. A program takes and returns all parts, laid end to end along the dimension named above; an argument that names none is the same for every part. Nothing has to cross between parts.
Inputs may be any that keep to these rules, and one draw needn't show every extreme that they name: half_table[l, s] + half_table[l, s XOR 2**l] == 1 for every level l and block s.
All inputs are finite; a program needn't handle non-finite values.
Results may differ from the reference program's by a relative error of at most 0.0074.
Values may be sent and summed in bfloat16 or wider, within the bound.
No kernel may reach another device: no remote copies, remote signals or barrier semaphores. Data moves between devices by JAX's collectives and lax.ppermute only.
A program may use at most 64 MiB of HBM per device.

```python
import jax
import jax.numpy as jnp
from jax import lax

R = 4096
BEAMS = 64
UTAPS = 32
RTAPS = 4
PHASES = 16
SHIFT = 48
LEVELS = 4
NSUB = 16
ALLBEAMS = 1024


def draw_half_table(key, part):
    coins = jax.random.randint(jax.random.fold_in(key, 7), (LEVELS, NSUB), 0, 2).astype(jnp.int32)
    index = jnp.arange(NSUB, dtype=jnp.int32)
    rows = []
    for level in range(LEVELS):
        lower = jnp.bitwise_and(index, jnp.int32(NSUB - 1 - (1 << level)))
        bit = jnp.bitwise_and(jnp.right_shift(index, level), 1)
        rows.append(jnp.bitwise_xor(coins[level][lower], bit))
    return jnp.stack(rows).astype(jnp.int32)


def set_ends(array, key, least, largest):
    longest = array.shape.index(max(array.shape))
    spots = []
    for shift in (0, 1):
        where = [jax.random.randint(jax.random.fold_in(key, axis), (), 0, length) for axis, length in enumerate(array.shape)]
        where[longest] = (where[longest] + shift) % array.shape[longest]
        spots.append(tuple(where))
    return array.at[spots[0]].set(least).at[spots[1]].set(largest)


def shard_levels(stream_key, dims, shards, low, top_value):
    level, own = 1.0, jax.random.fold_in(stream_key, 6)
    for position, shards_of in shards:
        heights = jnp.exp(jax.random.uniform(jax.random.fold_in(own, position), (shards_of,), jnp.float32, low / len(shards), top_value / len(shards)))
        level = level * jnp.repeat(heights, dims[position] // shards_of).reshape([-1 if axis == position else 1 for axis in range(len(dims))])
    return level


def centred(key, extent, scale, reach, split=(), held_as=jnp.bfloat16):
    values = jax.random.normal(key, extent, jnp.float32) * scale
    if len(split) > 0:
        values = shard_levels(key, extent, split, -0.22, 0.18) * values
    return jnp.clip(values, min=-reach, max=reach).astype(held_as)


def setup_inputs(seed: int = 0, part: int = 0) -> dict:
    keys = jax.random.split(jax.random.key(seed), 8)
    part_splits = jax.random.split(jax.random.fold_in(keys[7], part), 8)
    return {
        "beams": centred(part_splits[0], (2, ALLBEAMS, R), 1.0, 6.0, ((1, 16),)),
        "ukern": centred(keys[1], (2, UTAPS), UTAPS ** -0.5, 1.0),
        "rkern": centred(keys[2], (PHASES, RTAPS), RTAPS ** -0.5, 3.0, (), jnp.float32),
        "angles": jnp.clip(jax.random.uniform(keys[3], (LEVELS, 2, 2 * BEAMS), jnp.float32, -3.140625, 3.140625), -3.140625, 3.140625),
        "taps": set_ends(jax.random.randint(part_splits[4], (LEVELS, ALLBEAMS), 0, PHASES), jax.random.fold_in(part_splits[4], 1), 0, PHASES - 1).astype(jnp.int32),
        "shifts": set_ends(jax.random.randint(keys[5], (LEVELS, NSUB), -SHIFT, SHIFT + 1), jax.random.fold_in(keys[5], 1), -SHIFT, SHIFT).astype(jnp.int32),
        "half_table": draw_half_table(jax.random.fold_in(keys[7], 71), part),
    }


def band_matrix(ukern, half, count, utaps):
    width = count // 2 + utaps
    local = jnp.arange(count, dtype=jnp.int32)
    rows = half * count + local
    cols = half * (count // 2) + jnp.arange(width, dtype=jnp.int32)
    offset = cols[None, :] - rows[:, None] // 2 - 1
    kernel = jnp.where((local % 2 == 0)[:, None], ukern[0].astype(jnp.float32)[None, :], ukern[1].astype(jnp.float32)[None, :])
    picks = (offset[:, :, None] == jnp.arange(utaps, dtype=jnp.int32)[None, None, :]).astype(jnp.float32)
    return jnp.sum(picks * kernel[:, None, :], axis=2)


def tap_weights(tap_row, rkern):
    onehot = (tap_row[:, None] == jnp.arange(rkern.shape[0], dtype=jnp.int32)[None, :]).astype(jnp.float32)
    return jnp.dot(onehot, rkern, precision=lax.Precision.HIGHEST, preferred_element_type=jnp.float32)


def child_term(range_band, sample_window, weights, shift, segment):
    blended_beam = jnp.einsum("dp,upe->ude", range_band, sample_window, precision=lax.Precision.HIGHEST, preferred_element_type=jnp.float32)
    length = blended_beam.shape[2]
    margin = SHIFT + RTAPS
    padded = jnp.pad(blended_beam, ((0, 0), (0, 0), (margin, margin)))
    shifted = jnp.zeros(blended_beam.shape, jnp.float32)
    for tap in range(RTAPS):
        piece = lax.dynamic_slice_in_dim(padded, margin + shift + tap - 1, length, 2)
        shifted = shifted + weights[None, :, tap, None] * piece
    cosine = jnp.cos(segment)[:, None]
    sine = jnp.sin(segment)[:, None]
    real_part = cosine * shifted[0] - sine * shifted[1]
    imag_part = sine * shifted[0] + cosine * shifted[1]
    return jnp.stack([real_part, imag_part])


def reference(beams, ukern, rkern, angles, taps, shifts, half_table):
    current = beams
    for level in range(LEVELS):
        def one_block(block_number):
            partner = jnp.bitwise_xor(block_number, 1 << level)
            half = half_table[level, block_number]
            range_band = band_matrix(ukern, half, BEAMS, UTAPS)
            weights = tap_weights(lax.dynamic_slice_in_dim(taps[level], block_number * BEAMS, BEAMS, 0), rkern)
            own_bit = jnp.bitwise_and(jnp.right_shift(block_number, level), 1)
            total = jnp.zeros((2, BEAMS, R), jnp.float32)
            for child, bit in ((block_number, own_bit), (partner, 1 - own_bit)):
                block = lax.dynamic_slice_in_dim(current, child * BEAMS, BEAMS, 1).astype(jnp.float32)
                padded = jnp.pad(block, ((0, 0), (UTAPS // 2, UTAPS // 2), (0, 0)))
                sample_window = lax.dynamic_slice_in_dim(padded, half * (BEAMS // 2), BEAMS // 2 + UTAPS, 1)
                row = jnp.where(bit == 0, angles[level, 0], angles[level, 1])
                segment = lax.dynamic_slice_in_dim(row, half * BEAMS, BEAMS, 0)
                total = total + child_term(range_band, sample_window, weights, shifts[level, child], segment)
            return (0.70710678 * total).astype(jnp.bfloat16)

        blocks = lax.map(one_block, jnp.arange(NSUB, dtype=jnp.int32))
        current = jnp.transpose(blocks, (1, 0, 2, 3)).reshape(2, NSUB * BEAMS, R)
    return current
```

```python
import functools

import jax
import jax.numpy as jnp
from jax import lax
from jax.experimental import pallas as pl
from jax.experimental.pallas import tpu as pltpu
from jax.sharding import PartitionSpec as P

LANES = 128
TILE = 256
CHUNKS = 4
SCALE = 0.70710678


def prep_kernel(levels, beams, utaps, half_ref, rkern_ref, angles_ref, taps_ref, ukern_ref,
                mix_ref, band_ref, flat_ref):
    window = beams // 2 + utaps // 2
    phases, rtaps = rkern_ref.shape
    myself = lax.axis_index("pulse")
    lane = lax.broadcasted_iota(jnp.int32, (1, 2 * beams), 1)
    first = lane < beams
    beam = jnp.where(first, lane, lane - beams)
    depth = beams // 2 + utaps
    row = lax.broadcasted_iota(jnp.int32, (depth, 2 * beams), 0)
    offset = row - beam // 2 - 1
    band = jnp.zeros((depth, 2 * beams), jnp.float32)
    even = beam % 2 == 0
    for k in range(utaps):
        value = jnp.where(even, ukern_ref[0, k], ukern_ref[1, k])
        band = jnp.where(offset == k, value, band)
    band_ref[...] = band

    def one_level(level, carry):
        half = half_ref[level, myself]
        bit = lax.rem(lax.shift_right_logical(myself, level), 2)
        start = pl.multiple_of((1 - half) * (utaps // 2), 8)
        near = band_ref[pl.ds(start, window), :]
        chosen = taps_ref[pl.ds(level, 1), :]
        weights = []
        for tap in range(rtaps):
            weight = jnp.zeros((1, 2 * beams), jnp.float32)
            for phase in range(phases):
                weight = jnp.where(chosen == phase, rkern_ref[phase, tap], weight)
            weights.append(weight)
        for child in range(2):
            side = bit if child == 0 else 1 - bit
            angle = angles_ref[pl.ds(2 * level + side, 1), :]
            turned = pltpu.roll(angle, beams, 1)
            angle = jnp.where(first == (half == 0), angle, turned)
            cosine = SCALE * jnp.cos(angle)
            sine = SCALE * jnp.sin(angle)
            factors = (jnp.where(first, cosine, sine), jnp.where(first, -sine, cosine))
            for tap in range(rtaps):
                for part in range(2):
                    place = ((child * rtaps + tap) * 2 + part) * window
                    flat_ref[place:place + window, :] = near * (factors[part] * weights[tap])
        for block in range(flat_ref.shape[0] // LANES):
            mixed = flat_ref[block * LANES:(block + 1) * LANES, :].T
            high = mixed.astype(jnp.bfloat16)
            low = (mixed - high.astype(jnp.float32)).astype(jnp.bfloat16)
            columns = pl.ds(block * LANES, LANES)
            mix_ref[level, 0:2 * beams, columns] = high
            mix_ref[level, 2 * beams:4 * beams, columns] = low
        return carry

    lax.fori_loop(0, levels, one_level, 0)


def mixing(ukern, rkern, angles, taps, half_table):
    levels = half_table.shape[0]
    beams = taps.shape[1]
    utaps = ukern.shape[1]
    window = beams // 2 + utaps // 2
    depth = 2 * rkern.shape[1] * 2 * window
    smem = pl.BlockSpec(memory_space=pltpu.SMEM)
    vmem = pl.BlockSpec(memory_space=pltpu.VMEM)
    return pl.pallas_call(
        functools.partial(prep_kernel, levels, beams, utaps),
        out_shape=jax.ShapeDtypeStruct((levels, 4 * beams, depth), jnp.bfloat16),
        in_specs=[smem, smem, vmem, vmem, smem],
        out_specs=vmem,
        scratch_shapes=[
            pltpu.VMEM((beams // 2 + utaps, 2 * beams), jnp.float32),
            pltpu.VMEM((depth, 2 * beams), jnp.float32),
        ],
        compiler_params=pltpu.CompilerParams(vmem_limit_bytes=24 * 2**20),
        name="mixing",
    )(
        half_table,
        rkern,
        angles.reshape(2 * levels, 2 * beams),
        jnp.concatenate([taps, taps], axis=1),
        ukern.astype(jnp.float32),
    )


def merge_kernel(level, plan, start, stop, length, beams, window, rtaps, last, *refs):
    half_ref, shift_ref, mix_ref = refs[:3]
    count = len(plan)
    own_refs, far_refs = refs[3:3 + count], refs[3 + count:3 + 2 * count]
    outs = refs[4 + 2 * count:]
    out_ref = outs[0]
    send_ref = None if last else outs[1]
    wide_ref, stack_ref, sem = outs[1 if last else 2:]
    myself = lax.axis_index("pulse")
    half = half_ref[level, myself]
    rows = pl.ds(pl.multiple_of(half * (beams - window), 16), window)
    base = start - LANES
    copies = []
    for number, (piece, source, target, width) in enumerate(plan):
        for child, ref in ((0, own_refs[number]), (1, far_refs[number])):
            for part in range(2):
                taken = rows if child == 0 else pl.ds(0, window)
                copy = pltpu.make_async_copy(
                    ref.at[part, taken, pl.ds(source, width)],
                    wide_ref.at[child, part, :, pl.ds(target - base, width)],
                    sem.at[child, number, part],
                )
                copy.start()
                copies.append(copy)
    if base < 0:
        wide_ref[:, :, :, 0:LANES] = jnp.zeros((2, 2, window, LANES), jnp.bfloat16)
    if stop + LANES > length:
        wide_ref[:, :, :, stop - base:stop - base + LANES] = jnp.zeros(
            (2, 2, window, LANES), jnp.bfloat16
        )
    shifts = (shift_ref[level, myself], shift_ref[level, jnp.bitwise_xor(myself, 1 << level)])
    for copy in copies:
        copy.wait()
    span = stop - start
    tile = min(TILE, span)
    reach = tile + LANES

    def one_tile(step, carry):
        column = pl.multiple_of(jnp.minimum(step * tile, span - tile), LANES)
        for child in range(2):
            for tap in range(rtaps):
                shift = shifts[child] + (tap - 1 + LANES)
                whole = pl.multiple_of(column + shift // LANES * LANES, LANES)
                turn = lax.rem(reach - lax.rem(shift, LANES), reach)
                piece = wide_ref[child, :, :, pl.ds(whole, reach)].reshape(2 * window, reach)
                piece = pltpu.roll(piece, turn, 1)[:, :tile]
                place = (child * rtaps + tap) * 2 * window
                stack_ref[place:place + 2 * window, :] = piece
        both = jnp.dot(mix_ref[0], stack_ref[...], preferred_element_type=jnp.float32)
        total = (both[:2 * beams] + both[2 * beams:]).astype(jnp.bfloat16)
        out_ref[:, :, pl.ds(column, tile)] = total.reshape(2, beams, tile)
        return carry

    lax.fori_loop(0, pl.cdiv(span, tile), one_tile, 0)
    if not last:
        following = half_ref[level + 1, myself]
        other = pl.ds(pl.multiple_of((1 - following) * (beams - window), 16), window)
        send_ref[...] = out_ref[:, other, :]


def pieces_of(bounds, start, stop):
    found = []
    for chunk in range(len(bounds) - 1):
        low, high = max(bounds[chunk], start), min(bounds[chunk + 1], stop)
        if low < high:
            found.append((chunk, low - bounds[chunk], low, high - low))
    return found


def merge(level, levels, half_table, shifts, mix, own, far, bounds, start, stop, sizes, before):
    beams, window, rtaps, length = sizes
    last = level == levels - 1
    plan = pieces_of(bounds, max(start - LANES, 0), min(stop + LANES, length))
    span = stop - start
    smem = pl.BlockSpec(memory_space=pltpu.SMEM)
    vmem = pl.BlockSpec(memory_space=pltpu.VMEM)
    anywhere = pl.BlockSpec(memory_space=pl.ANY)
    depth = mix.shape[2]
    out_shape = [jax.ShapeDtypeStruct((2, beams, span), jnp.bfloat16)]
    if not last:
        out_shape.append(jax.ShapeDtypeStruct((2, window, span), jnp.bfloat16))
    return pl.pallas_call(
        functools.partial(
            merge_kernel, level, plan, start, stop, length, beams, window, rtaps, last
        ),
        grid=(1,),
        out_shape=out_shape,
        in_specs=[smem, smem, pl.BlockSpec((1, 4 * beams, depth), lambda i: (level, 0, 0))]
        + [anywhere] * (2 * len(plan) + 1),
        out_specs=[vmem] * len(out_shape),
        scratch_shapes=[
            pltpu.VMEM((2, 2, window, span + 2 * LANES), jnp.bfloat16),
            pltpu.VMEM((depth, min(TILE, span)), jnp.bfloat16),
            pltpu.SemaphoreType.DMA((2, len(plan), 2)),
        ],
        compiler_params=pltpu.CompilerParams(vmem_limit_bytes=24 * 2**20),
        cost_estimate=pl.CostEstimate(
            flops=2 * 4 * beams * depth * span,
            bytes_accessed=8 * beams * span * 2,
            transcendentals=0,
        ),
        name=f"merge_{level}",
    )(
        half_table,
        shifts,
        mix,
        *[own[piece[0]] for piece in plan],
        *[far[piece[0]] for piece in plan],
        before,
    )


def merge_order(levels, bounds):
    sending = [8.0] + [18.0] * (levels - 2) + [36.0]
    working, fixed = 3.0, 1.0
    length = bounds[0][-1]
    ready = {}
    clock = 3.0
    link = [clock] * levels
    for chunk in range(CHUNKS):
        link[0] += sending[0] * (bounds[0][chunk + 1] - bounds[0][chunk]) / length
        ready[0, chunk] = link[0]
    order = []
    following = [0] * levels
    while len(order) < levels * CHUNKS:
        choices = [
            (ready[level, following[level]], -level, level)
            for level in range(levels)
            if (level, following[level]) in ready
        ]
        now = [choice for choice in choices if choice[0] <= clock]
        level = max(choice[2] for choice in now) if now else min(choices)[2]
        chunk = following[level]
        following[level] += 1
        order.append((level, chunk))
        width = (bounds[level + 1][chunk + 1] - bounds[level + 1][chunk]) / length
        clock = max(clock, ready[level, chunk]) + fixed + working * width
        if level < levels - 1:
            link[level + 1] = max(link[level + 1], clock) + sending[level + 1] * width
            ready[level + 1, chunk] = link[level + 1]
    return order


def from_partner(value, bit):
    mask = 1 << bit
    pairs = [(source, source ^ mask) for source in range(lax.axis_size("pulse"))]
    return lax.ppermute(value, "pulse", pairs)


def on_device(beams_in, ukern, rkern, angles, taps, shifts, half_table):
    beams, length = beams_in.shape[1:]
    utaps, rtaps = ukern.shape[1], rkern.shape[1]
    window = beams // 2 + utaps // 2
    levels = half_table.shape[0]
    sizes = (beams, window, rtaps, length)
    step = length // CHUNKS
    ends = [min((chunk + 1) * step, length) for chunk in range(CHUNKS)]
    bounds = [
        [0] + [min(end + (levels - level) * LANES, length) for end in ends]
        for level in range(levels + 1)
    ]
    half = half_table[0, lax.axis_index("pulse")]
    own = [beams_in[:, :, low:high] for low, high in zip(bounds[0][:-1], bounds[0][1:])]
    gap = beams - window
    send = [
        jnp.where(half == 0, piece[:, gap:gap + window], piece[:, :window]) for piece in own
    ]
    far = [from_partner(piece, 0) for piece in send]
    mix = mixing(ukern, rkern, angles, taps, half_table)
    owns = [own] + [[None] * CHUNKS for _ in range(levels)]
    fars = [far] + [[None] * CHUNKS for _ in range(levels - 1)]
    before = mix
    for level, chunk in merge_order(levels, bounds):
        start, stop = bounds[level + 1][chunk], bounds[level + 1][chunk + 1]
        done = merge(
            level, levels, half_table, shifts, mix, owns[level], fars[level], bounds[level],
            start, stop, sizes, before,
        )
        before = owns[level + 1][chunk] = done[0]
        if level < levels - 1:
            fars[level + 1][chunk] = from_partner(done[1], level + 1)
    return jnp.concatenate(owns[levels], axis=2)


def solution(mesh):
    in_specs = (
        P(None, ("scene", "pulse"), None),
        P(),
        P(),
        P(),
        P(None, ("scene", "pulse")),
        P(),
        P(),
    )
    out_specs = P(None, ("scene", "pulse"), None)
    return jax.shard_map(
        on_device, mesh=mesh, in_specs=in_specs, out_specs=out_specs, check_vma=False
    )
```

```python
import functools

import jax
import jax.numpy as jnp
from jax import lax
from jax.experimental import pallas as pl
from jax.experimental.pallas import tpu as pltpu
from jax.sharding import PartitionSpec as P

LANES = 128
TILE = 256
CHUNKS = 4
SCALE = 0.70710678


def prep_kernel(levels, beams, utaps, half_ref, rkern_ref, angles_ref, taps_ref, ukern_ref,
                mix_ref, band_ref, flat_ref):
    window = beams // 2 + utaps // 2
    phases, rtaps = rkern_ref.shape
    myself = lax.axis_index("pulse")
    lane = lax.broadcasted_iota(jnp.int32, (1, 2 * beams), 1)
    first = lane < beams
    beam = jnp.where(first, lane, lane - beams)
    depth = beams // 2 + utaps
    row = lax.broadcasted_iota(jnp.int32, (depth, 2 * beams), 0)
    offset = row - beam // 2 - 1
    band = jnp.zeros((depth, 2 * beams), jnp.float32)
    even = beam % 2 == 0
    for k in range(utaps):
        value = jnp.where(even, ukern_ref[0, k], ukern_ref[1, k])
        band = jnp.where(offset == k, value, band)
    band_ref[...] = band

    def one_level(level, carry):
        half = half_ref[level, myself]
        bit = lax.rem(lax.shift_right_logical(myself, level), 2)
        start = pl.multiple_of((1 - half) * (utaps // 2), 8)
        near = band_ref[pl.ds(start, window), :]
        chosen = taps_ref[pl.ds(level, 1), :]
        weights = []
        for tap in range(rtaps):
            weight = jnp.zeros((1, 2 * beams), jnp.float32)
            for phase in range(phases):
                weight = jnp.where(chosen == phase, rkern_ref[phase, tap], weight)
            weights.append(weight)
        for child in range(2):
            side = bit if child == 0 else 1 - bit
            angle = angles_ref[pl.ds(2 * level + side, 1), :]
            turned = pltpu.roll(angle, beams, 1)
            angle = jnp.where(first == (half == 0), angle, turned)
            cosine = SCALE * jnp.cos(angle)
            sine = SCALE * jnp.sin(angle)
            factors = (jnp.where(first, cosine, sine), jnp.where(first, -sine, cosine))
            for tap in range(rtaps):
                for part in range(2):
                    place = ((child * rtaps + tap) * 2 + part) * window
                    flat_ref[place:place + window, :] = near * (factors[part] * weights[tap])
        for block in range(flat_ref.shape[0] // LANES):
            mixed = flat_ref[block * LANES:(block + 1) * LANES, :].T
            high = mixed.astype(jnp.bfloat16)
            low = (mixed - high.astype(jnp.float32)).astype(jnp.bfloat16)
            columns = pl.ds(block * LANES, LANES)
            mix_ref[level, 0:2 * beams, columns] = high
            mix_ref[level, 2 * beams:4 * beams, columns] = low
        return carry

    lax.fori_loop(0, levels, one_level, 0)


def mixing(ukern, rkern, angles, taps, half_table):
    levels = half_table.shape[0]
    beams = taps.shape[1]
    utaps = ukern.shape[1]
    window = beams // 2 + utaps // 2
    depth = 2 * rkern.shape[1] * 2 * window
    smem = pl.BlockSpec(memory_space=pltpu.SMEM)
    vmem = pl.BlockSpec(memory_space=pltpu.VMEM)
    return pl.pallas_call(
        functools.partial(prep_kernel, levels, beams, utaps),
        out_shape=jax.ShapeDtypeStruct((levels, 4 * beams, depth), jnp.bfloat16),
        in_specs=[smem, smem, vmem, vmem, smem],
        out_specs=vmem,
        scratch_shapes=[
            pltpu.VMEM((beams // 2 + utaps, 2 * beams), jnp.float32),
            pltpu.VMEM((depth, 2 * beams), jnp.float32),
        ],
        compiler_params=pltpu.CompilerParams(vmem_limit_bytes=24 * 2**20),
        name="mixing",
    )(
        half_table,
        rkern,
        angles.reshape(2 * levels, 2 * beams),
        jnp.concatenate([taps, taps], axis=1),
        ukern.astype(jnp.float32),
    )


def merge_kernel(level, plan, start, stop, length, beams, window, rtaps, last, *refs):
    half_ref, shift_ref, mix_ref = refs[:3]
    count = len(plan)
    own_refs, far_refs = refs[3:3 + count], refs[3 + count:3 + 2 * count]
    outs = refs[4 + 2 * count:]
    out_ref = outs[0]
    send_ref = None if last else outs[1]
    wide_ref, even_ref, odd_ref = outs[1 if last else 2:]
    myself = lax.axis_index("pulse")
    half = half_ref[level, myself]
    rows = pl.ds(pl.multiple_of(half * (beams - window), 16), window)
    base = start - LANES
    for number, (piece, source, target, width) in enumerate(plan):
        for child, ref in ((0, own_refs[number]), (1, far_refs[number])):
            taken = rows if ref.shape[1] == beams else pl.ds(0, window)
            for part in range(2):
                wide_ref[child, part, :, target - base:target - base + width] = ref[
                    part, taken, source:source + width
                ]
    edge = jnp.zeros((2, 2, window, LANES), jnp.bfloat16)
    if base < 0:
        wide_ref[:, :, :, 0:LANES] = edge
    if stop + LANES > length:
        wide_ref[:, :, :, stop - base:stop - base + LANES] = edge
    shifts = (shift_ref[level, myself], shift_ref[level, jnp.bitwise_xor(myself, 1 << level)])
    span = stop - start
    tile = min(TILE, span)
    tiles = pl.cdiv(span, tile)
    lane = lax.broadcasted_iota(jnp.int32, (2 * window, LANES), 1).astype(jnp.int16)
    moves = []
    for child in range(2):
        for tap in range(rtaps):
            shift = shifts[child] + (tap - 1 + LANES)
            part_tile = lax.rem(shift, LANES)
            kept = jnp.full((2 * window, LANES), LANES - part_tile, jnp.int32).astype(jnp.int16)
            turn = lax.rem(LANES - part_tile, LANES)
            moves.append((child, tap, shift // LANES * LANES, turn, lane < kept))

    def column_of(step):
        return pl.multiple_of(jnp.minimum(step * tile, span - tile), LANES)

    def build(stack_ref, step):
        column = column_of(step)
        for child, tap, whole, turn, kept in moves:
            place = (child * rtaps + tap) * 2 * window
            held = None
            for block in range(tile // LANES + 1):
                at = pl.multiple_of(column + whole + block * LANES, LANES)
                piece = wide_ref[child, :, :, pl.ds(at, LANES)].reshape(2 * window, LANES)
                piece = pltpu.roll(piece, turn, 1)
                if block > 0:
                    columns = pl.ds((block - 1) * LANES, LANES)
                    stack_ref[place:place + 2 * window, columns] = jnp.where(kept, held, piece)
                held = piece

    def multiply(stack_ref, step):
        column = column_of(step)
        both = jnp.dot(mix_ref[level], stack_ref[...], preferred_element_type=jnp.float32)
        total = (both[:2 * beams] + both[2 * beams:]).astype(jnp.bfloat16)
        out_ref[:, :, pl.ds(column, tile)] = total.reshape(2, beams, tile)

    def two_tiles(pair, carry):
        build(odd_ref, 2 * pair + 1)
        multiply(even_ref, 2 * pair)
        build(even_ref, 2 * pair + 2)
        multiply(odd_ref, 2 * pair + 1)
        return carry

    build(even_ref, 0)
    lax.fori_loop(0, tiles // 2, two_tiles, 0)
    if tiles % 2 == 1:
        multiply(even_ref, tiles - 1)
    if not last:
        following = half_ref[level + 1, myself]
        other = pl.ds(pl.multiple_of((1 - following) * (beams - window), 16), window)
        send_ref[...] = out_ref[:, other, :]


def pieces_of(bounds, start, stop):
    found = []
    for chunk in range(len(bounds) - 1):
        low, high = max(bounds[chunk], start), min(bounds[chunk + 1], stop)
        if low < high:
            found.append((chunk, low - bounds[chunk], low, high - low))
    return found


def merge(level, levels, half_table, shifts, mix, own, far, bounds, start, stop, sizes, before):
    beams, window, rtaps, length = sizes
    last = level == levels - 1
    plan = pieces_of(bounds, max(start - LANES, 0), min(stop + LANES, length))
    span = stop - start
    smem = pl.BlockSpec(memory_space=pltpu.SMEM)
    vmem = pl.BlockSpec(memory_space=pltpu.VMEM)
    anywhere = pl.BlockSpec(memory_space=pl.ANY)
    depth = mix.shape[2]
    out_shape = [jax.ShapeDtypeStruct((2, beams, span), jnp.bfloat16)]
    if not last:
        out_shape.append(jax.ShapeDtypeStruct((2, window, span), jnp.bfloat16))
    return pl.pallas_call(
        functools.partial(
            merge_kernel, level, plan, start, stop, length, beams, window, rtaps, last
        ),
        out_shape=out_shape,
        in_specs=[smem, smem, vmem] + [vmem] * (2 * len(plan)) + [anywhere],
        out_specs=[vmem] * len(out_shape),
        scratch_shapes=[
            pltpu.VMEM((2, 2, window, span + 2 * LANES), jnp.bfloat16),
            pltpu.VMEM((depth, min(TILE, span)), jnp.bfloat16),
            pltpu.VMEM((depth, min(TILE, span)), jnp.bfloat16),
        ],
        compiler_params=pltpu.CompilerParams(vmem_limit_bytes=24 * 2**20),
        cost_estimate=pl.CostEstimate(
            flops=2 * 4 * beams * depth * span,
            bytes_accessed=8 * beams * span * 2,
            transcendentals=0,
        ),
        name=f"merge_{level}",
    )(
        half_table,
        shifts,
        mix,
        *[own[piece[0]] for piece in plan],
        *[far[piece[0]] for piece in plan],
        before,
    )


def merge_order(levels):
    places = [(level, chunk) for level in range(levels) for chunk in range(CHUNKS)]
    return sorted(places, key=lambda place: (place[0] + place[1], place[0]))


def from_partner(value, bit):
    mask = 1 << bit
    pairs = [(source, source ^ mask) for source in range(lax.axis_size("pulse"))]
    return lax.ppermute(value, "pulse", pairs)


def on_device(beams_in, ukern, rkern, angles, taps, shifts, half_table):
    beams, length = beams_in.shape[1:]
    utaps, rtaps = ukern.shape[1], rkern.shape[1]
    window = beams // 2 + utaps // 2
    levels = half_table.shape[0]
    sizes = (beams, window, rtaps, length)
    step = length // CHUNKS
    ends = [min((chunk + 1) * step, length) for chunk in range(CHUNKS)]
    bounds = [
        [0] + [min(end + (levels - level) * LANES, length) for end in ends]
        for level in range(levels + 1)
    ]
    bounds[0] = [0, length]
    mix = mixing(ukern, rkern, angles, taps, half_table)
    owns = [[beams_in]] + [[None] * CHUNKS for _ in range(levels)]
    fars = [[from_partner(beams_in, 0)]] + [[None] * CHUNKS for _ in range(levels - 1)]
    before = mix
    for level, chunk in merge_order(levels):
        start, stop = bounds[level + 1][chunk], bounds[level + 1][chunk + 1]
        done = merge(
            level, levels, half_table, shifts, mix, owns[level], fars[level], bounds[level],
            start, stop, sizes, before,
        )
        before = owns[level + 1][chunk] = done[0]
        if level < levels - 1:
            fars[level + 1][chunk] = from_partner(done[1], level + 1)
    return jnp.concatenate(owns[levels], axis=2)


def solution(mesh):
    in_specs = (
        P(None, ("scene", "pulse"), None),
        P(),
        P(),
        P(),
        P(None, ("scene", "pulse")),
        P(),
        P(),
    )
    out_specs = P(None, ("scene", "pulse"), None)
    return jax.shard_map(
        on_device, mesh=mesh, in_specs=in_specs, out_specs=out_specs, check_vma=False
    )
```

```python
import functools

import jax
import jax.numpy as jnp
from jax import lax
from jax.experimental import pallas as pl
from jax.experimental.pallas import tpu as pltpu
from jax.sharding import PartitionSpec as P

LANES = 128
TILE = 256
SCALE = 0.70710678


def prep_kernel(levels, beams, utaps, phases, rtaps, whole_ref, real_ref, mix_ref, plan_ref, band_ref, flat_ref):
    at_shifts, at_taps = levels, 2 * levels
    at_ukern, at_rkern = 2 * levels, 2 * levels + 2
    window = beams // 2 + utaps // 2
    myself = lax.axis_index("pulse")
    lane = lax.broadcasted_iota(jnp.int32, (1, 2 * beams), 1)
    first = lane < beams
    beam = jnp.where(first, lane, lane - beams)
    depth = beams // 2 + utaps
    row = lax.broadcasted_iota(jnp.int32, (depth, 2 * beams), 0)
    offset = row - beam // 2 - 1
    even = beam % 2 == 0
    halves = whole_ref[0:levels, :].astype(jnp.float32)
    shifts = whole_ref[at_shifts:at_shifts + levels, :].astype(jnp.float32)
    place = lax.broadcasted_iota(jnp.int32, (levels, LANES), 1)
    level_of = lax.broadcasted_iota(jnp.int32, (levels, LANES), 0)
    partner = jnp.bitwise_xor(myself, lax.shift_left(jnp.ones_like(level_of), level_of))

    def pick(table, index):
        return jnp.sum(jnp.where(place == index, table, 0.0), axis=1, keepdims=True)

    half_of = pick(halves, myself)
    after_of = jnp.concatenate([half_of[1:], half_of[:1]], axis=0)
    near_of = pick(shifts, myself) + LANES
    far_of = pick(shifts, partner) + LANES
    codes = ((half_of * 2 + after_of) * 256 + near_of) * 256 + far_of
    for level in range(levels):
        plan_ref[level] = jnp.broadcast_to(codes[level:level + 1, :], (8, LANES))
    kernel = real_ref[at_ukern:at_ukern + 2, :]
    band = jnp.zeros((depth, 2 * beams), jnp.float32)
    for k in range(utaps):
        value = jnp.where(even, kernel[0:1, k:k + 1], kernel[1:2, k:k + 1])
        band = jnp.where(offset == k, value, band)
    band_ref[...] = band
    table = real_ref[at_rkern:at_rkern + rtaps, :]
    for level in range(levels):
        low_half = half_of[level:level + 1, :] == 0.0
        bit = lax.rem(lax.shift_right_logical(myself, level), 2)
        near = jnp.where(
            low_half, band_ref[utaps // 2:utaps // 2 + window, :], band_ref[0:window, :]
        )
        chosen = whole_ref[at_taps + level:at_taps + level + 1, :]
        weights = []
        for tap in range(rtaps):
            weight = jnp.zeros((1, 2 * beams), jnp.float32)
            for phase in range(phases):
                weight = jnp.where(
                    chosen == phase, table[tap:tap + 1, phase:phase + 1], weight
                )
            weights.append(weight)
        for child in range(2):
            side = bit if child == 0 else 1 - bit
            angle = real_ref[pl.ds(2 * level + side, 1), :]
            turned = pltpu.roll(angle, beams, 1)
            angle = jnp.where(first == low_half, angle, turned)
            cosine = SCALE * jnp.cos(angle)
            sine = SCALE * jnp.sin(angle)
            factors = (jnp.where(first, cosine, sine), jnp.where(first, -sine, cosine))
            for tap in range(rtaps):
                for part in range(2):
                    place = ((child * rtaps + tap) * 2 + part) * window
                    flat_ref[place:place + window, :] = near * (factors[part] * weights[tap])
        for block in range(flat_ref.shape[0] // LANES):
            mixed = flat_ref[block * LANES:(block + 1) * LANES, :].T
            high = mixed.astype(jnp.bfloat16)
            low = (mixed - high.astype(jnp.float32)).astype(jnp.bfloat16)
            columns = pl.ds(block * LANES, LANES)
            mix_ref[level, 0:2 * beams, columns] = high
            mix_ref[level, 2 * beams:4 * beams, columns] = low


def stacked(height, pieces):
    total = jnp.zeros((height, LANES), pieces[0][0].dtype)
    for piece, top, left in pieces:
        below, right = height - top - piece.shape[0], LANES - left - piece.shape[1]
        zero = jnp.zeros((), piece.dtype)
        total = total + lax.pad(piece, zero, ((top, below, 0), (left, right, 0)))
    return total


def mixing(ukern, rkern, angles, taps, shifts, half_table):
    levels = half_table.shape[0]
    beams = taps.shape[1]
    utaps = ukern.shape[1]
    phases, rtaps = rkern.shape
    window = beams // 2 + utaps // 2
    depth = 2 * rtaps * 2 * window
    vmem = pl.BlockSpec(memory_space=pltpu.VMEM)

    whole = stacked(
        3 * levels,
        [
            (half_table, 0, 0),
            (shifts, levels, 0),
            (taps, 2 * levels, 0),
            (taps, 2 * levels, beams),
        ],
    )
    real = stacked(
        2 * levels + 2 + rtaps,
        [
            (angles.reshape(2 * levels, 2 * beams), 0, 0),
            (ukern.astype(jnp.float32), 2 * levels, 0),
            (rkern.T, 2 * levels + 2, 0),
        ],
    )
    return pl.pallas_call(
        functools.partial(prep_kernel, levels, beams, utaps, phases, rtaps),
        out_shape=[
            jax.ShapeDtypeStruct((levels, 4 * beams, depth), jnp.bfloat16),
            jax.ShapeDtypeStruct((levels, 8, LANES), jnp.float32),
        ],
        in_specs=[vmem, vmem],
        out_specs=[vmem, vmem],
        scratch_shapes=[
            pltpu.VMEM((beams // 2 + utaps, 2 * beams), jnp.float32),
            pltpu.VMEM((depth, 2 * beams), jnp.float32),
        ],
        compiler_params=pltpu.CompilerParams(vmem_limit_bytes=24 * 2**20),
        cost_estimate=pl.CostEstimate(
            flops=2 * 10**9, bytes_accessed=2 * levels * 4 * beams * depth, transcendentals=0
        ),
        name="mixing",
    )(whole, real)


def merge_kernel(level, plan, start, stop, length, beams, window, rtaps, last, *refs):
    code_ref, mix_ref = refs[:2]
    count = len(plan)
    own_refs, far_refs = refs[2:2 + count], refs[2 + count:2 + 2 * count]
    outs = refs[3 + 2 * count:]
    out_ref = outs[0]
    send_ref = None if last else outs[1]
    wide_ref, even_ref, odd_ref = outs[1 if last else 2:]
    code = jnp.max(code_ref[level]).astype(jnp.int32)
    half, following = code // 131072, code // 65536 % 2
    shifts = (code // 256 % 256 - LANES, code % 256 - LANES)
    rows = pl.ds(pl.multiple_of(half * (beams - window), 16), window)
    base = start - LANES
    for number, (piece, source, target, width) in enumerate(plan):
        for child, ref in ((0, own_refs[number]), (1, far_refs[number])):
            taken = rows if ref.shape[1] == beams else pl.ds(0, window)
            for part in range(2):
                wide_ref[child, part, :, target - base:target - base + width] = ref[
                    part, taken, source:source + width
                ]
    edge = jnp.zeros((2, 2, window, LANES), jnp.bfloat16)
    if base < 0:
        wide_ref[:, :, :, 0:LANES] = edge
    if stop + LANES > length:
        wide_ref[:, :, :, stop - base:stop - base + LANES] = edge
    span = stop - start
    tile = min(TILE, span)
    tiles = pl.cdiv(span, tile)
    lane = lax.broadcasted_iota(jnp.int32, (2 * window, LANES), 1).astype(jnp.int16)
    moves = []
    for child in range(2):
        for tap in range(rtaps):
            shift = shifts[child] + (tap - 1 + LANES)
            part_tile = lax.rem(shift, LANES)
            kept = jnp.full((2 * window, LANES), LANES - part_tile, jnp.int32).astype(jnp.int16)
            turn = lax.rem(LANES - part_tile, LANES)
            moves.append((child, tap, shift // LANES * LANES, turn, lane < kept))

    def column_of(step):
        return pl.multiple_of(jnp.minimum(step * tile, span - tile), LANES)

    def build(stack_ref, step):
        column = column_of(step)
        for child, tap, whole, turn, kept in moves:
            place = (child * rtaps + tap) * 2 * window
            held = None
            for block in range(tile // LANES + 1):
                at = pl.multiple_of(column + whole + block * LANES, LANES)
                piece = wide_ref[child, :, :, pl.ds(at, LANES)].reshape(2 * window, LANES)
                piece = pltpu.roll(piece, turn, 1)
                if block > 0:
                    columns = pl.ds((block - 1) * LANES, LANES)
                    stack_ref[place:place + 2 * window, columns] = jnp.where(kept, held, piece)
                held = piece

    def multiply(stack_ref, step):
        column = column_of(step)
        both = jnp.dot(mix_ref[level], stack_ref[...], preferred_element_type=jnp.float32)
        total = (both[:2 * beams] + both[2 * beams:]).astype(jnp.bfloat16)
        out_ref[:, :, pl.ds(column, tile)] = total.reshape(2, beams, tile)

    def two_tiles(pair, carry):
        build(odd_ref, 2 * pair + 1)
        multiply(even_ref, 2 * pair)
        build(even_ref, 2 * pair + 2)
        multiply(odd_ref, 2 * pair + 1)
        return carry

    build(even_ref, 0)
    lax.fori_loop(0, tiles // 2, two_tiles, 0)
    if tiles % 2 == 1:
        multiply(even_ref, tiles - 1)
    if not last:
        other = pl.ds(pl.multiple_of((1 - following) * (beams - window), 16), window)
        send_ref[...] = out_ref[:, other, :]


def pieces_of(bounds, start, stop):
    found = []
    for chunk in range(len(bounds) - 1):
        low, high = max(bounds[chunk], start), min(bounds[chunk + 1], stop)
        if low < high:
            found.append((chunk, low - bounds[chunk], low, high - low))
    return found


def merge(level, levels, codes, mix, own, far, bounds, start, stop, sizes, before):
    beams, window, rtaps, length = sizes
    last = level == levels - 1
    plan = pieces_of(bounds, max(start - LANES, 0), min(stop + LANES, length))
    span = stop - start
    vmem = pl.BlockSpec(memory_space=pltpu.VMEM)
    anywhere = pl.BlockSpec(memory_space=pl.ANY)
    depth = mix.shape[2]
    out_shape = [jax.ShapeDtypeStruct((2, beams, span), jnp.bfloat16)]
    if not last:
        out_shape.append(jax.ShapeDtypeStruct((2, window, span), jnp.bfloat16))
    return pl.pallas_call(
        functools.partial(
            merge_kernel, level, plan, start, stop, length, beams, window, rtaps, last
        ),
        out_shape=out_shape,
        in_specs=[vmem, vmem] + [vmem] * (2 * len(plan)) + [anywhere],
        out_specs=[vmem] * len(out_shape),
        scratch_shapes=[
            pltpu.VMEM((2, 2, window, span + 2 * LANES), jnp.bfloat16),
            pltpu.VMEM((depth, min(TILE, span)), jnp.bfloat16),
            pltpu.VMEM((depth, min(TILE, span)), jnp.bfloat16),
        ],
        compiler_params=pltpu.CompilerParams(vmem_limit_bytes=24 * 2**20),
        cost_estimate=pl.CostEstimate(
            flops=32 * beams * depth * span,
            bytes_accessed=0,
            transcendentals=0,
        ),
        name=f"merge_{level}",
    )(
        codes,
        mix,
        *[own[piece[0]] for piece in plan],
        *[far[piece[0]] for piece in plan],
        before,
    )


def chunk_bounds(level, levels, length):
    marks = ((4, 12, 20, 28), (6, 14, 21, 29), (7, 16, 22), (8, 18))
    tiles = length // LANES
    chosen = marks[min(levels - level, len(marks) - 1)]
    inner = [tiles * mark // 32 for mark in chosen]
    return [0] + [mark * LANES for mark in inner] + [length]


def merge_order(levels, bounds):
    length = bounds[0][-1]
    sending = [18.0] * (levels - 1) + [36.0]
    fixed, working, starting, flying = 0.75, 9.0, 1.5, 2.0
    clock = 5.0
    arrival = {(0, 0): clock}
    busy = [clock] * levels
    following = [0] * levels
    order = []
    while len(order) < sum(len(bound) - 1 for bound in bounds[1:]):
        choices = []
        for level in range(levels):
            chunk = following[level]
            if chunk == len(bounds[level + 1]) - 1:
                continue
            needed = pieces_of(bounds[level], 0, min(bounds[level + 1][chunk + 1] + LANES, length))
            times = [arrival.get((level, piece[0])) for piece in needed]
            if None not in times:
                choices.append((max(times + [clock]), -level, chunk))
        begin, level, chunk = min(choices)
        level = -level
        following[level] += 1
        order.append((level, chunk))
        width = (bounds[level + 1][chunk + 1] - bounds[level + 1][chunk]) / length
        clock = begin + fixed + working * width
        if level < levels - 1:
            clock += starting
            busy[level + 1] = max(busy[level + 1], clock) + sending[level + 1] * width
            arrival[level + 1, chunk] = busy[level + 1] + flying
    return order


def from_partner(value, bit):
    mask = 1 << bit
    pairs = [(source, source ^ mask) for source in range(lax.axis_size("pulse"))]
    return lax.ppermute(value, "pulse", pairs)


def on_device(beams_in, ukern, rkern, angles, taps, shifts, half_table):
    beams, length = beams_in.shape[1:]
    utaps, rtaps = ukern.shape[1], rkern.shape[1]
    window = beams // 2 + utaps // 2
    levels = half_table.shape[0]
    sizes = (beams, window, rtaps, length)
    bounds = [[0, length]]
    bounds += [chunk_bounds(level, levels, length) for level in range(1, levels + 1)]
    mix, codes = mixing(ukern, rkern, angles, taps, shifts, half_table)
    owns = [[beams_in]] + [[None] * (len(bound) - 1) for bound in bounds[1:]]
    fars = [[from_partner(beams_in, 0)]] + [[None] * (len(bound) - 1) for bound in bounds[1:]]
    before = mix
    for level, chunk in merge_order(levels, bounds):
        start, stop = bounds[level + 1][chunk], bounds[level + 1][chunk + 1]
        done = merge(
            level, levels, codes, mix, owns[level], fars[level], bounds[level],
            start, stop, sizes, before,
        )
        before = owns[level + 1][chunk] = done[0]
        if level < levels - 1:
            fars[level + 1][chunk] = from_partner(done[1], level + 1)
    return jnp.concatenate(owns[levels], axis=2)


def solution(mesh):
    in_specs = (
        P(None, ("scene", "pulse"), None),
        P(),
        P(),
        P(),
        P(None, ("scene", "pulse")),
        P(),
        P(),
    )
    out_specs = P(None, ("scene", "pulse"), None)
    return jax.shard_map(
        on_device, mesh=mesh, in_specs=in_specs, out_specs=out_specs, check_vma=False
    )
```

```python
import functools

import jax
import jax.numpy as jnp
from jax import lax
from jax.experimental import pallas as pl
from jax.experimental.pallas import tpu as pltpu
from jax.sharding import PartitionSpec as P

LANES = 128
TILE = 256
SCALE = 0.70710678


def prep_kernel(levels, beams, utaps, phases, rtaps, whole_ref, real_ref, mix_ref, plan_ref, band_ref, flat_ref):
    at_shifts, at_taps = levels, 2 * levels
    at_ukern, at_rkern = 2 * levels, 2 * levels + 2
    window = beams // 2 + utaps // 2
    myself = lax.axis_index("pulse")
    lane = lax.broadcasted_iota(jnp.int32, (1, 2 * beams), 1)
    first = lane < beams
    beam = jnp.where(first, lane, lane - beams)
    depth = beams // 2 + utaps
    row = lax.broadcasted_iota(jnp.int32, (depth, 2 * beams), 0)
    offset = row - beam // 2 - 1
    even = beam % 2 == 0
    halves = whole_ref[0:levels, :].astype(jnp.float32)
    shifts = whole_ref[at_shifts:at_shifts + levels, :].astype(jnp.float32)
    place = lax.broadcasted_iota(jnp.int32, (levels, LANES), 1)
    level_of = lax.broadcasted_iota(jnp.int32, (levels, LANES), 0)
    partner = jnp.bitwise_xor(myself, lax.shift_left(jnp.ones_like(level_of), level_of))

    def pick(table, index):
        return jnp.sum(jnp.where(place == index, table, 0.0), axis=1, keepdims=True)

    half_of = pick(halves, myself)
    after_of = jnp.concatenate([half_of[1:], half_of[:1]], axis=0)
    near_of = pick(shifts, myself) + LANES
    far_of = pick(shifts, partner) + LANES
    codes = ((half_of * 2 + after_of) * 256 + near_of) * 256 + far_of
    for level in range(levels):
        plan_ref[level] = jnp.broadcast_to(codes[level:level + 1, :], (8, LANES))
    kernel = real_ref[at_ukern:at_ukern + 2, :]
    band = jnp.zeros((depth, 2 * beams), jnp.float32)
    for k in range(utaps):
        value = jnp.where(even, kernel[0:1, k:k + 1], kernel[1:2, k:k + 1])
        band = jnp.where(offset == k, value, band)
    band_ref[...] = band
    table = real_ref[at_rkern:at_rkern + rtaps, :]
    for level in range(levels):
        low_half = half_of[level:level + 1, :] == 0.0
        bit = lax.rem(lax.shift_right_logical(myself, level), 2)
        near = jnp.where(
            low_half, band_ref[utaps // 2:utaps // 2 + window, :], band_ref[0:window, :]
        )
        chosen = whole_ref[at_taps + level:at_taps + level + 1, :]
        weights = []
        for tap in range(rtaps):
            weight = jnp.zeros((1, 2 * beams), jnp.float32)
            for phase in range(phases):
                weight = jnp.where(
                    chosen == phase, table[tap:tap + 1, phase:phase + 1], weight
                )
            weights.append(weight)
        for child in range(2):
            side = bit if child == 0 else 1 - bit
            angle = real_ref[pl.ds(2 * level + side, 1), :]
            turned = pltpu.roll(angle, beams, 1)
            angle = jnp.where(first == low_half, angle, turned)
            cosine = SCALE * jnp.cos(angle)
            sine = SCALE * jnp.sin(angle)
            factors = (jnp.where(first, cosine, sine), jnp.where(first, -sine, cosine))
            for tap in range(rtaps):
                for part in range(2):
                    place = ((child * rtaps + tap) * 2 + part) * window
                    flat_ref[place:place + window, :] = near * (factors[part] * weights[tap])
        for block in range(flat_ref.shape[0] // LANES):
            mixed = flat_ref[block * LANES:(block + 1) * LANES, :].T
            high = mixed.astype(jnp.bfloat16)
            low = (mixed - high.astype(jnp.float32)).astype(jnp.bfloat16)
            columns = pl.ds(block * LANES, LANES)
            mix_ref[level, 0:2 * beams, columns] = high
            mix_ref[level, 2 * beams:4 * beams, columns] = low


def stacked(height, pieces):
    total = jnp.zeros((height, LANES), pieces[0][0].dtype)
    for piece, top, left in pieces:
        below, right = height - top - piece.shape[0], LANES - left - piece.shape[1]
        zero = jnp.zeros((), piece.dtype)
        total = total + lax.pad(piece, zero, ((top, below, 0), (left, right, 0)))
    return total


def mixing(ukern, rkern, angles, taps, shifts, half_table):
    levels = half_table.shape[0]
    beams = taps.shape[1]
    utaps = ukern.shape[1]
    phases, rtaps = rkern.shape
    window = beams // 2 + utaps // 2
    depth = 2 * rtaps * 2 * window
    vmem = pl.BlockSpec(memory_space=pltpu.VMEM)

    whole = stacked(
        3 * levels,
        [
            (half_table, 0, 0),
            (shifts, levels, 0),
            (taps, 2 * levels, 0),
            (taps, 2 * levels, beams),
        ],
    )
    real = stacked(
        2 * levels + 2 + rtaps,
        [
            (angles.reshape(2 * levels, 2 * beams), 0, 0),
            (ukern.astype(jnp.float32), 2 * levels, 0),
            (rkern.T, 2 * levels + 2, 0),
        ],
    )
    return pl.pallas_call(
        functools.partial(prep_kernel, levels, beams, utaps, phases, rtaps),
        out_shape=[
            jax.ShapeDtypeStruct((levels, 4 * beams, depth), jnp.bfloat16),
            jax.ShapeDtypeStruct((levels, 8, LANES), jnp.float32),
        ],
        in_specs=[vmem, vmem],
        out_specs=[vmem, vmem],
        scratch_shapes=[
            pltpu.VMEM((beams // 2 + utaps, 2 * beams), jnp.float32),
            pltpu.VMEM((depth, 2 * beams), jnp.float32),
        ],
        compiler_params=pltpu.CompilerParams(vmem_limit_bytes=24 * 2**20),
        cost_estimate=pl.CostEstimate(
            flops=2 * 10**9, bytes_accessed=2 * levels * 4 * beams * depth, transcendentals=0
        ),
        name="mixing",
    )(whole, real)


def merge_kernel(level, plan, start, stop, length, beams, window, rtaps, last, *refs):
    code_ref, mix_ref = refs[:2]
    count = len(plan)
    own_refs, far_refs = refs[2:2 + count], refs[2 + count:2 + 2 * count]
    outs = refs[3 + 2 * count:]
    out_ref = outs[0]
    send_ref = None if last else outs[1]
    wide_ref, even_ref, odd_ref = outs[1 if last else 2:]
    code = jnp.max(code_ref[level]).astype(jnp.int32)
    half, following = code // 131072, code // 65536 % 2
    shifts = (code // 256 % 256 - LANES, code % 256 - LANES)
    rows = pl.ds(pl.multiple_of(half * (beams - window), 16), window)
    base = start - LANES
    bit = lax.rem(lax.shift_right_logical(lax.axis_index("pulse"), level), 2)
    other = 2 * (1 - bit)
    for number, (piece, source, target, width) in enumerate(plan):
        for child, ref in ((0, own_refs[number]), (1, far_refs[number])):
            taken = rows if ref.shape[1] == beams else pl.ds(0, window)
            for part in range(2):
                which = part if ref.shape[0] == 2 else other + part
                wide_ref[child, part, :, target - base:target - base + width] = ref[
                    which, taken, source:source + width
                ]
    edge = jnp.zeros((2, 2, window, LANES), jnp.bfloat16)
    if base < 0:
        wide_ref[:, :, :, 0:LANES] = edge
    if stop + LANES > length:
        wide_ref[:, :, :, stop - base:stop - base + LANES] = edge
    span = stop - start
    tile = min(TILE, span)
    tiles = pl.cdiv(span, tile)
    lane = lax.broadcasted_iota(jnp.int32, (2 * window, LANES), 1).astype(jnp.int16)
    moves = []
    for child in range(2):
        for tap in range(rtaps):
            shift = shifts[child] + (tap - 1 + LANES)
            part_tile = lax.rem(shift, LANES)
            kept = jnp.full((2 * window, LANES), LANES - part_tile, jnp.int32).astype(jnp.int16)
            turn = lax.rem(LANES - part_tile, LANES)
            moves.append((child, tap, shift // LANES * LANES, turn, lane < kept))

    def column_of(step):
        return pl.multiple_of(jnp.minimum(step * tile, span - tile), LANES)

    def build(stack_ref, step):
        column = column_of(step)
        for child, tap, whole, turn, kept in moves:
            place = (child * rtaps + tap) * 2 * window
            held = None
            for block in range(tile // LANES + 1):
                at = pl.multiple_of(column + whole + block * LANES, LANES)
                piece = wide_ref[child, :, :, pl.ds(at, LANES)].reshape(2 * window, LANES)
                piece = pltpu.roll(piece, turn, 1)
                if block > 0:
                    columns = pl.ds((block - 1) * LANES, LANES)
                    stack_ref[place:place + 2 * window, columns] = jnp.where(kept, held, piece)
                held = piece

    def multiply(stack_ref, step):
        column = column_of(step)
        both = jnp.dot(mix_ref[level], stack_ref[...], preferred_element_type=jnp.float32)
        total = (both[:2 * beams] + both[2 * beams:]).astype(jnp.bfloat16)
        out_ref[:, :, pl.ds(column, tile)] = total.reshape(2, beams, tile)

    def two_tiles(pair, carry):
        build(odd_ref, 2 * pair + 1)
        multiply(even_ref, 2 * pair)
        build(even_ref, 2 * pair + 2)
        multiply(odd_ref, 2 * pair + 1)
        return carry

    build(even_ref, 0)
    lax.fori_loop(0, tiles // 2, two_tiles, 0)
    if tiles % 2 == 1:
        multiply(even_ref, tiles - 1)
    if not last:
        other = pl.ds(pl.multiple_of((1 - following) * (beams - window), 16), window)
        send_ref[...] = out_ref[:, other, :]


def pieces_of(bounds, start, stop):
    found = []
    for chunk in range(len(bounds) - 1):
        low, high = max(bounds[chunk], start), min(bounds[chunk + 1], stop)
        if low < high:
            found.append((chunk, low - bounds[chunk], low, high - low))
    return found


def merge(level, levels, codes, mix, own, far, bounds, start, stop, sizes, before):
    beams, window, rtaps, length = sizes
    last = level == levels - 1
    plan = pieces_of(bounds, max(start - LANES, 0), min(stop + LANES, length))
    span = stop - start
    vmem = pl.BlockSpec(memory_space=pltpu.VMEM)
    anywhere = pl.BlockSpec(memory_space=pl.ANY)
    depth = mix.shape[2]
    out_shape = [jax.ShapeDtypeStruct((2, beams, span), jnp.bfloat16)]
    if not last:
        out_shape.append(jax.ShapeDtypeStruct((2, window, span), jnp.bfloat16))
    return pl.pallas_call(
        functools.partial(
            merge_kernel, level, plan, start, stop, length, beams, window, rtaps, last
        ),
        out_shape=out_shape,
        in_specs=[vmem, vmem] + [vmem] * (2 * len(plan)) + [anywhere],
        out_specs=[vmem] * len(out_shape),
        scratch_shapes=[
            pltpu.VMEM((2, 2, window, span + 2 * LANES), jnp.bfloat16),
            pltpu.VMEM((depth, min(TILE, span)), jnp.bfloat16),
            pltpu.VMEM((depth, min(TILE, span)), jnp.bfloat16),
        ],
        compiler_params=pltpu.CompilerParams(vmem_limit_bytes=24 * 2**20),
        cost_estimate=pl.CostEstimate(
            flops=32 * beams * depth * span,
            bytes_accessed=0,
            transcendentals=0,
        ),
        name=f"merge_{level}",
    )(
        codes,
        mix,
        *[own[piece[0]] for piece in plan],
        *[far[piece[0]] for piece in plan],
        before,
    )


def chunk_bounds(level, levels, length):
    marks = ((4, 12, 20, 28), (6, 14, 21, 29), (7, 16, 22), (8, 18))
    tiles = length // LANES
    chosen = marks[min(levels - level, len(marks) - 1)]
    inner = [tiles * mark // 32 for mark in chosen]
    return [0] + [mark * LANES for mark in inner] + [length]


def merge_order(levels, bounds):
    length = bounds[0][-1]
    sending = [18.0] * (levels - 1) + [36.0]
    fixed, working, starting, flying = 0.75, 9.0, 1.5, 2.0
    clock = 5.0
    arrival = {(0, 0): clock}
    busy = [clock] * levels
    following = [0] * levels
    order = []
    while len(order) < sum(len(bound) - 1 for bound in bounds[1:]):
        choices = []
        for level in range(levels):
            chunk = following[level]
            if chunk == len(bounds[level + 1]) - 1:
                continue
            needed = pieces_of(bounds[level], 0, min(bounds[level + 1][chunk + 1] + LANES, length))
            times = [arrival.get((level, piece[0])) for piece in needed]
            if None not in times:
                choices.append((max(times + [clock]), -level, chunk))
        begin, level, chunk = min(choices)
        level = -level
        following[level] += 1
        order.append((level, chunk))
        width = (bounds[level + 1][chunk + 1] - bounds[level + 1][chunk]) / length
        clock = begin + fixed + working * width
        if level < levels - 1:
            clock += starting
            busy[level + 1] = max(busy[level + 1], clock) + sending[level + 1] * width
            arrival[level + 1, chunk] = busy[level + 1] + flying
    return order


def from_partner(value, bit):
    mask = 1 << bit
    pairs = [(source, source ^ mask) for source in range(lax.axis_size("pulse"))]
    return lax.ppermute(value, "pulse", pairs)


def gathered(value, bit):
    mask = 1 << bit
    groups = [[s, s | mask] for s in range(lax.axis_size("pulse")) if s & mask == 0]
    return lax.all_gather(value, "pulse", axis_index_groups=groups, tiled=True)


def on_device(beams_in, ukern, rkern, angles, taps, shifts, half_table):
    beams, length = beams_in.shape[1:]
    utaps, rtaps = ukern.shape[1], rkern.shape[1]
    window = beams // 2 + utaps // 2
    levels = half_table.shape[0]
    sizes = (beams, window, rtaps, length)
    bounds = [[0, length]]
    bounds += [chunk_bounds(level, levels, length) for level in range(1, levels + 1)]
    mix, codes = mixing(ukern, rkern, angles, taps, shifts, half_table)
    owns = [[beams_in]] + [[None] * (len(bound) - 1) for bound in bounds[1:]]
    fars = [[from_partner(beams_in, 0)]] + [[None] * (len(bound) - 1) for bound in bounds[1:]]
    before = mix
    for level, chunk in merge_order(levels, bounds):
        start, stop = bounds[level + 1][chunk], bounds[level + 1][chunk + 1]
        done = merge(
            level, levels, codes, mix, owns[level], fars[level], bounds[level],
            start, stop, sizes, before,
        )
        before = owns[level + 1][chunk] = done[0]
        if level < levels - 1:
            send = gathered if level + 2 == levels else from_partner
            fars[level + 1][chunk] = send(done[1], level + 1)
    return jnp.concatenate(owns[levels], axis=2)


def solution(mesh):
    in_specs = (
        P(None, ("scene", "pulse"), None),
        P(),
        P(),
        P(),
        P(None, ("scene", "pulse")),
        P(),
        P(),
    )
    out_specs = P(None, ("scene", "pulse"), None)
    return jax.shard_map(
        on_device, mesh=mesh, in_specs=in_specs, out_specs=out_specs, check_vma=False
    )
```

```python
import functools

import jax
import jax.numpy as jnp
from jax import lax
from jax.experimental import pallas as pl
from jax.experimental.pallas import tpu as pltpu
from jax.sharding import PartitionSpec as P

LANES = 128
TILE = 256
SCALE = 0.70710678


def prep_kernel(levels, beams, utaps, phases, rtaps, whole_ref, real_ref, mix_ref, plan_ref, band_ref, flat_ref):
    at_shifts, at_taps = levels, 2 * levels
    at_ukern, at_rkern = 2 * levels, 2 * levels + 2
    window = beams // 2 + utaps // 2
    myself = lax.axis_index("pulse")
    lane = lax.broadcasted_iota(jnp.int32, (1, 2 * beams), 1)
    first = lane < beams
    beam = jnp.where(first, lane, lane - beams)
    depth = beams // 2 + utaps
    row = lax.broadcasted_iota(jnp.int32, (depth, 2 * beams), 0)
    offset = row - beam // 2 - 1
    even = beam % 2 == 0
    halves = whole_ref[0:levels, :].astype(jnp.float32)
    shifts = whole_ref[at_shifts:at_shifts + levels, :].astype(jnp.float32)
    place = lax.broadcasted_iota(jnp.int32, (levels, LANES), 1)
    level_of = lax.broadcasted_iota(jnp.int32, (levels, LANES), 0)
    partner = jnp.bitwise_xor(myself, lax.shift_left(jnp.ones_like(level_of), level_of))

    def pick(table, index):
        return jnp.sum(jnp.where(place == index, table, 0.0), axis=1, keepdims=True)

    half_of = pick(halves, myself)
    after_of = jnp.concatenate([half_of[1:], half_of[:1]], axis=0)
    near_of = pick(shifts, myself) + LANES
    far_of = pick(shifts, partner) + LANES
    codes = ((half_of * 2 + after_of) * 256 + near_of) * 256 + far_of
    for level in range(levels):
        plan_ref[level] = jnp.broadcast_to(codes[level:level + 1, :], (8, LANES))
    kernel = real_ref[at_ukern:at_ukern + 2, :]
    band = jnp.zeros((depth, 2 * beams), jnp.float32)
    for k in range(utaps):
        value = jnp.where(even, kernel[0:1, k:k + 1], kernel[1:2, k:k + 1])
        band = jnp.where(offset == k, value, band)
    band_ref[...] = band
    table = real_ref[at_rkern:at_rkern + rtaps, :]
    for level in range(levels):
        low_half = half_of[level:level + 1, :] == 0.0
        bit = lax.rem(lax.shift_right_logical(myself, level), 2)
        near = jnp.where(
            low_half, band_ref[utaps // 2:utaps // 2 + window, :], band_ref[0:window, :]
        )
        chosen = whole_ref[at_taps + level:at_taps + level + 1, :]
        weights = []
        for tap in range(rtaps):
            weight = jnp.zeros((1, 2 * beams), jnp.float32)
            for phase in range(phases):
                weight = jnp.where(
                    chosen == phase, table[tap:tap + 1, phase:phase + 1], weight
                )
            weights.append(weight)
        for child in range(2):
            side = bit if child == 0 else 1 - bit
            angle = real_ref[pl.ds(2 * level + side, 1), :]
            turned = pltpu.roll(angle, beams, 1)
            angle = jnp.where(first == low_half, angle, turned)
            cosine = SCALE * jnp.cos(angle)
            sine = SCALE * jnp.sin(angle)
            factors = (jnp.where(first, cosine, sine), jnp.where(first, -sine, cosine))
            for tap in range(rtaps):
                for part in range(2):
                    place = ((child * rtaps + tap) * 2 + part) * window
                    flat_ref[place:place + window, :] = near * (factors[part] * weights[tap])
        for block in range(flat_ref.shape[0] // LANES):
            mixed = flat_ref[block * LANES:(block + 1) * LANES, :].T
            high = mixed.astype(jnp.bfloat16)
            low = (mixed - high.astype(jnp.float32)).astype(jnp.bfloat16)
            columns = pl.ds(block * LANES, LANES)
            mix_ref[level, 0:2 * beams, columns] = high
            mix_ref[level, 2 * beams:4 * beams, columns] = low


def stacked(height, pieces):
    total = jnp.zeros((height, LANES), pieces[0][0].dtype)
    for piece, top, left in pieces:
        below, right = height - top - piece.shape[0], LANES - left - piece.shape[1]
        zero = jnp.zeros((), piece.dtype)
        total = total + lax.pad(piece, zero, ((top, below, 0), (left, right, 0)))
    return total


def mixing(ukern, rkern, angles, taps, shifts, half_table):
    levels = half_table.shape[0]
    beams = taps.shape[1]
    utaps = ukern.shape[1]
    phases, rtaps = rkern.shape
    window = beams // 2 + utaps // 2
    depth = 2 * rtaps * 2 * window
    vmem = pl.BlockSpec(memory_space=pltpu.VMEM)

    whole = stacked(
        3 * levels,
        [
            (half_table, 0, 0),
            (shifts, levels, 0),
            (taps, 2 * levels, 0),
            (taps, 2 * levels, beams),
        ],
    )
    real = stacked(
        2 * levels + 2 + rtaps,
        [
            (angles.reshape(2 * levels, 2 * beams), 0, 0),
            (ukern.astype(jnp.float32), 2 * levels, 0),
            (rkern.T, 2 * levels + 2, 0),
        ],
    )
    return pl.pallas_call(
        functools.partial(prep_kernel, levels, beams, utaps, phases, rtaps),
        out_shape=[
            jax.ShapeDtypeStruct((levels, 4 * beams, depth), jnp.bfloat16),
            jax.ShapeDtypeStruct((levels, 8, LANES), jnp.float32),
        ],
        in_specs=[vmem, vmem],
        out_specs=[vmem, vmem],
        scratch_shapes=[
            pltpu.VMEM((beams // 2 + utaps, 2 * beams), jnp.float32),
            pltpu.VMEM((depth, 2 * beams), jnp.float32),
        ],
        compiler_params=pltpu.CompilerParams(vmem_limit_bytes=24 * 2**20),
        cost_estimate=pl.CostEstimate(
            flops=2 * 10**9, bytes_accessed=2 * levels * 4 * beams * depth, transcendentals=0
        ),
        name="mixing",
    )(whole, real)


def merge_kernel(level, plan, start, stop, length, beams, window, rtaps, last, *refs):
    code_ref, mix_ref = refs[:2]
    count = len(plan)
    own_refs, far_refs = refs[2:2 + count], refs[2 + count:2 + 2 * count]
    outs = refs[3 + 2 * count:]
    out_ref = outs[0]
    send_ref = None if last else outs[1]
    wide_ref, even_ref, odd_ref = outs[1 if last else 2:]
    code = jnp.max(code_ref[level]).astype(jnp.int32)
    half, following = code // 131072, code // 65536 % 2
    shifts = (code // 256 % 256 - LANES, code % 256 - LANES)
    rows = pl.ds(pl.multiple_of(half * (beams - window), 16), window)
    base = start - LANES
    for number, (piece, source, target, width) in enumerate(plan):
        for child, ref in ((0, own_refs[number]), (1, far_refs[number])):
            taken = rows if ref.shape[1] == beams else pl.ds(0, window)
            for part in range(2):
                wide_ref[child, part, :, target - base:target - base + width] = ref[
                    part, taken, source:source + width
                ]
    edge = jnp.zeros((2, 2, window, LANES), jnp.bfloat16)
    if base < 0:
        wide_ref[:, :, :, 0:LANES] = edge
    if stop + LANES > length:
        wide_ref[:, :, :, stop - base:stop - base + LANES] = edge
    span = stop - start
    tile = min(TILE, span)
    tiles = pl.cdiv(span, tile)
    lane = lax.broadcasted_iota(jnp.int32, (2 * window, LANES), 1).astype(jnp.int16)
    moves = []
    for child in range(2):
        for tap in range(rtaps):
            shift = shifts[child] + (tap - 1 + LANES)
            part_tile = lax.rem(shift, LANES)
            kept = jnp.full((2 * window, LANES), LANES - part_tile, jnp.int32).astype(jnp.int16)
            turn = lax.rem(LANES - part_tile, LANES)
            moves.append((child, tap, shift // LANES * LANES, turn, lane < kept))

    def column_of(step):
        return pl.multiple_of(jnp.minimum(step * tile, span - tile), LANES)

    def build(stack_ref, step):
        column = column_of(step)
        for child, tap, whole, turn, kept in moves:
            place = (child * rtaps + tap) * 2 * window
            held = None
            for block in range(tile // LANES + 1):
                at = pl.multiple_of(column + whole + block * LANES, LANES)
                piece = wide_ref[child, :, :, pl.ds(at, LANES)].reshape(2 * window, LANES)
                piece = pltpu.roll(piece, turn, 1)
                if block > 0:
                    columns = pl.ds((block - 1) * LANES, LANES)
                    stack_ref[place:place + 2 * window, columns] = jnp.where(kept, held, piece)
                held = piece

    def multiply(stack_ref, step):
        column = column_of(step)
        both = jnp.dot(mix_ref[level], stack_ref[...], preferred_element_type=jnp.float32)
        total = (both[:2 * beams] + both[2 * beams:]).astype(jnp.bfloat16)
        out_ref[:, :, pl.ds(column, tile)] = total.reshape(2, beams, tile)

    def two_tiles(pair, carry):
        build(odd_ref, 2 * pair + 1)
        multiply(even_ref, 2 * pair)
        build(even_ref, 2 * pair + 2)
        multiply(odd_ref, 2 * pair + 1)
        return carry

    build(even_ref, 0)
    lax.fori_loop(0, tiles // 2, two_tiles, 0)
    if tiles % 2 == 1:
        multiply(even_ref, tiles - 1)
    if not last:
        other = pl.ds(pl.multiple_of((1 - following) * (beams - window), 16), window)
        send_ref[...] = out_ref[:, other, :]


def pieces_of(bounds, start, stop):
    found = []
    for chunk in range(len(bounds) - 1):
        low, high = max(bounds[chunk], start), min(bounds[chunk + 1], stop)
        if low < high:
            found.append((chunk, low - bounds[chunk], low, high - low))
    return found


def merge(level, levels, codes, mix, own, far, bounds, start, stop, sizes, before):
    beams, window, rtaps, length = sizes
    last = level == levels - 1
    plan = pieces_of(bounds, max(start - LANES, 0), min(stop + LANES, length))
    span = stop - start
    vmem = pl.BlockSpec(memory_space=pltpu.VMEM)
    anywhere = pl.BlockSpec(memory_space=pl.ANY)
    depth = mix.shape[2]
    out_shape = [jax.ShapeDtypeStruct((2, beams, span), jnp.bfloat16)]
    if not last:
        out_shape.append(jax.ShapeDtypeStruct((2, window, span), jnp.bfloat16))
    return pl.pallas_call(
        functools.partial(
            merge_kernel, level, plan, start, stop, length, beams, window, rtaps, last
        ),
        out_shape=out_shape,
        in_specs=[vmem, vmem] + [vmem] * (2 * len(plan)) + [anywhere],
        out_specs=[vmem] * len(out_shape),
        scratch_shapes=[
            pltpu.VMEM((2, 2, window, span + 2 * LANES), jnp.bfloat16),
            pltpu.VMEM((depth, min(TILE, span)), jnp.bfloat16),
            pltpu.VMEM((depth, min(TILE, span)), jnp.bfloat16),
        ],
        compiler_params=pltpu.CompilerParams(vmem_limit_bytes=24 * 2**20),
        cost_estimate=pl.CostEstimate(
            flops=32 * beams * depth * span,
            bytes_accessed=0,
            transcendentals=0,
        ),
        name=f"merge_{level}",
    )(
        codes,
        mix,
        *[own[piece[0]] for piece in plan],
        *[far[piece[0]] for piece in plan],
        before,
    )


MARKS = (
    (6, 12, 24),
    (5, 11, 17, 23, 29),
    (4, 10, 16, 22, 27),
    (1, 3, 8, 22, 26),
)
ORDER = (
    (0, 0), (0, 1), (0, 2), (1, 0), (1, 1), (2, 0), (1, 2), (2, 1), (0, 3), (1, 3), (2, 2),
    (3, 0), (1, 4), (2, 3), (3, 1), (3, 2), (1, 5), (2, 4), (2, 5), (3, 3), (3, 4), (3, 5),
)


def chunk_bounds(level, levels, length):
    marks = MARKS[len(MARKS) - 1 - min(levels - level, len(MARKS) - 1)]
    tiles = length // LANES
    return [0] + [tiles * mark // 32 * LANES for mark in marks] + [length]


def merge_order(levels, bounds):
    if levels == len(MARKS):
        return ORDER
    length = bounds[0][-1]
    made = [0] * levels
    order = []
    while len(order) < sum(len(bound) - 1 for bound in bounds[1:]):
        ready = []
        for level in range(levels):
            chunk = made[level]
            if chunk < len(bounds[level + 1]) - 1:
                stop = min(bounds[level + 1][chunk + 1] + LANES, length)
                needed = len(pieces_of(bounds[level], 0, stop))
                if level == 0 or needed <= made[level - 1]:
                    ready.append((level + chunk, level, chunk))
        _, level, chunk = min(ready)
        made[level] += 1
        order.append((level, chunk))
    return order


def from_partner(value, bit):
    mask = 1 << bit
    pairs = [(source, source ^ mask) for source in range(lax.axis_size("pulse"))]
    return lax.ppermute(value, "pulse", pairs)


def on_device(beams_in, ukern, rkern, angles, taps, shifts, half_table):
    beams, length = beams_in.shape[1:]
    utaps, rtaps = ukern.shape[1], rkern.shape[1]
    window = beams // 2 + utaps // 2
    levels = half_table.shape[0]
    sizes = (beams, window, rtaps, length)
    bounds = [[0, length]]
    bounds += [chunk_bounds(level, levels, length) for level in range(1, levels + 1)]
    mix, codes = mixing(ukern, rkern, angles, taps, shifts, half_table)
    owns = [[beams_in]] + [[None] * (len(bound) - 1) for bound in bounds[1:]]
    fars = [[from_partner(beams_in, 0)]] + [[None] * (len(bound) - 1) for bound in bounds[1:]]
    before = mix
    for level, chunk in merge_order(levels, bounds):
        start, stop = bounds[level + 1][chunk], bounds[level + 1][chunk + 1]
        done = merge(
            level, levels, codes, mix, owns[level], fars[level], bounds[level],
            start, stop, sizes, before,
        )
        before = owns[level + 1][chunk] = done[0]
        if level < levels - 1:
            fars[level + 1][chunk] = from_partner(done[1], level + 1)
    return jnp.concatenate(owns[levels], axis=2)


def solution(mesh):
    in_specs = (
        P(None, ("scene", "pulse"), None),
        P(),
        P(),
        P(),
        P(None, ("scene", "pulse")),
        P(),
        P(),
    )
    out_specs = P(None, ("scene", "pulse"), None)
    return jax.shard_map(
        on_device, mesh=mesh, in_specs=in_specs, out_specs=out_specs, check_vma=False
    )
```

```python
import functools

import jax
import jax.numpy as jnp
from jax import lax
from jax.experimental import pallas as pl
from jax.experimental.pallas import tpu as pltpu
from jax.sharding import PartitionSpec as P

LANES = 128
TILE = 256
GROUP = 16
SCALE = 0.70710678


def prep_kernel(levels, beams, utaps, phases, rtaps, whole_ref, real_ref, mix_ref, weight_ref,
                plan_ref, band_ref, flat_ref):
    at_shifts, at_taps = levels, 2 * levels
    at_ukern, at_rkern = 2 * levels, 2 * levels + 2
    window = beams // 2 + utaps // 2
    myself = lax.axis_index("pulse")
    lane = lax.broadcasted_iota(jnp.int32, (1, 2 * beams), 1)
    first = lane < beams
    beam = jnp.where(first, lane, lane - beams)
    depth = beams // 2 + utaps
    row = lax.broadcasted_iota(jnp.int32, (depth, 2 * beams), 0)
    offset = row - beam // 2 - 1
    even = beam % 2 == 0
    halves = whole_ref[0:levels, :].astype(jnp.float32)
    shifts = whole_ref[at_shifts:at_shifts + levels, :].astype(jnp.float32)
    place = lax.broadcasted_iota(jnp.int32, (levels, LANES), 1)
    level_of = lax.broadcasted_iota(jnp.int32, (levels, LANES), 0)
    partner = jnp.bitwise_xor(myself, lax.shift_left(jnp.ones_like(level_of), level_of))

    def pick(table, index):
        return jnp.sum(jnp.where(place == index, table, 0.0), axis=1, keepdims=True)

    half_of = pick(halves, myself)
    after_of = jnp.concatenate([half_of[1:], half_of[:1]], axis=0)
    near_of = pick(shifts, myself) + LANES
    far_of = pick(shifts, partner) + LANES
    codes = ((half_of * 2 + after_of) * 256 + near_of) * 256 + far_of
    for level in range(levels):
        plan_ref[level] = jnp.broadcast_to(codes[level:level + 1, :], (8, LANES))
    kernel = real_ref[at_ukern:at_ukern + 2, :]
    band = jnp.zeros((depth, 2 * beams), jnp.float32)
    for k in range(utaps):
        value = jnp.where(even, kernel[0:1, k:k + 1], kernel[1:2, k:k + 1])
        band = jnp.where(offset == k, value, band)
    band_ref[...] = band
    table = real_ref[at_rkern:at_rkern + rtaps, :]
    for level in range(levels):
        low_half = half_of[level:level + 1, :] == 0.0
        bit = lax.rem(lax.shift_right_logical(myself, level), 2)
        near = jnp.where(
            low_half, band_ref[utaps // 2:utaps // 2 + window, :], band_ref[0:window, :]
        )
        chosen = whole_ref[at_taps + level:at_taps + level + 1, :]
        for tap in range(rtaps):
            weight = jnp.zeros((1, 2 * beams), jnp.float32)
            for phase in range(phases):
                weight = jnp.where(
                    chosen == phase, table[tap:tap + 1, phase:phase + 1], weight
                )
            weight_ref[level, tap] = jnp.broadcast_to(weight, (LANES, 2 * beams)).T
        for child in range(2):
            side = bit if child == 0 else 1 - bit
            angle = real_ref[pl.ds(2 * level + side, 1), :]
            turned = pltpu.roll(angle, beams, 1)
            angle = jnp.where(first == low_half, angle, turned)
            cosine = SCALE * jnp.cos(angle)
            sine = SCALE * jnp.sin(angle)
            factors = (jnp.where(first, cosine, sine), jnp.where(first, -sine, cosine))
            for part in range(2):
                spot = (child * 2 + part) * window
                flat_ref[spot:spot + window, :] = near * factors[part]
        for top in range(0, 4 * window, LANES):
            bottom = min(top + LANES, 4 * window)
            mixed = flat_ref[top:bottom, :].T
            high = mixed.astype(jnp.bfloat16)
            low = (mixed - high.astype(jnp.float32)).astype(jnp.bfloat16)
            mix_ref[level, 0:2 * beams, top:bottom] = high
            mix_ref[level, 2 * beams:4 * beams, top:bottom] = low


def stacked(height, pieces):
    total = jnp.zeros((height, LANES), pieces[0][0].dtype)
    for piece, top, left in pieces:
        below, right = height - top - piece.shape[0], LANES - left - piece.shape[1]
        zero = jnp.zeros((), piece.dtype)
        total = total + lax.pad(piece, zero, ((top, below, 0), (left, right, 0)))
    return total


def mixing(ukern, rkern, angles, taps, shifts, half_table):
    levels = half_table.shape[0]
    beams = taps.shape[1]
    utaps = ukern.shape[1]
    phases, rtaps = rkern.shape
    window = beams // 2 + utaps // 2
    depth = 4 * window
    vmem = pl.BlockSpec(memory_space=pltpu.VMEM)

    whole = stacked(
        3 * levels,
        [
            (half_table, 0, 0),
            (shifts, levels, 0),
            (taps, 2 * levels, 0),
            (taps, 2 * levels, beams),
        ],
    )
    real = stacked(
        2 * levels + 2 + rtaps,
        [
            (angles.reshape(2 * levels, 2 * beams), 0, 0),
            (ukern.astype(jnp.float32), 2 * levels, 0),
            (rkern.T, 2 * levels + 2, 0),
        ],
    )
    return pl.pallas_call(
        functools.partial(prep_kernel, levels, beams, utaps, phases, rtaps),
        out_shape=[
            jax.ShapeDtypeStruct((levels, 4 * beams, depth), jnp.bfloat16),
            jax.ShapeDtypeStruct((levels, rtaps, 2 * beams, LANES), jnp.float32),
            jax.ShapeDtypeStruct((levels, 8, LANES), jnp.float32),
        ],
        in_specs=[vmem, vmem],
        out_specs=[vmem, vmem, vmem],
        scratch_shapes=[
            pltpu.VMEM((beams // 2 + utaps, 2 * beams), jnp.float32),
            pltpu.VMEM((depth, 2 * beams), jnp.float32),
        ],
        compiler_params=pltpu.CompilerParams(vmem_limit_bytes=24 * 2**20),
        cost_estimate=pl.CostEstimate(
            flops=2 * 10**9, bytes_accessed=32 * levels * beams * depth, transcendentals=0
        ),
        name="mixing",
    )(whole, real)


def merge_kernel(level, plan, start, stop, length, beams, window, rtaps, last, *refs):
    code_ref, mix_ref, weight_ref = refs[:3]
    count = len(plan)
    own_refs, far_refs = refs[3:3 + count], refs[3 + count:3 + 2 * count]
    outs = refs[4 + 2 * count:]
    out_ref = outs[0]
    send_ref = None if last else outs[1]
    wide_ref, even_ref, odd_ref, even_sum_ref, odd_sum_ref = outs[1 if last else 2:]
    code = jnp.max(code_ref[level]).astype(jnp.int32)
    half, following = code // 131072, code // 65536 % 2
    shifts = (code // 256 % 256 - LANES, code % 256 - LANES)
    rows = pl.ds(pl.multiple_of(half * (beams - window), 16), window)
    base = start - LANES
    for number, (piece, source, target, width) in enumerate(plan):
        for child, ref in ((0, own_refs[number]), (1, far_refs[number])):
            taken = rows if ref.shape[1] == beams else pl.ds(0, window)
            for part in range(2):
                wide_ref[child, part, :, target - base:target - base + width] = ref[
                    part, taken, source:source + width
                ]
    edge = jnp.zeros((2, 2, window, LANES), jnp.bfloat16)
    if base < 0:
        wide_ref[:, :, :, 0:LANES] = edge
    if stop + LANES > length:
        wide_ref[:, :, :, stop - base:stop - base + LANES] = edge
    wide_ref[:, :, :, stop - base + LANES:stop - base + 2 * LANES] = edge
    span = stop - start
    tile = min(TILE, span)
    tiles = pl.cdiv(span, tile)
    lane = lax.broadcasted_iota(jnp.int32, (2 * window, LANES), 1).astype(jnp.int16)
    moves = []
    for child in range(2):
        shift = shifts[child] + (LANES - 1)
        part_tile = lax.rem(shift, LANES)
        kept = jnp.full((2 * window, LANES), LANES - part_tile, jnp.int32).astype(jnp.int16)
        turn = lax.rem(LANES - part_tile, LANES)
        moves.append((child, shift // LANES * LANES, turn, lane < kept))
    blocks = tile // LANES
    place = lax.broadcasted_iota(jnp.int32, (GROUP, LANES), 1)

    def column_of(step):
        return pl.multiple_of(jnp.minimum(step * tile, span - tile), LANES)

    def build(stack_ref, step):
        column = column_of(step)
        for child, whole, turn, kept in moves:
            top = child * 2 * window
            held = None
            for block in range(blocks + 2):
                at = pl.multiple_of(column + whole + block * LANES, LANES)
                piece = wide_ref[child, :, :, pl.ds(at, LANES)].reshape(2 * window, LANES)
                piece = pltpu.roll(piece, turn, 1)
                if block > 0:
                    columns = pl.ds((block - 1) * LANES, LANES)
                    stack_ref[top:top + 2 * window, columns] = jnp.where(kept, held, piece)
                held = piece

    def multiply(stack_ref, sum_ref, step):
        column = column_of(step)
        both = jnp.dot(mix_ref[level], stack_ref[...], preferred_element_type=jnp.float32)
        sum_ref[...] = both[:2 * beams] + both[2 * beams:]
        for top in range(0, 2 * beams, GROUP):
            rows = pl.ds(top, GROUP)
            turned = []
            for block in range(blocks + 1):
                value = sum_ref[rows, pl.ds(block * LANES, LANES)]
                turned.append(
                    [value] + [pltpu.roll(value, LANES - tap, 1) for tap in range(1, rtaps)]
                )
            for block in range(blocks):
                total = weight_ref[level, 0, rows, :] * turned[block][0]
                for tap in range(1, rtaps):
                    moved = jnp.where(
                        place < LANES - tap, turned[block][tap], turned[block + 1][tap]
                    )
                    total = total + weight_ref[level, tap, rows, :] * moved
                columns = pl.ds(pl.multiple_of(column + block * LANES, LANES), LANES)
                part, beam = top // beams, top % beams
                out_ref[part, beam:beam + GROUP, columns] = total.astype(jnp.bfloat16)

    def two_tiles(pair, carry):
        build(odd_ref, 2 * pair + 1)
        multiply(even_ref, even_sum_ref, 2 * pair)
        build(even_ref, 2 * pair + 2)
        multiply(odd_ref, odd_sum_ref, 2 * pair + 1)
        return carry

    build(even_ref, 0)
    lax.fori_loop(0, tiles // 2, two_tiles, 0)
    if tiles % 2 == 1:
        multiply(even_ref, even_sum_ref, tiles - 1)
    if not last:
        other = pl.ds(pl.multiple_of((1 - following) * (beams - window), 16), window)
        send_ref[...] = out_ref[:, other, :]


def pieces_of(bounds, start, stop):
    found = []
    for chunk in range(len(bounds) - 1):
        low, high = max(bounds[chunk], start), min(bounds[chunk + 1], stop)
        if low < high:
            found.append((chunk, low - bounds[chunk], low, high - low))
    return found


def merge(level, levels, codes, mix, weights, own, far, bounds, start, stop, sizes, before):
    beams, window, rtaps, length = sizes
    last = level == levels - 1
    plan = pieces_of(bounds, max(start - LANES, 0), min(stop + LANES, length))
    span = stop - start
    vmem = pl.BlockSpec(memory_space=pltpu.VMEM)
    anywhere = pl.BlockSpec(memory_space=pl.ANY)
    depth = mix.shape[2]
    tile = min(TILE, span)
    out_shape = [jax.ShapeDtypeStruct((2, beams, span), jnp.bfloat16)]
    if not last:
        out_shape.append(jax.ShapeDtypeStruct((2, window, span), jnp.bfloat16))
    return pl.pallas_call(
        functools.partial(
            merge_kernel, level, plan, start, stop, length, beams, window, rtaps, last
        ),
        out_shape=out_shape,
        in_specs=[vmem] * (3 + 2 * len(plan)) + [anywhere],
        out_specs=[vmem] * len(out_shape),
        scratch_shapes=[
            pltpu.VMEM((2, 2, window, span + 3 * LANES), jnp.bfloat16),
            pltpu.VMEM((depth, tile + LANES), jnp.bfloat16),
            pltpu.VMEM((depth, tile + LANES), jnp.bfloat16),
            pltpu.VMEM((2 * beams, tile + LANES), jnp.float32),
            pltpu.VMEM((2 * beams, tile + LANES), jnp.float32),
        ],
        compiler_params=pltpu.CompilerParams(vmem_limit_bytes=24 * 2**20),
        cost_estimate=pl.CostEstimate(
            flops=128 * beams * depth * span,
            bytes_accessed=0,
            transcendentals=0,
        ),
        name=f"merge_{level}",
    )(
        codes,
        mix,
        weights,
        *[own[piece[0]] for piece in plan],
        *[far[piece[0]] for piece in plan],
        before,
    )


MARKS = (
    (6, 12, 24),
    (5, 11, 17, 23, 29),
    (4, 10, 16, 22, 27),
    (1, 3, 8, 22, 26),
)
ORDER = (
    (0, 0), (0, 1), (0, 2), (1, 0), (1, 1), (2, 0), (1, 2), (2, 1), (0, 3), (1, 3), (2, 2),
    (3, 0), (1, 4), (2, 3), (3, 1), (3, 2), (1, 5), (2, 4), (2, 5), (3, 3), (3, 4), (3, 5),
)


def chunk_bounds(level, levels, length):
    marks = MARKS[len(MARKS) - 1 - min(levels - level, len(MARKS) - 1)]
    tiles = length // LANES
    return [0] + [tiles * mark // 32 * LANES for mark in marks] + [length]


def merge_order(levels, bounds):
    if levels == len(MARKS):
        return ORDER
    length = bounds[0][-1]
    made = [0] * levels
    order = []
    while len(order) < sum(len(bound) - 1 for bound in bounds[1:]):
        ready = []
        for level in range(levels):
            chunk = made[level]
            if chunk < len(bounds[level + 1]) - 1:
                stop = min(bounds[level + 1][chunk + 1] + LANES, length)
                needed = len(pieces_of(bounds[level], 0, stop))
                if level == 0 or needed <= made[level - 1]:
                    ready.append((level + chunk, level, chunk))
        _, level, chunk = min(ready)
        made[level] += 1
        order.append((level, chunk))
    return order


def from_partner(value, bit):
    mask = 1 << bit
    pairs = [(source, source ^ mask) for source in range(lax.axis_size("pulse"))]
    return lax.ppermute(value, "pulse", pairs)


def on_device(beams_in, ukern, rkern, angles, taps, shifts, half_table):
    beams, length = beams_in.shape[1:]
    utaps, rtaps = ukern.shape[1], rkern.shape[1]
    window = beams // 2 + utaps // 2
    levels = half_table.shape[0]
    sizes = (beams, window, rtaps, length)
    bounds = [[0, length]]
    bounds += [chunk_bounds(level, levels, length) for level in range(1, levels + 1)]
    mix, weights, codes = mixing(ukern, rkern, angles, taps, shifts, half_table)
    owns = [[beams_in]] + [[None] * (len(bound) - 1) for bound in bounds[1:]]
    fars = [[from_partner(beams_in, 0)]] + [[None] * (len(bound) - 1) for bound in bounds[1:]]
    before = mix
    for level, chunk in merge_order(levels, bounds):
        start, stop = bounds[level + 1][chunk], bounds[level + 1][chunk + 1]
        done = merge(
            level, levels, codes, mix, weights, owns[level], fars[level], bounds[level],
            start, stop, sizes, before,
        )
        before = owns[level + 1][chunk] = done[0]
        if level < levels - 1:
            fars[level + 1][chunk] = from_partner(done[1], level + 1)
    return jnp.concatenate(owns[levels], axis=2)


def solution(mesh):
    in_specs = (
        P(None, ("scene", "pulse"), None),
        P(),
        P(),
        P(),
        P(None, ("scene", "pulse")),
        P(),
        P(),
    )
    out_specs = P(None, ("scene", "pulse"), None)
    return jax.shard_map(
        on_device, mesh=mesh, in_specs=in_specs, out_specs=out_specs, check_vma=False
    )
```

```python
import functools

import jax
import jax.numpy as jnp
from jax import lax
from jax.experimental import pallas as pl
from jax.experimental.pallas import tpu as pltpu
from jax.sharding import PartitionSpec as P

LANES = 128
TILE = 256
SCALE = 0.70710678


def prep_kernel(levels, beams, utaps, phases, rtaps, whole_ref, real_ref, mix_ref, plan_ref, band_ref, flat_ref):
    at_shifts, at_taps = levels, 2 * levels
    at_ukern, at_rkern = 2 * levels, 2 * levels + 2
    window = beams // 2 + utaps // 2
    myself = lax.axis_index("pulse")
    lane = lax.broadcasted_iota(jnp.int32, (1, 2 * beams), 1)
    first = lane < beams
    beam = jnp.where(first, lane, lane - beams)
    depth = beams // 2 + utaps
    row = lax.broadcasted_iota(jnp.int32, (depth, 2 * beams), 0)
    offset = row - beam // 2 - 1
    even = beam % 2 == 0
    halves = whole_ref[0:levels, :].astype(jnp.float32)
    shifts = whole_ref[at_shifts:at_shifts + levels, :].astype(jnp.float32)
    place = lax.broadcasted_iota(jnp.int32, (levels, LANES), 1)
    level_of = lax.broadcasted_iota(jnp.int32, (levels, LANES), 0)
    partner = jnp.bitwise_xor(myself, lax.shift_left(jnp.ones_like(level_of), level_of))

    def pick(table, index):
        return jnp.sum(jnp.where(place == index, table, 0.0), axis=1, keepdims=True)

    half_of = pick(halves, myself)
    after_of = jnp.concatenate([half_of[1:], half_of[:1]], axis=0)
    near_of = pick(shifts, myself) + LANES
    far_of = pick(shifts, partner) + LANES
    codes = ((half_of * 2 + after_of) * 256 + near_of) * 256 + far_of
    for level in range(levels):
        plan_ref[level] = jnp.broadcast_to(codes[level:level + 1, :], (8, LANES))
    kernel = real_ref[at_ukern:at_ukern + 2, :]
    band = jnp.zeros((depth, 2 * beams), jnp.float32)
    for k in range(utaps):
        value = jnp.where(even, kernel[0:1, k:k + 1], kernel[1:2, k:k + 1])
        band = jnp.where(offset == k, value, band)
    band_ref[...] = band
    table = real_ref[at_rkern:at_rkern + rtaps, :]
    for level in range(levels):
        low_half = half_of[level:level + 1, :] == 0.0
        bit = lax.rem(lax.shift_right_logical(myself, level), 2)
        near = jnp.where(
            low_half, band_ref[utaps // 2:utaps // 2 + window, :], band_ref[0:window, :]
        )
        chosen = whole_ref[at_taps + level:at_taps + level + 1, :]
        weights = []
        for tap in range(rtaps):
            weight = jnp.zeros((1, 2 * beams), jnp.float32)
            for phase in range(phases):
                weight = jnp.where(
                    chosen == phase, table[tap:tap + 1, phase:phase + 1], weight
                )
            weights.append(weight)
        for child in range(2):
            side = bit if child == 0 else 1 - bit
            angle = real_ref[pl.ds(2 * level + side, 1), :]
            turned = pltpu.roll(angle, beams, 1)
            angle = jnp.where(first == low_half, angle, turned)
            cosine = SCALE * jnp.cos(angle)
            sine = SCALE * jnp.sin(angle)
            factors = (jnp.where(first, cosine, sine), jnp.where(first, -sine, cosine))
            for tap in range(rtaps):
                for part in range(2):
                    place = ((child * rtaps + tap) * 2 + part) * window
                    flat_ref[place:place + window, :] = near * (factors[part] * weights[tap])
        for block in range(flat_ref.shape[0] // LANES):
            mixed = flat_ref[block * LANES:(block + 1) * LANES, :].T
            high = mixed.astype(jnp.bfloat16)
            low = (mixed - high.astype(jnp.float32)).astype(jnp.bfloat16)
            columns = pl.ds(block * LANES, LANES)
            mix_ref[level, 0:2 * beams, columns] = high
            mix_ref[level, 2 * beams:4 * beams, columns] = low


def stacked(height, pieces):
    total = jnp.zeros((height, LANES), pieces[0][0].dtype)
    for piece, top, left in pieces:
        below, right = height - top - piece.shape[0], LANES - left - piece.shape[1]
        zero = jnp.zeros((), piece.dtype)
        total = total + lax.pad(piece, zero, ((top, below, 0), (left, right, 0)))
    return total


def mixing(ukern, rkern, angles, taps, shifts, half_table):
    levels = half_table.shape[0]
    beams = taps.shape[1]
    utaps = ukern.shape[1]
    phases, rtaps = rkern.shape
    window = beams // 2 + utaps // 2
    depth = 2 * rtaps * 2 * window
    vmem = pl.BlockSpec(memory_space=pltpu.VMEM)

    whole = stacked(
        3 * levels,
        [
            (half_table, 0, 0),
            (shifts, levels, 0),
            (taps, 2 * levels, 0),
            (taps, 2 * levels, beams),
        ],
    )
    real = stacked(
        2 * levels + 2 + rtaps,
        [
            (angles.reshape(2 * levels, 2 * beams), 0, 0),
            (ukern.astype(jnp.float32), 2 * levels, 0),
            (rkern.T, 2 * levels + 2, 0),
        ],
    )
    return pl.pallas_call(
        functools.partial(prep_kernel, levels, beams, utaps, phases, rtaps),
        out_shape=[
            jax.ShapeDtypeStruct((levels, 4 * beams, depth), jnp.bfloat16),
            jax.ShapeDtypeStruct((levels, 8, LANES), jnp.float32),
        ],
        in_specs=[vmem, vmem],
        out_specs=[vmem, vmem],
        scratch_shapes=[
            pltpu.VMEM((beams // 2 + utaps, 2 * beams), jnp.float32),
            pltpu.VMEM((depth, 2 * beams), jnp.float32),
        ],
        compiler_params=pltpu.CompilerParams(vmem_limit_bytes=24 * 2**20),
        cost_estimate=pl.CostEstimate(
            flops=2 * 10**9, bytes_accessed=2 * levels * 4 * beams * depth, transcendentals=0
        ),
        name="mixing",
    )(whole, real)


def merge_kernel(level, plan, start, stop, length, beams, window, rtaps, last, *refs):
    code_ref, mix_ref = refs[:2]
    count = len(plan)
    own_refs, far_refs = refs[2:2 + count], refs[2 + count:2 + 2 * count]
    outs = refs[3 + 2 * count:]
    out_ref = outs[0]
    send_ref = None if last else outs[1]
    wide_ref, even_ref, odd_ref, held_ref = outs[1 if last else 2:]
    code = jnp.max(code_ref[level]).astype(jnp.int32)
    half, following = code // 131072, code // 65536 % 2
    shifts = (code // 256 % 256 - LANES, code % 256 - LANES)
    rows = pl.ds(pl.multiple_of(half * (beams - window), 16), window)
    base = start - LANES
    for number, (piece, source, target, width) in enumerate(plan):
        for child, ref in ((0, own_refs[number]), (1, far_refs[number])):
            taken = rows if ref.shape[1] == beams else pl.ds(0, window)
            for part in range(2):
                wide_ref[child, part, :, target - base:target - base + width] = ref[
                    part, taken, source:source + width
                ]
    edge = jnp.zeros((2, 2, window, LANES), jnp.bfloat16)
    if base < 0:
        wide_ref[:, :, :, 0:LANES] = edge
    if stop + LANES > length:
        wide_ref[:, :, :, stop - base:stop - base + LANES] = edge
    span = stop - start
    tiles = pl.cdiv(span, TILE)
    lane = lax.broadcasted_iota(jnp.int32, (2 * window, LANES), 1).astype(jnp.int16)
    moves = []
    for child in range(2):
        for tap in range(rtaps):
            shift = shifts[child] + (tap - 1 + LANES)
            part_tile = lax.rem(shift, LANES)
            kept = jnp.full((2 * window, LANES), LANES - part_tile, jnp.int32).astype(jnp.int16)
            turn = lax.rem(LANES - part_tile, LANES)
            moves.append((child, tap, shift // LANES * LANES, turn, lane < kept))

    def rolled(child, at, turn):
        piece = wide_ref[child, :, :, pl.ds(pl.multiple_of(at, LANES), LANES)]
        return pltpu.roll(piece.reshape(2 * window, LANES), turn, 1)

    def build(stack_ref, step):
        for number, (child, tap, whole, turn, kept) in enumerate(moves):
            place = (child * rtaps + tap) * 2 * window
            held = held_ref[number]
            for block in range(TILE // LANES):
                piece = rolled(child, step * TILE + whole + (block + 1) * LANES, turn)
                columns = pl.ds(block * LANES, LANES)
                stack_ref[place:place + 2 * window, columns] = jnp.where(kept, held, piece)
                held = piece
            held_ref[number] = held

    def multiply(stack_ref, step):
        column = pl.multiple_of(step * TILE, TILE)
        both = jnp.dot(mix_ref[level], stack_ref[...], preferred_element_type=jnp.float32)
        total = (both[:2 * beams] + both[2 * beams:]).astype(jnp.bfloat16)
        out_ref[:, :, pl.ds(column, TILE)] = total.reshape(2, beams, TILE)

    def two_tiles(pair, carry):
        build(odd_ref, 2 * pair + 1)
        multiply(even_ref, 2 * pair)
        build(even_ref, 2 * pair + 2)
        multiply(odd_ref, 2 * pair + 1)
        return carry

    for number, (child, tap, whole, turn, kept) in enumerate(moves):
        held_ref[number] = rolled(child, whole, turn)
    build(even_ref, 0)
    lax.fori_loop(0, tiles // 2, two_tiles, 0)
    if tiles % 2 == 1:
        multiply(even_ref, tiles - 1)
    if not last:
        other = pl.ds(pl.multiple_of((1 - following) * (beams - window), 16), window)
        send_ref[...] = out_ref[:, other, :span]


def pieces_of(bounds, start, stop):
    found = []
    for chunk in range(len(bounds) - 1):
        low, high = max(bounds[chunk], start), min(bounds[chunk + 1], stop)
        if low < high:
            found.append((chunk, low - bounds[chunk], low, high - low))
    return found


def merge(level, levels, codes, mix, own, far, bounds, start, stop, sizes, before):
    beams, window, rtaps, length = sizes
    last = level == levels - 1
    plan = pieces_of(bounds, max(start - LANES, 0), min(stop + LANES, length))
    span = stop - start
    vmem = pl.BlockSpec(memory_space=pltpu.VMEM)
    anywhere = pl.BlockSpec(memory_space=pl.ANY)
    depth = mix.shape[2]
    padded = pl.cdiv(span, TILE) * TILE
    out_shape = [jax.ShapeDtypeStruct((2, beams, padded), jnp.bfloat16)]
    if not last:
        out_shape.append(jax.ShapeDtypeStruct((2, window, span), jnp.bfloat16))
    return pl.pallas_call(
        functools.partial(
            merge_kernel, level, plan, start, stop, length, beams, window, rtaps, last
        ),
        out_shape=out_shape,
        in_specs=[vmem, vmem] + [vmem] * (2 * len(plan)) + [anywhere],
        out_specs=[vmem] * len(out_shape),
        scratch_shapes=[
            pltpu.VMEM((2, 2, window, padded + TILE + 2 * LANES), jnp.bfloat16),
            pltpu.VMEM((depth, TILE), jnp.bfloat16),
            pltpu.VMEM((depth, TILE), jnp.bfloat16),
            pltpu.VMEM((2 * rtaps, 2 * window, LANES), jnp.bfloat16),
        ],
        compiler_params=pltpu.CompilerParams(vmem_limit_bytes=24 * 2**20),
        cost_estimate=pl.CostEstimate(
            flops=32 * beams * depth * span,
            bytes_accessed=0,
            transcendentals=0,
        ),
        name=f"merge_{level}",
    )(
        codes,
        mix,
        *[own[piece[0]] for piece in plan],
        *[far[piece[0]] for piece in plan],
        before,
    )


MARKS = (
    (6, 12, 24),
    (5, 11, 17, 23, 29),
    (4, 10, 16, 22, 27),
    (1, 3, 8, 22, 26),
)
ORDER = (
    (0, 0), (0, 1), (0, 2), (1, 0), (1, 1), (2, 0), (1, 2), (2, 1), (0, 3), (1, 3), (2, 2),
    (3, 0), (1, 4), (2, 3), (3, 1), (3, 2), (1, 5), (2, 4), (2, 5), (3, 3), (3, 4), (3, 5),
)


def chunk_bounds(level, levels, length):
    marks = MARKS[len(MARKS) - 1 - min(levels - level, len(MARKS) - 1)]
    tiles = length // LANES
    return [0] + [tiles * mark // 32 * LANES for mark in marks] + [length]


def merge_order(levels, bounds):
    if levels == len(MARKS):
        return ORDER
    length = bounds[0][-1]
    made = [0] * levels
    order = []
    while len(order) < sum(len(bound) - 1 for bound in bounds[1:]):
        ready = []
        for level in range(levels):
            chunk = made[level]
            if chunk < len(bounds[level + 1]) - 1:
                stop = min(bounds[level + 1][chunk + 1] + LANES, length)
                needed = len(pieces_of(bounds[level], 0, stop))
                if level == 0 or needed <= made[level - 1]:
                    ready.append((level + chunk, level, chunk))
        _, level, chunk = min(ready)
        made[level] += 1
        order.append((level, chunk))
    return order


def from_partner(value, bit):
    mask = 1 << bit
    pairs = [(source, source ^ mask) for source in range(lax.axis_size("pulse"))]
    return lax.ppermute(value, "pulse", pairs)


def on_device(beams_in, ukern, rkern, angles, taps, shifts, half_table):
    beams, length = beams_in.shape[1:]
    utaps, rtaps = ukern.shape[1], rkern.shape[1]
    window = beams // 2 + utaps // 2
    levels = half_table.shape[0]
    sizes = (beams, window, rtaps, length)
    bounds = [[0, length]]
    bounds += [chunk_bounds(level, levels, length) for level in range(1, levels + 1)]
    mix, codes = mixing(ukern, rkern, angles, taps, shifts, half_table)
    owns = [[beams_in]] + [[None] * (len(bound) - 1) for bound in bounds[1:]]
    fars = [[from_partner(beams_in, 0)]] + [[None] * (len(bound) - 1) for bound in bounds[1:]]
    before = mix
    for level, chunk in merge_order(levels, bounds):
        start, stop = bounds[level + 1][chunk], bounds[level + 1][chunk + 1]
        done = merge(
            level, levels, codes, mix, owns[level], fars[level], bounds[level],
            start, stop, sizes, before,
        )
        before = owns[level + 1][chunk] = done[0]
        if level < levels - 1:
            fars[level + 1][chunk] = from_partner(done[1], level + 1)
    edges = bounds[levels]
    made = [part[:, :, :high - low] for part, low, high in zip(owns[levels], edges, edges[1:])]
    return jnp.concatenate(made, axis=2)


def solution(mesh):
    in_specs = (
        P(None, ("scene", "pulse"), None),
        P(),
        P(),
        P(),
        P(None, ("scene", "pulse")),
        P(),
        P(),
    )
    out_specs = P(None, ("scene", "pulse"), None)
    return jax.shard_map(
        on_device, mesh=mesh, in_specs=in_specs, out_specs=out_specs, check_vma=False
    )
```

```python
import functools

import jax
import jax.numpy as jnp
from jax import lax
from jax.experimental import pallas as pl
from jax.experimental.pallas import tpu as pltpu
from jax.sharding import PartitionSpec as P

LANES = 128
TILE = 256
SCALE = 0.70710678


def prep_kernel(levels, beams, utaps, phases, rtaps, whole_ref, real_ref, mix_ref, plan_ref, band_ref, flat_ref):
    at_shifts, at_taps = levels, 2 * levels
    at_ukern, at_rkern = 2 * levels, 2 * levels + 2
    window = beams // 2 + utaps // 2
    myself = lax.axis_index("pulse")
    lane = lax.broadcasted_iota(jnp.int32, (1, 2 * beams), 1)
    first = lane < beams
    beam = jnp.where(first, lane, lane - beams)
    depth = beams // 2 + utaps
    row = lax.broadcasted_iota(jnp.int32, (depth, 2 * beams), 0)
    offset = row - beam // 2 - 1
    even = beam % 2 == 0
    halves = whole_ref[0:levels, :].astype(jnp.float32)
    shifts = whole_ref[at_shifts:at_shifts + levels, :].astype(jnp.float32)
    place = lax.broadcasted_iota(jnp.int32, (levels, LANES), 1)
    level_of = lax.broadcasted_iota(jnp.int32, (levels, LANES), 0)
    partner = jnp.bitwise_xor(myself, lax.shift_left(jnp.ones_like(level_of), level_of))

    def pick(table, index):
        return jnp.sum(jnp.where(place == index, table, 0.0), axis=1, keepdims=True)

    half_of = pick(halves, myself)
    after_of = jnp.concatenate([half_of[1:], half_of[:1]], axis=0)
    near_of = pick(shifts, myself) + LANES
    far_of = pick(shifts, partner) + LANES
    codes = ((half_of * 2 + after_of) * 256 + near_of) * 256 + far_of
    for level in range(levels):
        plan_ref[level] = jnp.broadcast_to(codes[level:level + 1, :], (8, LANES))
    kernel = real_ref[at_ukern:at_ukern + 2, :]
    band = jnp.zeros((depth, 2 * beams), jnp.float32)
    for k in range(utaps):
        value = jnp.where(even, kernel[0:1, k:k + 1], kernel[1:2, k:k + 1])
        band = jnp.where(offset == k, value, band)
    band_ref[...] = band
    table = real_ref[at_rkern:at_rkern + rtaps, :]
    for level in range(levels):
        low_half = half_of[level:level + 1, :] == 0.0
        bit = lax.rem(lax.shift_right_logical(myself, level), 2)
        near = jnp.where(
            low_half, band_ref[utaps // 2:utaps // 2 + window, :], band_ref[0:window, :]
        )
        chosen = whole_ref[at_taps + level:at_taps + level + 1, :]
        weights = []
        for tap in range(rtaps):
            weight = jnp.zeros((1, 2 * beams), jnp.float32)
            for phase in range(phases):
                weight = jnp.where(
                    chosen == phase, table[tap:tap + 1, phase:phase + 1], weight
                )
            weights.append(weight)
        for child in range(2):
            side = bit if child == 0 else 1 - bit
            angle = real_ref[pl.ds(2 * level + side, 1), :]
            turned = pltpu.roll(angle, beams, 1)
            angle = jnp.where(first == low_half, angle, turned)
            cosine = SCALE * jnp.cos(angle)
            sine = SCALE * jnp.sin(angle)
            factors = (jnp.where(first, cosine, sine), jnp.where(first, -sine, cosine))
            for tap in range(rtaps):
                for part in range(2):
                    place = ((child * rtaps + tap) * 2 + part) * window
                    flat_ref[place:place + window, :] = near * (factors[part] * weights[tap])
        for block in range(flat_ref.shape[0] // LANES):
            mixed = flat_ref[block * LANES:(block + 1) * LANES, :].T
            high = mixed.astype(jnp.bfloat16)
            low = (mixed - high.astype(jnp.float32)).astype(jnp.bfloat16)
            columns = pl.ds(block * LANES, LANES)
            mix_ref[level, 0:2 * beams, columns] = high
            mix_ref[level, 2 * beams:4 * beams, columns] = low


def stacked(height, pieces):
    total = jnp.zeros((height, LANES), pieces[0][0].dtype)
    for piece, top, left in pieces:
        below, right = height - top - piece.shape[0], LANES - left - piece.shape[1]
        zero = jnp.zeros((), piece.dtype)
        total = total + lax.pad(piece, zero, ((top, below, 0), (left, right, 0)))
    return total


def mixing(ukern, rkern, angles, taps, shifts, half_table):
    levels = half_table.shape[0]
    beams = taps.shape[1]
    utaps = ukern.shape[1]
    phases, rtaps = rkern.shape
    window = beams // 2 + utaps // 2
    depth = 2 * rtaps * 2 * window
    vmem = pl.BlockSpec(memory_space=pltpu.VMEM)

    whole = stacked(
        3 * levels,
        [
            (half_table, 0, 0),
            (shifts, levels, 0),
            (taps, 2 * levels, 0),
            (taps, 2 * levels, beams),
        ],
    )
    real = stacked(
        2 * levels + 2 + rtaps,
        [
            (angles.reshape(2 * levels, 2 * beams), 0, 0),
            (ukern.astype(jnp.float32), 2 * levels, 0),
            (rkern.T, 2 * levels + 2, 0),
        ],
    )
    return pl.pallas_call(
        functools.partial(prep_kernel, levels, beams, utaps, phases, rtaps),
        out_shape=[
            jax.ShapeDtypeStruct((levels, 4 * beams, depth), jnp.bfloat16),
            jax.ShapeDtypeStruct((levels, 8, LANES), jnp.float32),
        ],
        in_specs=[vmem, vmem],
        out_specs=[vmem, vmem],
        scratch_shapes=[
            pltpu.VMEM((beams // 2 + utaps, 2 * beams), jnp.float32),
            pltpu.VMEM((depth, 2 * beams), jnp.float32),
        ],
        compiler_params=pltpu.CompilerParams(vmem_limit_bytes=24 * 2**20),
        cost_estimate=pl.CostEstimate(
            flops=2 * 10**9, bytes_accessed=2 * levels * 4 * beams * depth, transcendentals=0
        ),
        name="mixing",
    )(whole, real)


def merge_kernel(level, plan, start, stop, length, beams, window, rtaps, last, *refs):
    code_ref, mix_ref = refs[:2]
    count = len(plan)
    own_refs, far_refs = refs[2:2 + count], refs[2 + count:2 + 2 * count]
    outs = refs[3 + 2 * count:]
    out_ref = outs[0]
    send_ref = None if last else outs[1]
    wide_ref, even_ref, odd_ref, held_ref = outs[1 if last else 2:]
    code = jnp.max(code_ref[level]).astype(jnp.int32)
    half, following = code // 131072, code // 65536 % 2
    shifts = (code // 256 % 256 - LANES, code % 256 - LANES)
    rows = pl.ds(pl.multiple_of(half * (beams - window), 16), window)
    base = start - LANES
    for number, (piece, source, target, width) in enumerate(plan):
        for child, ref in ((0, own_refs[number]), (1, far_refs[number])):
            taken = rows if ref.shape[1] == beams else pl.ds(0, window)
            for part in range(2):
                wide_ref[child, part, :, target - base:target - base + width] = ref[
                    part, taken, source:source + width
                ]
    edge = jnp.zeros((2, 2, window, LANES), jnp.bfloat16)
    if base < 0:
        wide_ref[:, :, :, 0:LANES] = edge
    if stop + LANES > length:
        wide_ref[:, :, :, stop - base:stop - base + LANES] = edge
    span = stop - start
    tiles = pl.cdiv(span, TILE)
    lane = lax.broadcasted_iota(jnp.int32, (2 * window, LANES), 1).astype(jnp.int16)
    moves = []
    for child in range(2):
        for tap in range(rtaps):
            shift = shifts[child] + (tap - 1 + LANES)
            part_tile = lax.rem(shift, LANES)
            kept = jnp.full((2 * window, LANES), LANES - part_tile, jnp.int32).astype(jnp.int16)
            turn = lax.rem(LANES - part_tile, LANES)
            moves.append((child, tap, shift // LANES * LANES, turn, lane < kept))

    def rolled(child, at, turn):
        piece = wide_ref[child, :, :, pl.ds(pl.multiple_of(at, LANES), LANES)]
        return pltpu.roll(piece.reshape(2 * window, LANES), turn, 1)

    def build(stack_ref, step):
        for number, (child, tap, whole, turn, kept) in enumerate(moves):
            place = (child * rtaps + tap) * 2 * window
            held = held_ref[number]
            for block in range(TILE // LANES):
                piece = rolled(child, step * TILE + whole + (block + 1) * LANES, turn)
                columns = pl.ds(block * LANES, LANES)
                stack_ref[place:place + 2 * window, columns] = jnp.where(kept, held, piece)
                held = piece
            held_ref[number] = held

    def multiply(stack_ref, step):
        column = pl.multiple_of(step * TILE, TILE)
        both = jnp.dot(mix_ref[level], stack_ref[...], preferred_element_type=jnp.float32)
        total = (both[:2 * beams] + both[2 * beams:]).astype(jnp.bfloat16)
        out_ref[:, :, pl.ds(column, TILE)] = total.reshape(2, beams, TILE)

    def two_tiles(pair, carry):
        build(odd_ref, 2 * pair + 1)
        multiply(even_ref, 2 * pair)
        build(even_ref, 2 * pair + 2)
        multiply(odd_ref, 2 * pair + 1)
        return carry

    for number, (child, tap, whole, turn, kept) in enumerate(moves):
        held_ref[number] = rolled(child, whole, turn)
    build(even_ref, 0)
    lax.fori_loop(0, (tiles - 1) // 2, two_tiles, 0)
    if tiles % 2 == 1:
        multiply(even_ref, tiles - 1)
    else:
        build(odd_ref, tiles - 1)
        multiply(even_ref, tiles - 2)
        multiply(odd_ref, tiles - 1)
    if not last:
        other = pl.ds(pl.multiple_of((1 - following) * (beams - window), 16), window)
        send_ref[...] = out_ref[:, other, :span]


def pieces_of(bounds, start, stop):
    found = []
    for chunk in range(len(bounds) - 1):
        low, high = max(bounds[chunk], start), min(bounds[chunk + 1], stop)
        if low < high:
            found.append((chunk, low - bounds[chunk], low, high - low))
    return found


def merge(level, levels, codes, mix, own, far, bounds, start, stop, sizes, before):
    beams, window, rtaps, length = sizes
    last = level == levels - 1
    plan = pieces_of(bounds, max(start - LANES, 0), min(stop + LANES, length))
    span = stop - start
    vmem = pl.BlockSpec(memory_space=pltpu.VMEM)
    anywhere = pl.BlockSpec(memory_space=pl.ANY)
    depth = mix.shape[2]
    padded = pl.cdiv(span, TILE) * TILE
    out_shape = [jax.ShapeDtypeStruct((2, beams, padded), jnp.bfloat16)]
    if not last:
        out_shape.append(jax.ShapeDtypeStruct((2, window, span), jnp.bfloat16))
    return pl.pallas_call(
        functools.partial(
            merge_kernel, level, plan, start, stop, length, beams, window, rtaps, last
        ),
        out_shape=out_shape,
        in_specs=[vmem, vmem] + [vmem] * (2 * len(plan)) + [anywhere],
        out_specs=[vmem] * len(out_shape),
        scratch_shapes=[
            pltpu.VMEM((2, 2, window, padded + TILE + 2 * LANES), jnp.bfloat16),
            pltpu.VMEM((depth, TILE), jnp.bfloat16),
            pltpu.VMEM((depth, TILE), jnp.bfloat16),
            pltpu.VMEM((2 * rtaps, 2 * window, LANES), jnp.bfloat16),
        ],
        compiler_params=pltpu.CompilerParams(vmem_limit_bytes=24 * 2**20),
        cost_estimate=pl.CostEstimate(
            flops=(8 if last else 32) * beams * depth * span,
            bytes_accessed=0,
            transcendentals=0,
        ),
        name=f"merge_{level}",
    )(
        codes,
        mix,
        *[own[piece[0]] for piece in plan],
        *[far[piece[0]] for piece in plan],
        before,
    )


MARKS = (
    (6, 13, 26),
    (5, 12, 20, 25),
    (4, 11, 17, 24, 29),
    (7, 15, 21, 28),
)
ORDER = (
    (0, 0), (0, 1), (0, 2), (1, 0), (1, 1), (2, 0), (1, 2), (2, 1), (1, 3), (0, 3), (2, 2),
    (3, 0), (1, 4), (2, 3), (3, 1), (2, 4), (3, 2), (2, 5), (3, 3), (3, 4),
)


def chunk_bounds(level, levels, length):
    marks = MARKS[len(MARKS) - 1 - min(levels - level, len(MARKS) - 1)]
    tiles = length // LANES
    return [0] + [tiles * mark // 32 * LANES for mark in marks] + [length]


def merge_order(levels, bounds):
    if levels == len(MARKS):
        return ORDER
    length = bounds[0][-1]
    made = [0] * levels
    order = []
    while len(order) < sum(len(bound) - 1 for bound in bounds[1:]):
        ready = []
        for level in range(levels):
            chunk = made[level]
            if chunk < len(bounds[level + 1]) - 1:
                stop = min(bounds[level + 1][chunk + 1] + LANES, length)
                needed = len(pieces_of(bounds[level], 0, stop))
                if level == 0 or needed <= made[level - 1]:
                    ready.append((level + chunk, level, chunk))
        _, level, chunk = min(ready)
        made[level] += 1
        order.append((level, chunk))
    return order


def from_partner(value, bit):
    mask = 1 << bit
    pairs = [(source, source ^ mask) for source in range(lax.axis_size("pulse"))]
    return lax.ppermute(value, "pulse", pairs)


def on_device(beams_in, ukern, rkern, angles, taps, shifts, half_table):
    beams, length = beams_in.shape[1:]
    utaps, rtaps = ukern.shape[1], rkern.shape[1]
    window = beams // 2 + utaps // 2
    levels = half_table.shape[0]
    sizes = (beams, window, rtaps, length)
    bounds = [[0, length]]
    bounds += [chunk_bounds(level, levels, length) for level in range(1, levels + 1)]
    mix, codes = mixing(ukern, rkern, angles, taps, shifts, half_table)
    owns = [[beams_in]] + [[None] * (len(bound) - 1) for bound in bounds[1:]]
    fars = [[from_partner(beams_in, 0)]] + [[None] * (len(bound) - 1) for bound in bounds[1:]]
    before = mix
    for level, chunk in merge_order(levels, bounds):
        start, stop = bounds[level + 1][chunk], bounds[level + 1][chunk + 1]
        done = merge(
            level, levels, codes, mix, owns[level], fars[level], bounds[level],
            start, stop, sizes, before,
        )
        before = owns[level + 1][chunk] = done[0]
        if level < levels - 1:
            fars[level + 1][chunk] = from_partner(done[1], level + 1)
    edges = bounds[levels]
    made = [part[:, :, :high - low] for part, low, high in zip(owns[levels], edges, edges[1:])]
    return jnp.concatenate(made, axis=2)


def solution(mesh):
    in_specs = (
        P(None, ("scene", "pulse"), None),
        P(),
        P(),
        P(),
        P(None, ("scene", "pulse")),
        P(),
        P(),
    )
    out_specs = P(None, ("scene", "pulse"), None)
    return jax.shard_map(
        on_device, mesh=mesh, in_specs=in_specs, out_specs=out_specs, check_vma=False
    )
```

```python
import functools

import jax
import jax.numpy as jnp
from jax import lax
from jax.experimental import pallas as pl
from jax.experimental.pallas import tpu as pltpu
from jax.sharding import PartitionSpec as P

LANES = 128
TILE = 256
SCALE = 0.70710678


def prep_kernel(levels, beams, utaps, phases, rtaps, whole_ref, real_ref, mix_ref, plan_ref, band_ref, flat_ref):
    at_shifts, at_taps = levels, 2 * levels
    at_ukern, at_rkern = 2 * levels, 2 * levels + 2
    window = beams // 2 + utaps // 2
    myself = lax.axis_index("pulse")
    lane = lax.broadcasted_iota(jnp.int32, (1, 2 * beams), 1)
    first = lane < beams
    beam = jnp.where(first, lane, lane - beams)
    depth = beams // 2 + utaps
    row = lax.broadcasted_iota(jnp.int32, (depth, 2 * beams), 0)
    offset = row - beam // 2 - 1
    even = beam % 2 == 0
    halves = whole_ref[0:levels, :].astype(jnp.float32)
    shifts = whole_ref[at_shifts:at_shifts + levels, :].astype(jnp.float32)
    place = lax.broadcasted_iota(jnp.int32, (levels, LANES), 1)
    level_of = lax.broadcasted_iota(jnp.int32, (levels, LANES), 0)
    partner = jnp.bitwise_xor(myself, lax.shift_left(jnp.ones_like(level_of), level_of))

    def pick(table, index):
        return jnp.sum(jnp.where(place == index, table, 0.0), axis=1, keepdims=True)

    half_of = pick(halves, myself)
    after_of = jnp.concatenate([half_of[1:], half_of[:1]], axis=0)
    near_of = pick(shifts, myself) + LANES
    far_of = pick(shifts, partner) + LANES
    codes = ((half_of * 2 + after_of) * 256 + near_of) * 256 + far_of
    for level in range(levels):
        plan_ref[level] = jnp.broadcast_to(codes[level:level + 1, :], (8, LANES))
    kernel = real_ref[at_ukern:at_ukern + 2, :]
    band = jnp.zeros((depth, 2 * beams), jnp.float32)
    for k in range(utaps):
        value = jnp.where(even, kernel[0:1, k:k + 1], kernel[1:2, k:k + 1])
        band = jnp.where(offset == k, value, band)
    band_ref[...] = band
    table = real_ref[at_rkern:at_rkern + rtaps, :]
    for level in range(levels):
        low_half = half_of[level:level + 1, :] == 0.0
        bit = lax.rem(lax.shift_right_logical(myself, level), 2)
        near = jnp.where(
            low_half, band_ref[utaps // 2:utaps // 2 + window, :], band_ref[0:window, :]
        )
        chosen = whole_ref[at_taps + level:at_taps + level + 1, :]
        weights = []
        for tap in range(rtaps):
            weight = jnp.zeros((1, 2 * beams), jnp.float32)
            for phase in range(phases):
                weight = jnp.where(
                    chosen == phase, table[tap:tap + 1, phase:phase + 1], weight
                )
            weights.append(weight)
        for child in range(2):
            side = bit if child == 0 else 1 - bit
            angle = real_ref[pl.ds(2 * level + side, 1), :]
            turned = pltpu.roll(angle, beams, 1)
            angle = jnp.where(first == low_half, angle, turned)
            cosine = SCALE * jnp.cos(angle)
            sine = SCALE * jnp.sin(angle)
            factors = (jnp.where(first, cosine, sine), jnp.where(first, -sine, cosine))
            for tap in range(rtaps):
                for part in range(2):
                    place = ((child * rtaps + tap) * 2 + part) * window
                    flat_ref[place:place + window, :] = near * (factors[part] * weights[tap])
        for block in range(flat_ref.shape[0] // LANES):
            mixed = flat_ref[block * LANES:(block + 1) * LANES, :].T
            high = mixed.astype(jnp.bfloat16)
            low = (mixed - high.astype(jnp.float32)).astype(jnp.bfloat16)
            columns = pl.ds(block * LANES, LANES)
            mix_ref[level, 0:2 * beams, columns] = high
            mix_ref[level, 2 * beams:4 * beams, columns] = low


def stacked(height, pieces):
    total = jnp.zeros((height, LANES), pieces[0][0].dtype)
    for piece, top, left in pieces:
        below, right = height - top - piece.shape[0], LANES - left - piece.shape[1]
        zero = jnp.zeros((), piece.dtype)
        total = total + lax.pad(piece, zero, ((top, below, 0), (left, right, 0)))
    return total


def mixing(ukern, rkern, angles, taps, shifts, half_table):
    levels = half_table.shape[0]
    beams = taps.shape[1]
    utaps = ukern.shape[1]
    phases, rtaps = rkern.shape
    window = beams // 2 + utaps // 2
    depth = 2 * rtaps * 2 * window
    vmem = pl.BlockSpec(memory_space=pltpu.VMEM)

    whole = stacked(
        3 * levels,
        [
            (half_table, 0, 0),
            (shifts, levels, 0),
            (taps, 2 * levels, 0),
            (taps, 2 * levels, beams),
        ],
    )
    real = stacked(
        2 * levels + 2 + rtaps,
        [
            (angles.reshape(2 * levels, 2 * beams), 0, 0),
            (ukern.astype(jnp.float32), 2 * levels, 0),
            (rkern.T, 2 * levels + 2, 0),
        ],
    )
    return pl.pallas_call(
        functools.partial(prep_kernel, levels, beams, utaps, phases, rtaps),
        out_shape=[
            jax.ShapeDtypeStruct((levels, 4 * beams, depth), jnp.bfloat16),
            jax.ShapeDtypeStruct((levels, 8, LANES), jnp.float32),
        ],
        in_specs=[vmem, vmem],
        out_specs=[vmem, vmem],
        scratch_shapes=[
            pltpu.VMEM((beams // 2 + utaps, 2 * beams), jnp.float32),
            pltpu.VMEM((depth, 2 * beams), jnp.float32),
        ],
        compiler_params=pltpu.CompilerParams(vmem_limit_bytes=24 * 2**20),
        cost_estimate=pl.CostEstimate(
            flops=2 * 10**9, bytes_accessed=2 * levels * 4 * beams * depth, transcendentals=0
        ),
        name="mixing",
    )(whole, real)


def merge_kernel(level, plan, start, stop, length, beams, window, rtaps, last, *refs):
    code_ref, mix_ref = refs[:2]
    count = len(plan)
    own_refs, far_refs = refs[2:2 + count], refs[2 + count:2 + 2 * count]
    outs = refs[3 + 2 * count:]
    out_ref = outs[0]
    send_ref = None if last else outs[1]
    wide_ref, even_ref, odd_ref, held_ref = outs[1 if last else 2:]
    code = jnp.max(code_ref[level]).astype(jnp.int32)
    half, following = code // 131072, code // 65536 % 2
    shifts = (code // 256 % 256 - LANES, code % 256 - LANES)
    rows = pl.ds(pl.multiple_of(half * (beams - window), 16), window)
    base = start - LANES
    for number, (piece, source, target, width) in enumerate(plan):
        for child, ref in ((0, own_refs[number]), (1, far_refs[number])):
            taken = rows if ref.shape[1] == beams else pl.ds(0, window)
            for part in range(2):
                wide_ref[child, part, :, target - base:target - base + width] = ref[
                    part, taken, source:source + width
                ]
    edge = jnp.zeros((2, 2, window, LANES), jnp.bfloat16)
    if base < 0:
        wide_ref[:, :, :, 0:LANES] = edge
    if stop + LANES > length:
        wide_ref[:, :, :, stop - base:stop - base + LANES] = edge
    span = stop - start
    tiles = pl.cdiv(span, TILE)
    lane = lax.broadcasted_iota(jnp.int32, (2 * window, LANES), 1).astype(jnp.int16)
    moves = []
    for child in range(2):
        for tap in range(rtaps):
            shift = shifts[child] + (tap - 1 + LANES)
            part_tile = lax.rem(shift, LANES)
            kept = jnp.full((2 * window, LANES), LANES - part_tile, jnp.int32).astype(jnp.int16)
            turn = lax.rem(LANES - part_tile, LANES)
            moves.append((child, tap, shift // LANES * LANES, turn, lane < kept))

    def rolled(child, at, turn):
        piece = wide_ref[child, :, :, pl.ds(pl.multiple_of(at, LANES), LANES)]
        return pltpu.roll(piece.reshape(2 * window, LANES), turn, 1)

    def build(stack_ref, step):
        for number, (child, tap, whole, turn, kept) in enumerate(moves):
            place = (child * rtaps + tap) * 2 * window
            held = held_ref[number]
            for block in range(TILE // LANES):
                piece = rolled(child, step * TILE + whole + (block + 1) * LANES, turn)
                columns = pl.ds(block * LANES, LANES)
                stack_ref[place:place + 2 * window, columns] = jnp.where(kept, held, piece)
                held = piece
            held_ref[number] = held

    def multiply(stack_ref, step):
        column = pl.multiple_of(step * TILE, TILE)
        both = jnp.dot(mix_ref[level], stack_ref[...], preferred_element_type=jnp.float32)
        total = (both[:2 * beams] + both[2 * beams:]).astype(jnp.bfloat16)
        out_ref[:, :, pl.ds(column, TILE)] = total.reshape(2, beams, TILE)

    def two_tiles(pair, carry):
        build(odd_ref, 2 * pair + 1)
        multiply(even_ref, 2 * pair)
        build(even_ref, 2 * pair + 2)
        multiply(odd_ref, 2 * pair + 1)
        return carry

    for number, (child, tap, whole, turn, kept) in enumerate(moves):
        held_ref[number] = rolled(child, whole, turn)
    build(even_ref, 0)
    lax.fori_loop(0, (tiles - 1) // 2, two_tiles, 0)
    if tiles % 2 == 1:
        multiply(even_ref, tiles - 1)
    else:
        build(odd_ref, tiles - 1)
        multiply(even_ref, tiles - 2)
        multiply(odd_ref, tiles - 1)
    if not last:
        other = pl.ds(pl.multiple_of((1 - following) * (beams - window), 16), window)
        send_ref[...] = out_ref[:, other, :span]


def pieces_of(bounds, start, stop):
    found = []
    for chunk in range(len(bounds) - 1):
        low, high = max(bounds[chunk], start), min(bounds[chunk + 1], stop)
        if low < high:
            found.append((chunk, low - bounds[chunk], low, high - low))
    return found


def merge(level, levels, codes, mix, own, far, bounds, start, stop, sizes, before):
    beams, window, rtaps, length = sizes
    last = level == levels - 1
    plan = pieces_of(bounds, max(start - LANES, 0), min(stop + LANES, length))
    span = stop - start
    vmem = pl.BlockSpec(memory_space=pltpu.VMEM)
    anywhere = pl.BlockSpec(memory_space=pl.ANY)
    depth = mix.shape[2]
    padded = pl.cdiv(span, TILE) * TILE
    out_shape = [jax.ShapeDtypeStruct((2, beams, padded), jnp.bfloat16)]
    if not last:
        out_shape.append(jax.ShapeDtypeStruct((2, window, span), jnp.bfloat16))
    return pl.pallas_call(
        functools.partial(
            merge_kernel, level, plan, start, stop, length, beams, window, rtaps, last
        ),
        out_shape=out_shape,
        in_specs=[vmem, vmem] + [vmem] * (2 * len(plan)) + [anywhere],
        out_specs=[vmem] * len(out_shape),
        scratch_shapes=[
            pltpu.VMEM((2, 2, window, padded + TILE + 2 * LANES), jnp.bfloat16),
            pltpu.VMEM((depth, TILE), jnp.bfloat16),
            pltpu.VMEM((depth, TILE), jnp.bfloat16),
            pltpu.VMEM((2 * rtaps, 2 * window, LANES), jnp.bfloat16),
        ],
        compiler_params=pltpu.CompilerParams(vmem_limit_bytes=24 * 2**20),
        cost_estimate=pl.CostEstimate(
            flops=(8 if last else 32) * beams * depth * span,
            bytes_accessed=0,
            transcendentals=0,
        ),
        name=f"merge_{level}",
    )(
        codes,
        mix,
        *[own[piece[0]] for piece in plan],
        *[far[piece[0]] for piece in plan],
        before,
    )


MARKS = (
    (8, 16),
    (7, 15, 21, 27),
    (6, 14, 20, 26),
    (5, 13, 25),
)
ORDER = (
    (0, 0), (0, 1), (0, 2), (1, 0), (1, 1), (2, 0), (1, 2), (2, 1), (1, 3), (3, 0), (1, 4),
    (2, 2), (3, 1), (2, 3), (2, 4), (3, 2), (3, 3),
)


def chunk_bounds(level, levels, length):
    marks = MARKS[len(MARKS) - 1 - min(levels - level, len(MARKS) - 1)]
    tiles = length // LANES
    return [0] + [tiles * mark // 32 * LANES for mark in marks] + [length]


def merge_order(levels, bounds):
    if levels == len(MARKS):
        return ORDER
    length = bounds[0][-1]
    made = [0] * levels
    order = []
    while len(order) < sum(len(bound) - 1 for bound in bounds[1:]):
        ready = []
        for level in range(levels):
            chunk = made[level]
            if chunk < len(bounds[level + 1]) - 1:
                stop = min(bounds[level + 1][chunk + 1] + LANES, length)
                needed = len(pieces_of(bounds[level], 0, stop))
                if level == 0 or needed <= made[level - 1]:
                    ready.append((level + chunk, level, chunk))
        _, level, chunk = min(ready)
        made[level] += 1
        order.append((level, chunk))
    return order


def from_partner(value, bit):
    mask = 1 << bit
    pairs = [(source, source ^ mask) for source in range(lax.axis_size("pulse"))]
    return lax.ppermute(value, "pulse", pairs)


def on_device(beams_in, ukern, rkern, angles, taps, shifts, half_table):
    beams, length = beams_in.shape[1:]
    utaps, rtaps = ukern.shape[1], rkern.shape[1]
    window = beams // 2 + utaps // 2
    levels = half_table.shape[0]
    sizes = (beams, window, rtaps, length)
    bounds = [[0, length]]
    bounds += [chunk_bounds(level, levels, length) for level in range(1, levels + 1)]
    mix, codes = mixing(ukern, rkern, angles, taps, shifts, half_table)
    owns = [[beams_in]] + [[None] * (len(bound) - 1) for bound in bounds[1:]]
    fars = [[from_partner(beams_in, 0)]] + [[None] * (len(bound) - 1) for bound in bounds[1:]]
    before = mix
    for level, chunk in merge_order(levels, bounds):
        start, stop = bounds[level + 1][chunk], bounds[level + 1][chunk + 1]
        done = merge(
            level, levels, codes, mix, owns[level], fars[level], bounds[level],
            start, stop, sizes, before,
        )
        before = owns[level + 1][chunk] = done[0]
        if level < levels - 1:
            fars[level + 1][chunk] = from_partner(done[1], level + 1)
    edges = bounds[levels]
    made = [part[:, :, :high - low] for part, low, high in zip(owns[levels], edges, edges[1:])]
    return jnp.concatenate(made, axis=2)


def solution(mesh):
    in_specs = (
        P(None, ("scene", "pulse"), None),
        P(),
        P(),
        P(),
        P(None, ("scene", "pulse")),
        P(),
        P(),
    )
    out_specs = P(None, ("scene", "pulse"), None)
    return jax.shard_map(
        on_device, mesh=mesh, in_specs=in_specs, out_specs=out_specs, check_vma=False
    )
```

```python
import functools

import jax
import jax.numpy as jnp
from jax import lax
from jax.experimental import pallas as pl
from jax.experimental.pallas import tpu as pltpu
from jax.sharding import PartitionSpec as P

LANES = 128
TILE = 256
SCALE = 0.70710678


def prep_kernel(levels, beams, utaps, phases, rtaps, whole_ref, real_ref, mix_ref, plan_ref, band_ref, flat_ref):
    at_shifts, at_taps = levels, 2 * levels
    at_ukern, at_rkern = 2 * levels, 2 * levels + 2
    window = beams // 2 + utaps // 2
    myself = lax.axis_index("pulse")
    lane = lax.broadcasted_iota(jnp.int32, (1, 2 * beams), 1)
    first = lane < beams
    beam = jnp.where(first, lane, lane - beams)
    depth = beams // 2 + utaps
    row = lax.broadcasted_iota(jnp.int32, (depth, 2 * beams), 0)
    offset = row - beam // 2 - 1
    even = beam % 2 == 0
    halves = whole_ref[0:levels, :].astype(jnp.float32)
    shifts = whole_ref[at_shifts:at_shifts + levels, :].astype(jnp.float32)
    place = lax.broadcasted_iota(jnp.int32, (levels, LANES), 1)
    level_of = lax.broadcasted_iota(jnp.int32, (levels, LANES), 0)
    partner = jnp.bitwise_xor(myself, lax.shift_left(jnp.ones_like(level_of), level_of))

    def pick(table, index):
        return jnp.sum(jnp.where(place == index, table, 0.0), axis=1, keepdims=True)

    half_of = pick(halves, myself)
    after_of = jnp.concatenate([half_of[1:], half_of[:1]], axis=0)
    near_of = pick(shifts, myself) + LANES
    far_of = pick(shifts, partner) + LANES
    codes = ((half_of * 2 + after_of) * 256 + near_of) * 256 + far_of
    for level in range(levels):
        plan_ref[level] = jnp.broadcast_to(codes[level:level + 1, :], (8, LANES))
    kernel = real_ref[at_ukern:at_ukern + 2, :]
    band = jnp.zeros((depth, 2 * beams), jnp.float32)
    for k in range(utaps):
        value = jnp.where(even, kernel[0:1, k:k + 1], kernel[1:2, k:k + 1])
        band = jnp.where(offset == k, value, band)
    band_ref[...] = band
    table = real_ref[at_rkern:at_rkern + rtaps, :]
    for level in range(levels):
        low_half = half_of[level:level + 1, :] == 0.0
        bit = lax.rem(lax.shift_right_logical(myself, level), 2)
        near = jnp.where(
            low_half, band_ref[utaps // 2:utaps // 2 + window, :], band_ref[0:window, :]
        )
        chosen = whole_ref[at_taps + level:at_taps + level + 1, :]
        weights = []
        for tap in range(rtaps):
            weight = jnp.zeros((1, 2 * beams), jnp.float32)
            for phase in range(phases):
                weight = jnp.where(
                    chosen == phase, table[tap:tap + 1, phase:phase + 1], weight
                )
            weights.append(weight)
        for child in range(2):
            side = bit if child == 0 else 1 - bit
            angle = real_ref[pl.ds(2 * level + side, 1), :]
            turned = pltpu.roll(angle, beams, 1)
            angle = jnp.where(first == low_half, angle, turned)
            cosine = SCALE * jnp.cos(angle)
            sine = SCALE * jnp.sin(angle)
            factors = (jnp.where(first, cosine, sine), jnp.where(first, -sine, cosine))
            for tap in range(rtaps):
                for part in range(2):
                    place = ((child * rtaps + tap) * 2 + part) * window
                    flat_ref[place:place + window, :] = near * (factors[part] * weights[tap])
        for block in range(flat_ref.shape[0] // LANES):
            mixed = flat_ref[block * LANES:(block + 1) * LANES, :].T
            high = mixed.astype(jnp.bfloat16)
            low = (mixed - high.astype(jnp.float32)).astype(jnp.bfloat16)
            columns = pl.ds(block * LANES, LANES)
            mix_ref[level, 0:2 * beams, columns] = high
            mix_ref[level, 2 * beams:4 * beams, columns] = low


def stacked(height, pieces):
    total = jnp.zeros((height, LANES), pieces[0][0].dtype)
    for piece, top, left in pieces:
        below, right = height - top - piece.shape[0], LANES - left - piece.shape[1]
        zero = jnp.zeros((), piece.dtype)
        total = total + lax.pad(piece, zero, ((top, below, 0), (left, right, 0)))
    return total


def mixing(ukern, rkern, angles, taps, shifts, half_table):
    levels = half_table.shape[0]
    beams = taps.shape[1]
    utaps = ukern.shape[1]
    phases, rtaps = rkern.shape
    window = beams // 2 + utaps // 2
    depth = 2 * rtaps * 2 * window
    vmem = pl.BlockSpec(memory_space=pltpu.VMEM)

    whole = stacked(
        3 * levels,
        [
            (half_table, 0, 0),
            (shifts, levels, 0),
            (taps, 2 * levels, 0),
            (taps, 2 * levels, beams),
        ],
    )
    real = stacked(
        2 * levels + 2 + rtaps,
        [
            (angles.reshape(2 * levels, 2 * beams), 0, 0),
            (ukern.astype(jnp.float32), 2 * levels, 0),
            (rkern.T, 2 * levels + 2, 0),
        ],
    )
    return pl.pallas_call(
        functools.partial(prep_kernel, levels, beams, utaps, phases, rtaps),
        out_shape=[
            jax.ShapeDtypeStruct((levels, 4 * beams, depth), jnp.bfloat16),
            jax.ShapeDtypeStruct((levels, 8, LANES), jnp.float32),
        ],
        in_specs=[vmem, vmem],
        out_specs=[vmem, vmem],
        scratch_shapes=[
            pltpu.VMEM((beams // 2 + utaps, 2 * beams), jnp.float32),
            pltpu.VMEM((depth, 2 * beams), jnp.float32),
        ],
        compiler_params=pltpu.CompilerParams(vmem_limit_bytes=24 * 2**20),
        cost_estimate=pl.CostEstimate(
            flops=2 * 10**9, bytes_accessed=2 * levels * 4 * beams * depth, transcendentals=0
        ),
        name="mixing",
    )(whole, real)


def merge_kernel(level, plan, start, stop, length, beams, window, rtaps, last, *refs):
    code_ref, mix_ref = refs[:2]
    count = len(plan)
    own_refs, far_refs = refs[2:2 + count], refs[2 + count:2 + 2 * count]
    outs = refs[3 + 2 * count:]
    out_ref = outs[0]
    send_ref = None if last else outs[1]
    wide_ref, even_ref, odd_ref, held_ref = outs[1 if last else 2:]
    code = jnp.max(code_ref[level]).astype(jnp.int32)
    half, following = code // 131072, code // 65536 % 2
    shifts = (code // 256 % 256 - LANES, code % 256 - LANES)
    rows = pl.ds(pl.multiple_of(half * (beams - window), 16), window)
    base = start - LANES
    for number, (piece, source, target, width) in enumerate(plan):
        for child, ref in ((0, own_refs[number]), (1, far_refs[number])):
            taken = rows if ref.shape[1] == beams else pl.ds(0, window)
            for part in range(2):
                wide_ref[child, part, :, target - base:target - base + width] = ref[
                    part, taken, source:source + width
                ]
    edge = jnp.zeros((2, 2, window, LANES), jnp.bfloat16)
    if base < 0:
        wide_ref[:, :, :, 0:LANES] = edge
    if stop + LANES > length:
        wide_ref[:, :, :, stop - base:stop - base + LANES] = edge
    span = stop - start
    tiles = pl.cdiv(span, TILE)
    lane = lax.broadcasted_iota(jnp.int32, (2 * window, LANES), 1).astype(jnp.int16)
    moves = []
    for child in range(2):
        for tap in range(rtaps):
            shift = shifts[child] + (tap - 1 + LANES)
            part_tile = lax.rem(shift, LANES)
            kept = jnp.full((2 * window, LANES), LANES - part_tile, jnp.int32).astype(jnp.int16)
            turn = lax.rem(LANES - part_tile, LANES)
            moves.append((child, tap, shift // LANES * LANES, turn, lane < kept))

    def rolled(child, at, turn):
        piece = wide_ref[child, :, :, pl.ds(pl.multiple_of(at, LANES), LANES)]
        return pltpu.roll(piece.reshape(2 * window, LANES), turn, 1)

    def build(stack_ref, step):
        for number, (child, tap, whole, turn, kept) in enumerate(moves):
            place = (child * rtaps + tap) * 2 * window
            held = held_ref[number]
            for block in range(TILE // LANES):
                piece = rolled(child, step * TILE + whole + (block + 1) * LANES, turn)
                columns = pl.ds(block * LANES, LANES)
                stack_ref[place:place + 2 * window, columns] = jnp.where(kept, held, piece)
                held = piece
            held_ref[number] = held

    def multiply(stack_ref, step):
        column = pl.multiple_of(step * TILE, TILE)
        both = jnp.dot(mix_ref[level], stack_ref[...], preferred_element_type=jnp.float32)
        total = (both[:2 * beams] + both[2 * beams:]).astype(jnp.bfloat16)
        out_ref[:, :, pl.ds(column, TILE)] = total.reshape(2, beams, TILE)

    def two_tiles(pair, carry):
        build(odd_ref, 2 * pair + 1)
        multiply(even_ref, 2 * pair)
        build(even_ref, 2 * pair + 2)
        multiply(odd_ref, 2 * pair + 1)
        return carry

    for number, (child, tap, whole, turn, kept) in enumerate(moves):
        held_ref[number] = rolled(child, whole, turn)
    build(even_ref, 0)
    lax.fori_loop(0, (tiles - 1) // 2, two_tiles, 0)
    if tiles % 2 == 1:
        multiply(even_ref, tiles - 1)
    else:
        build(odd_ref, tiles - 1)
        multiply(even_ref, tiles - 2)
        multiply(odd_ref, tiles - 1)
    if not last:
        other = pl.ds(pl.multiple_of((1 - following) * (beams - window), 16), window)
        send_ref[...] = out_ref[:, other, :span]


def pieces_of(bounds, start, stop):
    found = []
    for chunk in range(len(bounds) - 1):
        low, high = max(bounds[chunk], start), min(bounds[chunk + 1], stop)
        if low < high:
            found.append((chunk, low - bounds[chunk], low, high - low))
    return found


def merge(level, levels, codes, mix, own, far, bounds, start, stop, sizes, before):
    beams, window, rtaps, length = sizes
    last = level == levels - 1
    plan = pieces_of(bounds, max(start - LANES, 0), min(stop + LANES, length))
    span = stop - start
    vmem = pl.BlockSpec(memory_space=pltpu.VMEM)
    anywhere = pl.BlockSpec(memory_space=pl.ANY)
    depth = mix.shape[2]
    padded = pl.cdiv(span, TILE) * TILE
    out_shape = [jax.ShapeDtypeStruct((2, beams, padded), jnp.bfloat16)]
    if not last:
        out_shape.append(jax.ShapeDtypeStruct((2, window, span), jnp.bfloat16))
    return pl.pallas_call(
        functools.partial(
            merge_kernel, level, plan, start, stop, length, beams, window, rtaps, last
        ),
        out_shape=out_shape,
        in_specs=[vmem, vmem] + [vmem] * (2 * len(plan)) + [anywhere],
        out_specs=[vmem] * len(out_shape),
        scratch_shapes=[
            pltpu.VMEM((2, 2, window, padded + TILE + 2 * LANES), jnp.bfloat16),
            pltpu.VMEM((depth, TILE), jnp.bfloat16),
            pltpu.VMEM((depth, TILE), jnp.bfloat16),
            pltpu.VMEM((2 * rtaps, 2 * window, LANES), jnp.bfloat16),
        ],
        compiler_params=pltpu.CompilerParams(vmem_limit_bytes=24 * 2**20),
        cost_estimate=pl.CostEstimate(
            flops=(8 if last else 32) * beams * depth * span,
            bytes_accessed=0,
            transcendentals=0,
        ),
        name=f"merge_{level}",
    )(
        codes,
        mix,
        *[own[piece[0]] for piece in plan],
        *[far[piece[0]] for piece in plan],
        before,
    )


MARKS = (
    (8, 16),
    (7, 15, 21, 27),
    (6, 14, 20, 26),
    (5, 13, 19, 25),
)
ORDER = (
    (0, 0), (0, 1), (0, 2), (1, 0), (1, 1), (2, 0), (1, 2), (2, 1), (1, 3), (3, 0), (1, 4),
    (2, 2), (3, 1), (2, 3), (2, 4), (3, 2), (3, 3), (3, 4),
)


def chunk_bounds(level, levels, length):
    marks = MARKS[len(MARKS) - 1 - min(levels - level, len(MARKS) - 1)]
    tiles = length // LANES
    return [0] + [tiles * mark // 32 * LANES for mark in marks] + [length]


def merge_order(levels, bounds):
    if levels == len(MARKS):
        return ORDER
    length = bounds[0][-1]
    made = [0] * levels
    order = []
    while len(order) < sum(len(bound) - 1 for bound in bounds[1:]):
        ready = []
        for level in range(levels):
            chunk = made[level]
            if chunk < len(bounds[level + 1]) - 1:
                stop = min(bounds[level + 1][chunk + 1] + LANES, length)
                needed = len(pieces_of(bounds[level], 0, stop))
                if level == 0 or needed <= made[level - 1]:
                    ready.append((level + chunk, level, chunk))
        _, level, chunk = min(ready)
        made[level] += 1
        order.append((level, chunk))
    return order


def from_partner(value, bit):
    mask = 1 << bit
    pairs = [(source, source ^ mask) for source in range(lax.axis_size("pulse"))]
    return lax.ppermute(value, "pulse", pairs)


def on_device(beams_in, ukern, rkern, angles, taps, shifts, half_table):
    beams, length = beams_in.shape[1:]
    utaps, rtaps = ukern.shape[1], rkern.shape[1]
    window = beams // 2 + utaps // 2
    levels = half_table.shape[0]
    sizes = (beams, window, rtaps, length)
    bounds = [[0, length]]
    bounds += [chunk_bounds(level, levels, length) for level in range(1, levels + 1)]
    mix, codes = mixing(ukern, rkern, angles, taps, shifts, half_table)
    owns = [[beams_in]] + [[None] * (len(bound) - 1) for bound in bounds[1:]]
    fars = [[from_partner(beams_in, 0)]] + [[None] * (len(bound) - 1) for bound in bounds[1:]]
    before = mix
    for level, chunk in merge_order(levels, bounds):
        start, stop = bounds[level + 1][chunk], bounds[level + 1][chunk + 1]
        done = merge(
            level, levels, codes, mix, owns[level], fars[level], bounds[level],
            start, stop, sizes, before,
        )
        before = owns[level + 1][chunk] = done[0]
        if level < levels - 1:
            fars[level + 1][chunk] = from_partner(done[1], level + 1)
    edges = bounds[levels]
    made = [part[:, :, :high - low] for part, low, high in zip(owns[levels], edges, edges[1:])]
    return jnp.concatenate(made, axis=2)


def solution(mesh):
    in_specs = (
        P(None, ("scene", "pulse"), None),
        P(),
        P(),
        P(),
        P(None, ("scene", "pulse")),
        P(),
        P(),
    )
    out_specs = P(None, ("scene", "pulse"), None)
    return jax.shard_map(
        on_device, mesh=mesh, in_specs=in_specs, out_specs=out_specs, check_vma=False
    )
```

```python
import functools

import jax
import jax.numpy as jnp
from jax import lax
from jax.experimental import pallas as pl
from jax.experimental.pallas import tpu as pltpu
from jax.sharding import PartitionSpec as P

LANES = 128
TILE = 256
SCALE = 0.70710678


def prep_kernel(levels, beams, utaps, phases, rtaps, whole_ref, real_ref, mix_ref, plan_ref, band_ref, flat_ref):
    at_shifts, at_taps = levels, 2 * levels
    at_ukern, at_rkern = 2 * levels, 2 * levels + 2
    window = beams // 2 + utaps // 2
    myself = lax.axis_index("pulse")
    lane = lax.broadcasted_iota(jnp.int32, (1, 2 * beams), 1)
    first = lane < beams
    beam = jnp.where(first, lane, lane - beams)
    depth = beams // 2 + utaps
    row = lax.broadcasted_iota(jnp.int32, (depth, 2 * beams), 0)
    offset = row - beam // 2 - 1
    even = beam % 2 == 0
    halves = whole_ref[0:levels, :].astype(jnp.float32)
    shifts = whole_ref[at_shifts:at_shifts + levels, :].astype(jnp.float32)
    place = lax.broadcasted_iota(jnp.int32, (levels, LANES), 1)
    level_of = lax.broadcasted_iota(jnp.int32, (levels, LANES), 0)
    partner = jnp.bitwise_xor(myself, lax.shift_left(jnp.ones_like(level_of), level_of))

    def pick(table, index):
        return jnp.sum(jnp.where(place == index, table, 0.0), axis=1, keepdims=True)

    half_of = pick(halves, myself)
    after_of = jnp.concatenate([half_of[1:], half_of[:1]], axis=0)
    near_of = pick(shifts, myself) + LANES
    far_of = pick(shifts, partner) + LANES
    codes = ((half_of * 2 + after_of) * 256 + near_of) * 256 + far_of
    for level in range(levels):
        plan_ref[level] = jnp.broadcast_to(codes[level:level + 1, :], (8, LANES))
    kernel = real_ref[at_ukern:at_ukern + 2, :]
    band = jnp.zeros((depth, 2 * beams), jnp.float32)
    for k in range(utaps):
        value = jnp.where(even, kernel[0:1, k:k + 1], kernel[1:2, k:k + 1])
        band = jnp.where(offset == k, value, band)
    band_ref[...] = band
    table = real_ref[at_rkern:at_rkern + rtaps, :]
    for level in range(levels):
        low_half = half_of[level:level + 1, :] == 0.0
        bit = lax.rem(lax.shift_right_logical(myself, level), 2)
        near = jnp.where(
            low_half, band_ref[utaps // 2:utaps // 2 + window, :], band_ref[0:window, :]
        )
        chosen = whole_ref[at_taps + level:at_taps + level + 1, :]
        weights = []
        for tap in range(rtaps):
            weight = jnp.zeros((1, 2 * beams), jnp.float32)
            for phase in range(phases):
                weight = jnp.where(
                    chosen == phase, table[tap:tap + 1, phase:phase + 1], weight
                )
            weights.append(weight)
        for child in range(2):
            side = bit if child == 0 else 1 - bit
            angle = real_ref[pl.ds(2 * level + side, 1), :]
            turned = pltpu.roll(angle, beams, 1)
            angle = jnp.where(first == low_half, angle, turned)
            cosine = SCALE * jnp.cos(angle)
            sine = SCALE * jnp.sin(angle)
            factors = (jnp.where(first, cosine, sine), jnp.where(first, -sine, cosine))
            for tap in range(rtaps):
                for part in range(2):
                    place = ((child * rtaps + tap) * 2 + part) * window
                    flat_ref[place:place + window, :] = near * (factors[part] * weights[tap])
        for block in range(flat_ref.shape[0] // LANES):
            mixed = flat_ref[block * LANES:(block + 1) * LANES, :].T
            high = mixed.astype(jnp.bfloat16)
            low = (mixed - high.astype(jnp.float32)).astype(jnp.bfloat16)
            columns = pl.ds(block * LANES, LANES)
            mix_ref[level, 0:2 * beams, columns] = high
            mix_ref[level, 2 * beams:4 * beams, columns] = low


def stacked(height, pieces):
    total = jnp.zeros((height, LANES), pieces[0][0].dtype)
    for piece, top, left in pieces:
        below, right = height - top - piece.shape[0], LANES - left - piece.shape[1]
        zero = jnp.zeros((), piece.dtype)
        total = total + lax.pad(piece, zero, ((top, below, 0), (left, right, 0)))
    return total


def mixing(ukern, rkern, angles, taps, shifts, half_table):
    levels = half_table.shape[0]
    beams = taps.shape[1]
    utaps = ukern.shape[1]
    phases, rtaps = rkern.shape
    window = beams // 2 + utaps // 2
    depth = 2 * rtaps * 2 * window
    vmem = pl.BlockSpec(memory_space=pltpu.VMEM)

    whole = stacked(
        3 * levels,
        [
            (half_table, 0, 0),
            (shifts, levels, 0),
            (taps, 2 * levels, 0),
            (taps, 2 * levels, beams),
        ],
    )
    real = stacked(
        2 * levels + 2 + rtaps,
        [
            (angles.reshape(2 * levels, 2 * beams), 0, 0),
            (ukern.astype(jnp.float32), 2 * levels, 0),
            (rkern.T, 2 * levels + 2, 0),
        ],
    )
    return pl.pallas_call(
        functools.partial(prep_kernel, levels, beams, utaps, phases, rtaps),
        out_shape=[
            jax.ShapeDtypeStruct((levels, 4 * beams, depth), jnp.bfloat16),
            jax.ShapeDtypeStruct((levels, 8, LANES), jnp.float32),
        ],
        in_specs=[vmem, vmem],
        out_specs=[vmem, vmem],
        scratch_shapes=[
            pltpu.VMEM((beams // 2 + utaps, 2 * beams), jnp.float32),
            pltpu.VMEM((depth, 2 * beams), jnp.float32),
        ],
        compiler_params=pltpu.CompilerParams(vmem_limit_bytes=24 * 2**20),
        cost_estimate=pl.CostEstimate(
            flops=2 * 10**9, bytes_accessed=2 * levels * 4 * beams * depth, transcendentals=0
        ),
        name="mixing",
    )(whole, real)


def merge_kernel(level, plan, start, stop, length, beams, window, rtaps, last, *refs):
    code_ref, mix_ref = refs[:2]
    count = len(plan)
    own_refs, far_refs = refs[2:2 + count], refs[2 + count:2 + 2 * count]
    outs = refs[3 + 2 * count:]
    out_ref = outs[0]
    send_ref = None if last else outs[1]
    wide_ref, even_ref, odd_ref, held_ref = outs[1 if last else 2:]
    code = jnp.max(code_ref[level]).astype(jnp.int32)
    half, following = code // 131072, code // 65536 % 2
    shifts = (code // 256 % 256 - LANES, code % 256 - LANES)
    rows = pl.ds(pl.multiple_of(half * (beams - window), 16), window)
    base = start - LANES
    for number, (piece, source, target, width) in enumerate(plan):
        for child, ref in ((0, own_refs[number]), (1, far_refs[number])):
            taken = rows if ref.shape[1] == beams else pl.ds(0, window)
            for part in range(2):
                wide_ref[child, part, :, target - base:target - base + width] = ref[
                    part, taken, source:source + width
                ]
    edge = jnp.zeros((2, 2, window, LANES), jnp.bfloat16)
    if base < 0:
        wide_ref[:, :, :, 0:LANES] = edge
    if stop + LANES > length:
        wide_ref[:, :, :, stop - base:stop - base + LANES] = edge
    span = stop - start
    tiles = pl.cdiv(span, TILE)
    lane = lax.broadcasted_iota(jnp.int32, (2 * window, LANES), 1).astype(jnp.int16)
    moves = []
    for child in range(2):
        for tap in range(rtaps):
            shift = shifts[child] + (tap - 1 + LANES)
            part_tile = lax.rem(shift, LANES)
            kept = jnp.full((2 * window, LANES), LANES - part_tile, jnp.int32).astype(jnp.int16)
            turn = lax.rem(LANES - part_tile, LANES)
            moves.append((child, tap, shift // LANES * LANES, turn, lane < kept))

    def rolled(child, at, turn):
        piece = wide_ref[child, :, :, pl.ds(pl.multiple_of(at, LANES), LANES)]
        return pltpu.roll(piece.reshape(2 * window, LANES), turn, 1)

    def build(stack_ref, step):
        for number, (child, tap, whole, turn, kept) in enumerate(moves):
            place = (child * rtaps + tap) * 2 * window
            held = held_ref[number]
            for block in range(TILE // LANES):
                piece = rolled(child, step * TILE + whole + (block + 1) * LANES, turn)
                columns = pl.ds(block * LANES, LANES)
                stack_ref[place:place + 2 * window, columns] = jnp.where(kept, held, piece)
                held = piece
            held_ref[number] = held

    def multiply(stack_ref, step):
        column = pl.multiple_of(step * TILE, TILE)
        both = jnp.dot(mix_ref[level], stack_ref[...], preferred_element_type=jnp.float32)
        total = (both[:2 * beams] + both[2 * beams:]).astype(jnp.bfloat16)
        out_ref[:, :, pl.ds(column, TILE)] = total.reshape(2, beams, TILE)

    def two_tiles(pair, carry):
        build(odd_ref, 2 * pair + 1)
        multiply(even_ref, 2 * pair)
        build(even_ref, 2 * pair + 2)
        multiply(odd_ref, 2 * pair + 1)
        return carry

    for number, (child, tap, whole, turn, kept) in enumerate(moves):
        held_ref[number] = rolled(child, whole, turn)
    build(even_ref, 0)
    lax.fori_loop(0, (tiles - 1) // 2, two_tiles, 0)
    if tiles % 2 == 1:
        multiply(even_ref, tiles - 1)
    else:
        build(odd_ref, tiles - 1)
        multiply(even_ref, tiles - 2)
        multiply(odd_ref, tiles - 1)
    if not last:
        other = pl.ds(pl.multiple_of((1 - following) * (beams - window), 16), window)
        send_ref[...] = out_ref[:, other, :span]


def pieces_of(bounds, start, stop):
    found = []
    for chunk in range(len(bounds) - 1):
        low, high = max(bounds[chunk], start), min(bounds[chunk + 1], stop)
        if low < high:
            found.append((chunk, low - bounds[chunk], low, high - low))
    return found


def merge(level, levels, codes, mix, own, far, bounds, start, stop, sizes, before):
    beams, window, rtaps, length = sizes
    last = level == levels - 1
    plan = pieces_of(bounds, max(start - LANES, 0), min(stop + LANES, length))
    span = stop - start
    vmem = pl.BlockSpec(memory_space=pltpu.VMEM)
    anywhere = pl.BlockSpec(memory_space=pl.ANY)
    depth = mix.shape[2]
    padded = pl.cdiv(span, TILE) * TILE
    out_shape = [jax.ShapeDtypeStruct((2, beams, padded), jnp.bfloat16)]
    if not last:
        out_shape.append(jax.ShapeDtypeStruct((2, window, span), jnp.bfloat16))
    return pl.pallas_call(
        functools.partial(
            merge_kernel, level, plan, start, stop, length, beams, window, rtaps, last
        ),
        out_shape=out_shape,
        in_specs=[vmem, vmem] + [vmem] * (2 * len(plan)) + [anywhere],
        out_specs=[vmem] * len(out_shape),
        scratch_shapes=[
            pltpu.VMEM((2, 2, window, padded + TILE + 2 * LANES), jnp.bfloat16),
            pltpu.VMEM((depth, TILE), jnp.bfloat16),
            pltpu.VMEM((depth, TILE), jnp.bfloat16),
            pltpu.VMEM((2 * rtaps, 2 * window, LANES), jnp.bfloat16),
        ],
        compiler_params=pltpu.CompilerParams(vmem_limit_bytes=24 * 2**20),
        cost_estimate=pl.CostEstimate(
            flops=(8 if last else 32) * beams * depth * span,
            bytes_accessed=0,
            transcendentals=0,
        ),
        name=f"merge_{level}",
    )(
        codes,
        mix,
        *[own[piece[0]] for piece in plan],
        *[far[piece[0]] for piece in plan],
        before,
    )


MARKS = (
    (8, 16),
    (7, 15, 21, 27),
    (6, 14, 20, 26),
    (5, 13, 19, 25),
)
ORDER = (
    (0, 0), (0, 1), (0, 2), (1, 0), (1, 1), (2, 0), (1, 2), (2, 1), (1, 3), (3, 0), (1, 4),
    (2, 2), (3, 1), (2, 3), (2, 4), (3, 2), (3, 3), (3, 4),
)


def chunk_bounds(level, levels, length):
    marks = MARKS[len(MARKS) - 1 - min(levels - level, len(MARKS) - 1)]
    tiles = length // LANES
    return [0] + [tiles * mark // 32 * LANES for mark in marks] + [length]


def merge_order(levels, bounds):
    if levels == len(MARKS):
        return ORDER
    length = bounds[0][-1]
    made = [0] * levels
    order = []
    while len(order) < sum(len(bound) - 1 for bound in bounds[1:]):
        ready = []
        for level in range(levels):
            chunk = made[level]
            if chunk < len(bounds[level + 1]) - 1:
                stop = min(bounds[level + 1][chunk + 1] + LANES, length)
                needed = len(pieces_of(bounds[level], 0, stop))
                if level == 0 or needed <= made[level - 1]:
                    ready.append((level + chunk, level, chunk))
        _, level, chunk = min(ready)
        made[level] += 1
        order.append((level, chunk))
    return order


def from_partner(value, bit, turned=False):
    mask = 1 << bit
    pulses, scenes = lax.axis_size("pulse"), lax.axis_size("scene")
    order = range(scenes - 1, -1, -1) if turned else range(scenes)
    pairs = [
        (scene * pulses + source, scene * pulses + (source ^ mask))
        for scene in order
        for source in range(pulses)
    ]
    return lax.ppermute(value, ("scene", "pulse"), pairs)


def on_device(beams_in, ukern, rkern, angles, taps, shifts, half_table):
    beams, length = beams_in.shape[1:]
    utaps, rtaps = ukern.shape[1], rkern.shape[1]
    window = beams // 2 + utaps // 2
    levels = half_table.shape[0]
    sizes = (beams, window, rtaps, length)
    bounds = [[0, length]]
    bounds += [chunk_bounds(level, levels, length) for level in range(1, levels + 1)]
    mix, codes = mixing(ukern, rkern, angles, taps, shifts, half_table)
    owns = [[beams_in]] + [[None] * (len(bound) - 1) for bound in bounds[1:]]
    fars = [[from_partner(beams_in, 0)]] + [[None] * (len(bound) - 1) for bound in bounds[1:]]
    before = mix
    for level, chunk in merge_order(levels, bounds):
        start, stop = bounds[level + 1][chunk], bounds[level + 1][chunk + 1]
        done = merge(
            level, levels, codes, mix, owns[level], fars[level], bounds[level],
            start, stop, sizes, before,
        )
        before = owns[level + 1][chunk] = done[0]
        if level < levels - 1:
            turned = level == levels - 2 and chunk % 2 == 1
            fars[level + 1][chunk] = from_partner(done[1], level + 1, turned)
    edges = bounds[levels]
    made = [part[:, :, :high - low] for part, low, high in zip(owns[levels], edges, edges[1:])]
    return jnp.concatenate(made, axis=2)


def solution(mesh):
    in_specs = (
        P(None, ("scene", "pulse"), None),
        P(),
        P(),
        P(),
        P(None, ("scene", "pulse")),
        P(),
        P(),
    )
    out_specs = P(None, ("scene", "pulse"), None)
    return jax.shard_map(
        on_device, mesh=mesh, in_specs=in_specs, out_specs=out_specs, check_vma=False
    )
```

```python
import functools

import jax
import jax.numpy as jnp
from jax import lax
from jax.experimental import pallas as pl
from jax.experimental.pallas import tpu as pltpu
from jax.sharding import PartitionSpec as P

LANES = 128
TILE = 256
SCALE = 0.70710678


def prep_kernel(levels, beams, utaps, phases, rtaps, whole_ref, real_ref, mix_ref, plan_ref, band_ref, flat_ref):
    at_shifts, at_taps = levels, 2 * levels
    at_ukern, at_rkern = 2 * levels, 2 * levels + 2
    window = beams // 2 + utaps // 2
    myself = lax.axis_index("pulse")
    lane = lax.broadcasted_iota(jnp.int32, (1, 2 * beams), 1)
    first = lane < beams
    beam = jnp.where(first, lane, lane - beams)
    depth = beams // 2 + utaps
    row = lax.broadcasted_iota(jnp.int32, (depth, 2 * beams), 0)
    offset = row - beam // 2 - 1
    even = beam % 2 == 0
    halves = whole_ref[0:levels, :].astype(jnp.float32)
    shifts = whole_ref[at_shifts:at_shifts + levels, :].astype(jnp.float32)
    place = lax.broadcasted_iota(jnp.int32, (levels, LANES), 1)
    level_of = lax.broadcasted_iota(jnp.int32, (levels, LANES), 0)
    partner = jnp.bitwise_xor(myself, lax.shift_left(jnp.ones_like(level_of), level_of))

    def pick(table, index):
        return jnp.sum(jnp.where(place == index, table, 0.0), axis=1, keepdims=True)

    half_of = pick(halves, myself)
    after_of = jnp.concatenate([half_of[1:], half_of[:1]], axis=0)
    near_of = pick(shifts, myself) + LANES
    far_of = pick(shifts, partner) + LANES
    codes = ((half_of * 2 + after_of) * 256 + near_of) * 256 + far_of
    for level in range(levels):
        plan_ref[level] = jnp.broadcast_to(codes[level:level + 1, :], (8, LANES))
    kernel = real_ref[at_ukern:at_ukern + 2, :]
    band = jnp.zeros((depth, 2 * beams), jnp.float32)
    for k in range(utaps):
        value = jnp.where(even, kernel[0:1, k:k + 1], kernel[1:2, k:k + 1])
        band = jnp.where(offset == k, value, band)
    band_ref[...] = band
    table = real_ref[at_rkern:at_rkern + rtaps, :]
    for level in range(levels):
        low_half = half_of[level:level + 1, :] == 0.0
        bit = lax.rem(lax.shift_right_logical(myself, level), 2)
        near = jnp.where(
            low_half, band_ref[utaps // 2:utaps // 2 + window, :], band_ref[0:window, :]
        )
        chosen = whole_ref[at_taps + level:at_taps + level + 1, :]
        weights = []
        for tap in range(rtaps):
            weight = jnp.zeros((1, 2 * beams), jnp.float32)
            for phase in range(phases):
                weight = jnp.where(
                    chosen == phase, table[tap:tap + 1, phase:phase + 1], weight
                )
            weights.append(weight)
        for child in range(2):
            side = bit if child == 0 else 1 - bit
            angle = real_ref[pl.ds(2 * level + side, 1), :]
            turned = pltpu.roll(angle, beams, 1)
            angle = jnp.where(first == low_half, angle, turned)
            cosine = SCALE * jnp.cos(angle)
            sine = SCALE * jnp.sin(angle)
            factors = (jnp.where(first, cosine, sine), jnp.where(first, -sine, cosine))
            for tap in range(rtaps):
                for part in range(2):
                    place = ((child * rtaps + tap) * 2 + part) * window
                    flat_ref[place:place + window, :] = near * (factors[part] * weights[tap])
        for block in range(flat_ref.shape[0] // LANES):
            mixed = flat_ref[block * LANES:(block + 1) * LANES, :].T
            high = mixed.astype(jnp.bfloat16)
            low = (mixed - high.astype(jnp.float32)).astype(jnp.bfloat16)
            columns = pl.ds(block * LANES, LANES)
            mix_ref[level, 0:2 * beams, columns] = high
            mix_ref[level, 2 * beams:4 * beams, columns] = low


def stacked(height, pieces):
    total = jnp.zeros((height, LANES), pieces[0][0].dtype)
    for piece, top, left in pieces:
        below, right = height - top - piece.shape[0], LANES - left - piece.shape[1]
        zero = jnp.zeros((), piece.dtype)
        total = total + lax.pad(piece, zero, ((top, below, 0), (left, right, 0)))
    return total


def mixing(ukern, rkern, angles, taps, shifts, half_table):
    levels = half_table.shape[0]
    beams = taps.shape[1]
    utaps = ukern.shape[1]
    phases, rtaps = rkern.shape
    window = beams // 2 + utaps // 2
    depth = 2 * rtaps * 2 * window
    vmem = pl.BlockSpec(memory_space=pltpu.VMEM)

    whole = stacked(
        3 * levels,
        [
            (half_table, 0, 0),
            (shifts, levels, 0),
            (taps, 2 * levels, 0),
            (taps, 2 * levels, beams),
        ],
    )
    real = stacked(
        2 * levels + 2 + rtaps,
        [
            (angles.reshape(2 * levels, 2 * beams), 0, 0),
            (ukern.astype(jnp.float32), 2 * levels, 0),
            (rkern.T, 2 * levels + 2, 0),
        ],
    )
    return pl.pallas_call(
        functools.partial(prep_kernel, levels, beams, utaps, phases, rtaps),
        out_shape=[
            jax.ShapeDtypeStruct((levels, 4 * beams, depth), jnp.bfloat16),
            jax.ShapeDtypeStruct((levels, 8, LANES), jnp.float32),
        ],
        in_specs=[vmem, vmem],
        out_specs=[vmem, vmem],
        scratch_shapes=[
            pltpu.VMEM((beams // 2 + utaps, 2 * beams), jnp.float32),
            pltpu.VMEM((depth, 2 * beams), jnp.float32),
        ],
        compiler_params=pltpu.CompilerParams(vmem_limit_bytes=24 * 2**20),
        cost_estimate=pl.CostEstimate(
            flops=2 * 10**9, bytes_accessed=2 * levels * 4 * beams * depth, transcendentals=0
        ),
        name="mixing",
    )(whole, real)


def merge_kernel(level, plan, start, stop, length, beams, window, rtaps, last, *refs):
    code_ref, mix_ref = refs[:2]
    count = len(plan)
    own_refs, far_refs = refs[2:2 + count], refs[2 + count:2 + 2 * count]
    outs = refs[3 + 2 * count:]
    out_ref = outs[0]
    send_ref = None if last else outs[1]
    wide_ref, even_ref, odd_ref, held_ref = outs[1 if last else 2:]
    code = code_ref[level][0, 0].astype(jnp.int32)
    half, following = code // 131072, code // 65536 % 2
    shifts = (code // 256 % 256 - LANES, code % 256 - LANES)
    rows = pl.ds(pl.multiple_of(half * (beams - window), 16), window)
    base = start - LANES
    for number, (piece, source, target, width) in enumerate(plan):
        for child, ref in ((0, own_refs[number]), (1, far_refs[number])):
            taken = rows if ref.shape[1] == beams else pl.ds(0, window)
            for part in range(2):
                wide_ref[child, part, :, target - base:target - base + width] = ref[
                    part, taken, source:source + width
                ]
    edge = jnp.zeros((2, 2, window, LANES), jnp.bfloat16)
    if base < 0:
        wide_ref[:, :, :, 0:LANES] = edge
    if stop + LANES > length:
        wide_ref[:, :, :, stop - base:stop - base + LANES] = edge
    span = stop - start
    tiles = pl.cdiv(span, TILE)
    other = pl.ds(pl.multiple_of((1 - following) * (beams - window), 16), window)
    inline = not last and span % TILE == 0
    lane = lax.broadcasted_iota(jnp.int32, (2 * window, LANES), 1).astype(jnp.int16)
    moves = []
    for child in range(2):
        for tap in range(rtaps):
            shift = shifts[child] + (tap - 1 + LANES)
            part_tile = lax.rem(shift, LANES)
            kept = jnp.full((2 * window, LANES), LANES - part_tile, jnp.int32).astype(jnp.int16)
            turn = lax.rem(LANES - part_tile, LANES)
            moves.append((child, tap, shift // LANES * LANES, turn, lane < kept))

    def rolled(child, at, turn):
        piece = wide_ref[child, :, :, pl.ds(pl.multiple_of(at, LANES), LANES)]
        return pltpu.roll(piece.reshape(2 * window, LANES), turn, 1)

    def build(stack_ref, step):
        for number, (child, tap, whole, turn, kept) in enumerate(moves):
            place = (child * rtaps + tap) * 2 * window
            held = held_ref[number]
            for block in range(TILE // LANES):
                piece = rolled(child, step * TILE + whole + (block + 1) * LANES, turn)
                columns = pl.ds(block * LANES, LANES)
                stack_ref[place:place + 2 * window, columns] = jnp.where(kept, held, piece)
                held = piece
            held_ref[number] = held

    def multiply(stack_ref, step):
        column = pl.multiple_of(step * TILE, TILE)
        both = jnp.dot(mix_ref[level], stack_ref[...], preferred_element_type=jnp.float32)
        total = (both[:2 * beams] + both[2 * beams:]).astype(jnp.bfloat16)
        out_ref[:, :, pl.ds(column, TILE)] = total.reshape(2, beams, TILE)
        if inline:
            send_ref[:, :, pl.ds(column, TILE)] = out_ref[:, other, pl.ds(column, TILE)]

    def two_tiles(pair, carry):
        build(odd_ref, 2 * pair + 1)
        multiply(even_ref, 2 * pair)
        build(even_ref, 2 * pair + 2)
        multiply(odd_ref, 2 * pair + 1)
        return carry

    for number, (child, tap, whole, turn, kept) in enumerate(moves):
        held_ref[number] = rolled(child, whole, turn)
    build(even_ref, 0)
    lax.fori_loop(0, (tiles - 1) // 2, two_tiles, 0)
    if tiles % 2 == 1:
        multiply(even_ref, tiles - 1)
    else:
        build(odd_ref, tiles - 1)
        multiply(even_ref, tiles - 2)
        multiply(odd_ref, tiles - 1)
    if not last and not inline:
        send_ref[...] = out_ref[:, other, :span]


def pieces_of(bounds, start, stop):
    found = []
    for chunk in range(len(bounds) - 1):
        low, high = max(bounds[chunk], start), min(bounds[chunk + 1], stop)
        if low < high:
            found.append((chunk, low - bounds[chunk], low, high - low))
    return found


def merge(level, levels, codes, mix, own, far, bounds, start, stop, sizes, before):
    beams, window, rtaps, length = sizes
    last = level == levels - 1
    plan = pieces_of(bounds, max(start - LANES, 0), min(stop + LANES, length))
    span = stop - start
    vmem = pl.BlockSpec(memory_space=pltpu.VMEM)
    anywhere = pl.BlockSpec(memory_space=pl.ANY)
    depth = mix.shape[2]
    padded = pl.cdiv(span, TILE) * TILE
    out_shape = [jax.ShapeDtypeStruct((2, beams, padded), jnp.bfloat16)]
    if not last:
        out_shape.append(jax.ShapeDtypeStruct((2, window, span), jnp.bfloat16))
    return pl.pallas_call(
        functools.partial(
            merge_kernel, level, plan, start, stop, length, beams, window, rtaps, last
        ),
        out_shape=out_shape,
        in_specs=[vmem, vmem] + [vmem] * (2 * len(plan)) + [anywhere],
        out_specs=[vmem] * len(out_shape),
        scratch_shapes=[
            pltpu.VMEM((2, 2, window, padded + TILE + 2 * LANES), jnp.bfloat16),
            pltpu.VMEM((depth, TILE), jnp.bfloat16),
            pltpu.VMEM((depth, TILE), jnp.bfloat16),
            pltpu.VMEM((2 * rtaps, 2 * window, LANES), jnp.bfloat16),
        ],
        compiler_params=pltpu.CompilerParams(vmem_limit_bytes=24 * 2**20),
        cost_estimate=pl.CostEstimate(
            flops=(8 if last else 32) * beams * depth * span,
            bytes_accessed=0,
            transcendentals=0,
        ),
        name=f"merge_{level}",
    )(
        codes,
        mix,
        *[own[piece[0]] for piece in plan],
        *[far[piece[0]] for piece in plan],
        before,
    )


MARKS = (
    (8, 16),
    (7, 15, 21, 27),
    (6, 14, 20, 26),
    (5, 13, 19, 25),
)
ORDER = (
    (0, 0), (0, 1), (0, 2), (1, 0), (1, 1), (2, 0), (1, 2), (2, 1), (1, 3), (3, 0), (1, 4),
    (2, 2), (3, 1), (2, 3), (2, 4), (3, 2), (3, 3), (3, 4),
)


def chunk_bounds(level, levels, length):
    marks = MARKS[len(MARKS) - 1 - min(levels - level, len(MARKS) - 1)]
    tiles = length // LANES
    return [0] + [tiles * mark // 32 * LANES for mark in marks] + [length]


def merge_order(levels, bounds):
    if levels == len(MARKS):
        return ORDER
    length = bounds[0][-1]
    made = [0] * levels
    order = []
    while len(order) < sum(len(bound) - 1 for bound in bounds[1:]):
        ready = []
        for level in range(levels):
            chunk = made[level]
            if chunk < len(bounds[level + 1]) - 1:
                stop = min(bounds[level + 1][chunk + 1] + LANES, length)
                needed = len(pieces_of(bounds[level], 0, stop))
                if level == 0 or needed <= made[level - 1]:
                    ready.append((level + chunk, level, chunk))
        _, level, chunk = min(ready)
        made[level] += 1
        order.append((level, chunk))
    return order


def from_partner(value, bit):
    mask = 1 << bit
    pairs = [(source, source ^ mask) for source in range(lax.axis_size("pulse"))]
    return lax.ppermute(value, "pulse", pairs)


def on_device(beams_in, ukern, rkern, angles, taps, shifts, half_table):
    beams, length = beams_in.shape[1:]
    utaps, rtaps = ukern.shape[1], rkern.shape[1]
    window = beams // 2 + utaps // 2
    levels = half_table.shape[0]
    sizes = (beams, window, rtaps, length)
    bounds = [[0, length]]
    bounds += [chunk_bounds(level, levels, length) for level in range(1, levels + 1)]
    mix, codes = mixing(ukern, rkern, angles, taps, shifts, half_table)
    owns = [[beams_in]] + [[None] * (len(bound) - 1) for bound in bounds[1:]]
    fars = [[from_partner(beams_in, 0)]] + [[None] * (len(bound) - 1) for bound in bounds[1:]]
    before = mix
    for level, chunk in merge_order(levels, bounds):
        start, stop = bounds[level + 1][chunk], bounds[level + 1][chunk + 1]
        done = merge(
            level, levels, codes, mix, owns[level], fars[level], bounds[level],
            start, stop, sizes, before,
        )
        before = owns[level + 1][chunk] = done[0]
        if level < levels - 1:
            fars[level + 1][chunk] = from_partner(done[1], level + 1)
    edges = bounds[levels]
    made = [part[:, :, :high - low] for part, low, high in zip(owns[levels], edges, edges[1:])]
    return jnp.concatenate(made, axis=2)


def solution(mesh):
    in_specs = (
        P(None, ("scene", "pulse"), None),
        P(),
        P(),
        P(),
        P(None, ("scene", "pulse")),
        P(),
        P(),
    )
    out_specs = P(None, ("scene", "pulse"), None)
    return jax.shard_map(
        on_device, mesh=mesh, in_specs=in_specs, out_specs=out_specs, check_vma=False
    )
```

```python
import functools

import jax
import jax.numpy as jnp
from jax import lax
from jax.experimental import pallas as pl
from jax.experimental.pallas import tpu as pltpu
from jax.sharding import PartitionSpec as P

LANES = 128
TILE = 256
SCALE = 0.70710678


def prep_kernel(levels, beams, utaps, phases, rtaps, whole_ref, real_ref, mix_ref, plan_ref, band_ref, flat_ref):
    at_shifts, at_taps = levels, 2 * levels
    at_ukern, at_rkern = 2 * levels, 2 * levels + 2
    window = beams // 2 + utaps // 2
    myself = lax.axis_index("pulse")
    lane = lax.broadcasted_iota(jnp.int32, (1, 2 * beams), 1)
    first = lane < beams
    beam = jnp.where(first, lane, lane - beams)
    depth = beams // 2 + utaps
    row = lax.broadcasted_iota(jnp.int32, (depth, 2 * beams), 0)
    offset = row - beam // 2 - 1
    even = beam % 2 == 0
    halves = whole_ref[0:levels, :].astype(jnp.float32)
    shifts = whole_ref[at_shifts:at_shifts + levels, :].astype(jnp.float32)
    place = lax.broadcasted_iota(jnp.int32, (levels, LANES), 1)
    level_of = lax.broadcasted_iota(jnp.int32, (levels, LANES), 0)
    partner = jnp.bitwise_xor(myself, lax.shift_left(jnp.ones_like(level_of), level_of))

    def pick(table, index):
        return jnp.sum(jnp.where(place == index, table, 0.0), axis=1, keepdims=True)

    half_of = pick(halves, myself)
    after_of = jnp.concatenate([half_of[1:], half_of[:1]], axis=0)
    near_of = pick(shifts, myself) + LANES
    far_of = pick(shifts, partner) + LANES
    codes = ((half_of * 2 + after_of) * 256 + near_of) * 256 + far_of
    for level in range(levels):
        plan_ref[level] = jnp.broadcast_to(codes[level:level + 1, :], (8, LANES))
    kernel = real_ref[at_ukern:at_ukern + 2, :]
    band = jnp.zeros((depth, 2 * beams), jnp.float32)
    for k in range(utaps):
        value = jnp.where(even, kernel[0:1, k:k + 1], kernel[1:2, k:k + 1])
        band = jnp.where(offset == k, value, band)
    band_ref[...] = band
    table = real_ref[at_rkern:at_rkern + rtaps, :]
    for level in range(levels):
        low_half = half_of[level:level + 1, :] == 0.0
        bit = lax.rem(lax.shift_right_logical(myself, level), 2)
        near = jnp.where(
            low_half, band_ref[utaps // 2:utaps // 2 + window, :], band_ref[0:window, :]
        )
        chosen = whole_ref[at_taps + level:at_taps + level + 1, :]
        weights = []
        for tap in range(rtaps):
            weight = jnp.zeros((1, 2 * beams), jnp.float32)
            for phase in range(phases):
                weight = jnp.where(
                    chosen == phase, table[tap:tap + 1, phase:phase + 1], weight
                )
            weights.append(weight)
        for child in range(2):
            side = bit if child == 0 else 1 - bit
            angle = real_ref[pl.ds(2 * level + side, 1), :]
            turned = pltpu.roll(angle, beams, 1)
            angle = jnp.where(first == low_half, angle, turned)
            cosine = SCALE * jnp.cos(angle)
            sine = SCALE * jnp.sin(angle)
            factors = (jnp.where(first, cosine, sine), jnp.where(first, -sine, cosine))
            for tap in range(rtaps):
                for part in range(2):
                    place = ((child * rtaps + tap) * 2 + part) * window
                    flat_ref[place:place + window, :] = near * (factors[part] * weights[tap])
        for block in range(flat_ref.shape[0] // LANES):
            mixed = flat_ref[block * LANES:(block + 1) * LANES, :].T
            high = mixed.astype(jnp.bfloat16)
            low = (mixed - high.astype(jnp.float32)).astype(jnp.bfloat16)
            columns = pl.ds(block * LANES, LANES)
            mix_ref[level, 0:2 * beams, columns] = high
            mix_ref[level, 2 * beams:4 * beams, columns] = low


def stacked(height, pieces):
    total = jnp.zeros((height, LANES), pieces[0][0].dtype)
    for piece, top, left in pieces:
        below, right = height - top - piece.shape[0], LANES - left - piece.shape[1]
        zero = jnp.zeros((), piece.dtype)
        total = total + lax.pad(piece, zero, ((top, below, 0), (left, right, 0)))
    return total


def mixing(ukern, rkern, angles, taps, shifts, half_table):
    levels = half_table.shape[0]
    beams = taps.shape[1]
    utaps = ukern.shape[1]
    phases, rtaps = rkern.shape
    window = beams // 2 + utaps // 2
    depth = 2 * rtaps * 2 * window
    vmem = pl.BlockSpec(memory_space=pltpu.VMEM)

    whole = stacked(
        3 * levels,
        [
            (half_table, 0, 0),
            (shifts, levels, 0),
            (taps, 2 * levels, 0),
            (taps, 2 * levels, beams),
        ],
    )
    real = stacked(
        2 * levels + 2 + rtaps,
        [
            (angles.reshape(2 * levels, 2 * beams), 0, 0),
            (ukern.astype(jnp.float32), 2 * levels, 0),
            (rkern.T, 2 * levels + 2, 0),
        ],
    )
    return pl.pallas_call(
        functools.partial(prep_kernel, levels, beams, utaps, phases, rtaps),
        out_shape=[
            jax.ShapeDtypeStruct((levels, 4 * beams, depth), jnp.bfloat16),
            jax.ShapeDtypeStruct((levels, 8, LANES), jnp.float32),
        ],
        in_specs=[vmem, vmem],
        out_specs=[vmem, vmem],
        scratch_shapes=[
            pltpu.VMEM((beams // 2 + utaps, 2 * beams), jnp.float32),
            pltpu.VMEM((depth, 2 * beams), jnp.float32),
        ],
        compiler_params=pltpu.CompilerParams(vmem_limit_bytes=24 * 2**20),
        cost_estimate=pl.CostEstimate(
            flops=2 * 10**9, bytes_accessed=2 * levels * 4 * beams * depth, transcendentals=0
        ),
        name="mixing",
    )(whole, real)


def merge_kernel(level, plan, start, stop, length, beams, window, rtaps, last, *refs):
    code_ref, mix_ref = refs[:2]
    count = len(plan)
    own_refs, far_refs = refs[2:2 + count], refs[2 + count:2 + 2 * count]
    outs = refs[3 + 2 * count:]
    out_ref = outs[0]
    send_ref = None if last else outs[1]
    wide_ref, even_ref, odd_ref, held_ref = outs[1 if last else 2:]
    code = code_ref[level][0, 0].astype(jnp.int32)
    half, following = code // 131072, code // 65536 % 2
    shifts = (code // 256 % 256 - LANES, code % 256 - LANES)
    rows = pl.ds(pl.multiple_of(half * (beams - window), 16), window)
    base = start - LANES
    for number, (piece, source, target, width) in enumerate(plan):
        for child, ref in ((0, own_refs[number]), (1, far_refs[number])):
            taken = rows if ref.shape[1] == beams else pl.ds(0, window)
            for part in range(2):
                wide_ref[child, part, :, target - base:target - base + width] = ref[
                    part, taken, source:source + width
                ]
    edge = jnp.zeros((2, 2, window, LANES), jnp.bfloat16)
    if base < 0:
        wide_ref[:, :, :, 0:LANES] = edge
    if stop + LANES > length:
        wide_ref[:, :, :, stop - base:stop - base + LANES] = edge
    span = stop - start
    tiles = pl.cdiv(span, TILE)
    other = pl.ds(pl.multiple_of((1 - following) * (beams - window), 16), window)
    inline = not last and span % TILE == 0
    lane = lax.broadcasted_iota(jnp.int32, (2 * window, LANES), 1).astype(jnp.int16)
    moves = []
    for child in range(2):
        for tap in range(rtaps):
            shift = shifts[child] + (tap - 1 + LANES)
            part_tile = lax.rem(shift, LANES)
            kept = jnp.full((2 * window, LANES), LANES - part_tile, jnp.int32).astype(jnp.int16)
            turn = lax.rem(LANES - part_tile, LANES)
            moves.append((child, tap, shift // LANES * LANES, turn, lane < kept))

    def rolled(child, at, turn):
        piece = wide_ref[child, :, :, pl.ds(pl.multiple_of(at, LANES), LANES)]
        return pltpu.roll(piece.reshape(2 * window, LANES), turn, 1)

    def build(stack_ref, step):
        for number, (child, tap, whole, turn, kept) in enumerate(moves):
            place = (child * rtaps + tap) * 2 * window
            held = held_ref[number]
            for block in range(TILE // LANES):
                piece = rolled(child, step * TILE + whole + (block + 1) * LANES, turn)
                columns = pl.ds(block * LANES, LANES)
                stack_ref[place:place + 2 * window, columns] = jnp.where(kept, held, piece)
                held = piece
            held_ref[number] = held

    def multiply(stack_ref, step):
        column = pl.multiple_of(step * TILE, TILE)
        both = jnp.dot(mix_ref[level], stack_ref[...], preferred_element_type=jnp.float32)
        total = (both[:2 * beams] + both[2 * beams:]).astype(jnp.bfloat16)
        out_ref[:, :, pl.ds(column, TILE)] = total.reshape(2, beams, TILE)
        if inline:
            send_ref[:, :, pl.ds(column, TILE)] = out_ref[:, other, pl.ds(column, TILE)]

    def two_tiles(pair, carry):
        build(odd_ref, 2 * pair + 1)
        multiply(even_ref, 2 * pair)
        build(even_ref, 2 * pair + 2)
        multiply(odd_ref, 2 * pair + 1)
        return carry

    for number, (child, tap, whole, turn, kept) in enumerate(moves):
        held_ref[number] = rolled(child, whole, turn)
    build(even_ref, 0)
    lax.fori_loop(0, (tiles - 1) // 2, two_tiles, 0)
    if tiles % 2 == 1:
        multiply(even_ref, tiles - 1)
    else:
        build(odd_ref, tiles - 1)
        multiply(even_ref, tiles - 2)
        multiply(odd_ref, tiles - 1)
    if not last and not inline:
        send_ref[...] = out_ref[:, other, :span]


def pieces_of(bounds, start, stop):
    found = []
    for chunk in range(len(bounds) - 1):
        low, high = max(bounds[chunk], start), min(bounds[chunk + 1], stop)
        if low < high:
            found.append((chunk, low - bounds[chunk], low, high - low))
    return found


def merge(level, levels, codes, mix, own, far, bounds, start, stop, sizes, before):
    beams, window, rtaps, length = sizes
    last = level == levels - 1
    plan = pieces_of(bounds, max(start - LANES, 0), min(stop + LANES, length))
    span = stop - start
    vmem = pl.BlockSpec(memory_space=pltpu.VMEM)
    anywhere = pl.BlockSpec(memory_space=pl.ANY)
    depth = mix.shape[2]
    padded = pl.cdiv(span, TILE) * TILE
    out_shape = [jax.ShapeDtypeStruct((2, beams, padded), jnp.bfloat16)]
    if not last:
        out_shape.append(jax.ShapeDtypeStruct((2, window, span), jnp.bfloat16))
    return pl.pallas_call(
        functools.partial(
            merge_kernel, level, plan, start, stop, length, beams, window, rtaps, last
        ),
        out_shape=out_shape,
        in_specs=[vmem, vmem] + [vmem] * (2 * len(plan)) + [anywhere],
        out_specs=[vmem] * len(out_shape),
        scratch_shapes=[
            pltpu.VMEM((2, 2, window, padded + TILE + 2 * LANES), jnp.bfloat16),
            pltpu.VMEM((depth, TILE), jnp.bfloat16),
            pltpu.VMEM((depth, TILE), jnp.bfloat16),
            pltpu.VMEM((2 * rtaps, 2 * window, LANES), jnp.bfloat16),
        ],
        compiler_params=pltpu.CompilerParams(vmem_limit_bytes=24 * 2**20),
        cost_estimate=pl.CostEstimate(
            flops=(8 if last else 32) * beams * depth * span,
            bytes_accessed=0,
            transcendentals=0,
        ),
        name=f"merge_{level}",
    )(
        codes,
        mix,
        *[own[piece[0]] for piece in plan],
        *[far[piece[0]] for piece in plan],
        before,
    )


MARKS = (
    (8, 16),
    (7, 15, 21, 28),
    (6, 14, 20, 27),
    (5, 13, 19, 26),
)
ORDER = (
    (0, 0), (0, 1), (0, 2), (1, 0), (1, 1), (2, 0), (1, 2), (2, 1), (1, 3), (3, 0), (1, 4),
    (2, 2), (3, 1), (2, 3), (2, 4), (3, 2), (3, 3), (3, 4),
)


def chunk_bounds(level, levels, length):
    marks = MARKS[len(MARKS) - 1 - min(levels - level, len(MARKS) - 1)]
    tiles = length // LANES
    return [0] + [tiles * mark // 32 * LANES for mark in marks] + [length]


def merge_order(levels, bounds):
    if levels == len(MARKS):
        return ORDER
    length = bounds[0][-1]
    made = [0] * levels
    order = []
    while len(order) < sum(len(bound) - 1 for bound in bounds[1:]):
        ready = []
        for level in range(levels):
            chunk = made[level]
            if chunk < len(bounds[level + 1]) - 1:
                stop = min(bounds[level + 1][chunk + 1] + LANES, length)
                needed = len(pieces_of(bounds[level], 0, stop))
                if level == 0 or needed <= made[level - 1]:
                    ready.append((level + chunk, level, chunk))
        _, level, chunk = min(ready)
        made[level] += 1
        order.append((level, chunk))
    return order


def from_partner(value, bit):
    mask = 1 << bit
    pairs = [(source, source ^ mask) for source in range(lax.axis_size("pulse"))]
    return lax.ppermute(value, "pulse", pairs)


def on_device(beams_in, ukern, rkern, angles, taps, shifts, half_table):
    beams, length = beams_in.shape[1:]
    utaps, rtaps = ukern.shape[1], rkern.shape[1]
    window = beams // 2 + utaps // 2
    levels = half_table.shape[0]
    sizes = (beams, window, rtaps, length)
    bounds = [[0, length]]
    bounds += [chunk_bounds(level, levels, length) for level in range(1, levels + 1)]
    mix, codes = mixing(ukern, rkern, angles, taps, shifts, half_table)
    owns = [[beams_in]] + [[None] * (len(bound) - 1) for bound in bounds[1:]]
    fars = [[from_partner(beams_in, 0)]] + [[None] * (len(bound) - 1) for bound in bounds[1:]]
    before = mix
    for level, chunk in merge_order(levels, bounds):
        start, stop = bounds[level + 1][chunk], bounds[level + 1][chunk + 1]
        done = merge(
            level, levels, codes, mix, owns[level], fars[level], bounds[level],
            start, stop, sizes, before,
        )
        before = owns[level + 1][chunk] = done[0]
        if level < levels - 1:
            fars[level + 1][chunk] = from_partner(done[1], level + 1)
    edges = bounds[levels]
    made = [part[:, :, :high - low] for part, low, high in zip(owns[levels], edges, edges[1:])]
    return jnp.concatenate(made, axis=2)


def solution(mesh):
    in_specs = (
        P(None, ("scene", "pulse"), None),
        P(),
        P(),
        P(),
        P(None, ("scene", "pulse")),
        P(),
        P(),
    )
    out_specs = P(None, ("scene", "pulse"), None)
    return jax.shard_map(
        on_device, mesh=mesh, in_specs=in_specs, out_specs=out_specs, check_vma=False
    )
```

```python
import functools

import jax
import jax.numpy as jnp
from jax import lax
from jax.experimental import pallas as pl
from jax.experimental.pallas import tpu as pltpu
from jax.sharding import PartitionSpec as P

LANES = 128
TILE = 256
SCALE = 0.70710678


def prep_kernel(levels, beams, utaps, phases, rtaps, whole_ref, real_ref, mix_ref, plan_ref, band_ref, flat_ref):
    at_shifts, at_taps = levels, 2 * levels
    at_ukern, at_rkern = 2 * levels, 2 * levels + 2
    window = beams // 2 + utaps // 2
    myself = lax.axis_index("pulse")
    lane = lax.broadcasted_iota(jnp.int32, (1, 2 * beams), 1)
    first = lane < beams
    beam = jnp.where(first, lane, lane - beams)
    depth = beams // 2 + utaps
    row = lax.broadcasted_iota(jnp.int32, (depth, 2 * beams), 0)
    offset = row - beam // 2 - 1
    even = beam % 2 == 0
    halves = whole_ref[0:levels, :].astype(jnp.float32)
    shifts = whole_ref[at_shifts:at_shifts + levels, :].astype(jnp.float32)
    place = lax.broadcasted_iota(jnp.int32, (levels, LANES), 1)
    level_of = lax.broadcasted_iota(jnp.int32, (levels, LANES), 0)
    partner = jnp.bitwise_xor(myself, lax.shift_left(jnp.ones_like(level_of), level_of))

    def pick(table, index):
        return jnp.sum(jnp.where(place == index, table, 0.0), axis=1, keepdims=True)

    half_of = pick(halves, myself)
    after_of = jnp.concatenate([half_of[1:], half_of[:1]], axis=0)
    near_of = pick(shifts, myself) + LANES
    far_of = pick(shifts, partner) + LANES
    codes = ((half_of * 2 + after_of) * 256 + near_of) * 256 + far_of
    for level in range(levels):
        plan_ref[level] = jnp.broadcast_to(codes[level:level + 1, :], (8, LANES))
    kernel = real_ref[at_ukern:at_ukern + 2, :]
    band = jnp.zeros((depth, 2 * beams), jnp.float32)
    for k in range(utaps):
        value = jnp.where(even, kernel[0:1, k:k + 1], kernel[1:2, k:k + 1])
        band = jnp.where(offset == k, value, band)
    band_ref[...] = band
    table = real_ref[at_rkern:at_rkern + rtaps, :]
    for level in range(levels):
        low_half = half_of[level:level + 1, :] == 0.0
        bit = lax.rem(lax.shift_right_logical(myself, level), 2)
        near = jnp.where(
            low_half, band_ref[utaps // 2:utaps // 2 + window, :], band_ref[0:window, :]
        )
        chosen = whole_ref[at_taps + level:at_taps + level + 1, :]
        weights = []
        for tap in range(rtaps):
            weight = jnp.zeros((1, 2 * beams), jnp.float32)
            for phase in range(phases):
                weight = jnp.where(
                    chosen == phase, table[tap:tap + 1, phase:phase + 1], weight
                )
            weights.append(weight)
        for child in range(2):
            side = bit if child == 0 else 1 - bit
            angle = real_ref[pl.ds(2 * level + side, 1), :]
            turned = pltpu.roll(angle, beams, 1)
            angle = jnp.where(first == low_half, angle, turned)
            cosine = SCALE * jnp.cos(angle)
            sine = SCALE * jnp.sin(angle)
            factors = (jnp.where(first, cosine, sine), jnp.where(first, -sine, cosine))
            for tap in range(rtaps):
                for part in range(2):
                    place = ((child * rtaps + tap) * 2 + part) * window
                    flat_ref[place:place + window, :] = near * (factors[part] * weights[tap])
        for block in range(flat_ref.shape[0] // LANES):
            mixed = flat_ref[block * LANES:(block + 1) * LANES, :].T
            high = mixed.astype(jnp.bfloat16)
            low = (mixed - high.astype(jnp.float32)).astype(jnp.bfloat16)
            columns = pl.ds(block * LANES, LANES)
            mix_ref[level, 0:2 * beams, columns] = high
            mix_ref[level, 2 * beams:4 * beams, columns] = low


def stacked(height, pieces):
    total = jnp.zeros((height, LANES), pieces[0][0].dtype)
    for piece, top, left in pieces:
        below, right = height - top - piece.shape[0], LANES - left - piece.shape[1]
        zero = jnp.zeros((), piece.dtype)
        total = total + lax.pad(piece, zero, ((top, below, 0), (left, right, 0)))
    return total


def mixing(ukern, rkern, angles, taps, shifts, half_table):
    levels = half_table.shape[0]
    beams = taps.shape[1]
    utaps = ukern.shape[1]
    phases, rtaps = rkern.shape
    window = beams // 2 + utaps // 2
    depth = 2 * rtaps * 2 * window
    vmem = pl.BlockSpec(memory_space=pltpu.VMEM)

    whole = stacked(
        3 * levels,
        [
            (half_table, 0, 0),
            (shifts, levels, 0),
            (taps, 2 * levels, 0),
            (taps, 2 * levels, beams),
        ],
    )
    real = stacked(
        2 * levels + 2 + rtaps,
        [
            (angles.reshape(2 * levels, 2 * beams), 0, 0),
            (ukern.astype(jnp.float32), 2 * levels, 0),
            (rkern.T, 2 * levels + 2, 0),
        ],
    )
    return pl.pallas_call(
        functools.partial(prep_kernel, levels, beams, utaps, phases, rtaps),
        out_shape=[
            jax.ShapeDtypeStruct((levels, 4 * beams, depth), jnp.bfloat16),
            jax.ShapeDtypeStruct((levels, 8, LANES), jnp.float32),
        ],
        in_specs=[vmem, vmem],
        out_specs=[vmem, vmem],
        scratch_shapes=[
            pltpu.VMEM((beams // 2 + utaps, 2 * beams), jnp.float32),
            pltpu.VMEM((depth, 2 * beams), jnp.float32),
        ],
        compiler_params=pltpu.CompilerParams(vmem_limit_bytes=24 * 2**20),
        cost_estimate=pl.CostEstimate(
            flops=2 * 10**9, bytes_accessed=2 * levels * 4 * beams * depth, transcendentals=0
        ),
        name="mixing",
    )(whole, real)


def merge_kernel(level, plan, start, stop, length, beams, window, rtaps, last, *refs):
    code_ref, mix_ref = refs[:2]
    count = len(plan)
    own_refs, far_refs = refs[2:2 + count], refs[2 + count:2 + 2 * count]
    outs = refs[3 + 2 * count:]
    out_ref = outs[0]
    send_ref = None if last else outs[1]
    wide_ref, even_ref, odd_ref, held_ref = outs[1 if last else 2:]
    code = code_ref[level][0, 0].astype(jnp.int32)
    half, following = code // 131072, code // 65536 % 2
    shifts = (code // 256 % 256 - LANES, code % 256 - LANES)
    rows = pl.ds(pl.multiple_of(half * (beams - window), 16), window)
    base = start - LANES
    for number, (piece, source, target, width) in enumerate(plan):
        for child, ref in ((0, own_refs[number]), (1, far_refs[number])):
            taken = rows if ref.shape[1] == beams else pl.ds(0, window)
            for part in range(2):
                wide_ref[child, part, :, target - base:target - base + width] = ref[
                    part, taken, source:source + width
                ]
    edge = jnp.zeros((2, 2, window, LANES), jnp.bfloat16)
    if base < 0:
        wide_ref[:, :, :, 0:LANES] = edge
    if stop + LANES > length:
        wide_ref[:, :, :, stop - base:stop - base + LANES] = edge
    span = stop - start
    tiles = pl.cdiv(span, TILE)
    other = pl.ds(pl.multiple_of((1 - following) * (beams - window), 16), window)
    lane = lax.broadcasted_iota(jnp.int32, (2 * window, LANES), 1).astype(jnp.int16)
    moves = []
    for child in range(2):
        for tap in range(rtaps):
            shift = shifts[child] + (tap - 1 + LANES)
            part_tile = lax.rem(shift, LANES)
            kept = jnp.full((2 * window, LANES), LANES - part_tile, jnp.int32).astype(jnp.int16)
            turn = lax.rem(LANES - part_tile, LANES)
            moves.append((child, tap, shift // LANES * LANES, turn, lane < kept))

    def rolled(child, at, turn):
        piece = wide_ref[child, :, :, pl.ds(pl.multiple_of(at, LANES), LANES)]
        return pltpu.roll(piece.reshape(2 * window, LANES), turn, 1)

    def build(stack_ref, step):
        for number, (child, tap, whole, turn, kept) in enumerate(moves):
            place = (child * rtaps + tap) * 2 * window
            held = held_ref[number]
            for block in range(TILE // LANES):
                piece = rolled(child, step * TILE + whole + (block + 1) * LANES, turn)
                columns = pl.ds(block * LANES, LANES)
                stack_ref[place:place + 2 * window, columns] = jnp.where(kept, held, piece)
                held = piece
            held_ref[number] = held

    def multiply(stack_ref, step, width=TILE):
        column = pl.multiple_of(step * TILE, TILE)
        both = jnp.dot(mix_ref[level], stack_ref[...], preferred_element_type=jnp.float32)
        total = (both[:2 * beams] + both[2 * beams:]).astype(jnp.bfloat16)
        out_ref[:, :, pl.ds(column, TILE)] = total.reshape(2, beams, TILE)
        if not last:
            send_ref[:, :, pl.ds(column, width)] = out_ref[:, other, pl.ds(column, width)]

    def two_tiles(pair, carry):
        build(odd_ref, 2 * pair + 1)
        multiply(even_ref, 2 * pair)
        build(even_ref, 2 * pair + 2)
        multiply(odd_ref, 2 * pair + 1)
        return carry

    for number, (child, tap, whole, turn, kept) in enumerate(moves):
        held_ref[number] = rolled(child, whole, turn)
    build(even_ref, 0)
    lax.fori_loop(0, (tiles - 1) // 2, two_tiles, 0)
    if tiles % 2 == 1:
        multiply(even_ref, tiles - 1, span - (tiles - 1) * TILE)
    else:
        build(odd_ref, tiles - 1)
        multiply(even_ref, tiles - 2)
        multiply(odd_ref, tiles - 1, span - (tiles - 1) * TILE)


def pieces_of(bounds, start, stop):
    found = []
    for chunk in range(len(bounds) - 1):
        low, high = max(bounds[chunk], start), min(bounds[chunk + 1], stop)
        if low < high:
            found.append((chunk, low - bounds[chunk], low, high - low))
    return found


def merge(level, levels, codes, mix, own, far, bounds, start, stop, sizes, before):
    beams, window, rtaps, length = sizes
    last = level == levels - 1
    plan = pieces_of(bounds, max(start - LANES, 0), min(stop + LANES, length))
    span = stop - start
    vmem = pl.BlockSpec(memory_space=pltpu.VMEM)
    anywhere = pl.BlockSpec(memory_space=pl.ANY)
    depth = mix.shape[2]
    padded = pl.cdiv(span, TILE) * TILE
    out_shape = [jax.ShapeDtypeStruct((2, beams, padded), jnp.bfloat16)]
    if not last:
        out_shape.append(jax.ShapeDtypeStruct((2, window, span), jnp.bfloat16))
    return pl.pallas_call(
        functools.partial(
            merge_kernel, level, plan, start, stop, length, beams, window, rtaps, last
        ),
        out_shape=out_shape,
        in_specs=[vmem, vmem] + [vmem] * (2 * len(plan)) + [anywhere],
        out_specs=[vmem] * len(out_shape),
        scratch_shapes=[
            pltpu.VMEM((2, 2, window, padded + TILE + 2 * LANES), jnp.bfloat16),
            pltpu.VMEM((depth, TILE), jnp.bfloat16),
            pltpu.VMEM((depth, TILE), jnp.bfloat16),
            pltpu.VMEM((2 * rtaps, 2 * window, LANES), jnp.bfloat16),
        ],
        compiler_params=pltpu.CompilerParams(vmem_limit_bytes=24 * 2**20),
        cost_estimate=pl.CostEstimate(
            flops=(8 if last else 32) * beams * depth * span,
            bytes_accessed=0,
            transcendentals=0,
        ),
        name=f"merge_{level}",
    )(
        codes,
        mix,
        *[own[piece[0]] for piece in plan],
        *[far[piece[0]] for piece in plan],
        before,
    )


MARKS = (
    (8, 16),
    (7, 15, 21, 28),
    (6, 14, 20, 27),
    (5, 13, 19, 26),
)
ORDER = (
    (0, 0), (0, 1), (0, 2), (1, 0), (1, 1), (2, 0), (1, 2), (2, 1), (1, 3), (3, 0), (1, 4),
    (2, 2), (3, 1), (2, 3), (2, 4), (3, 2), (3, 3), (3, 4),
)


def chunk_bounds(level, levels, length):
    marks = MARKS[len(MARKS) - 1 - min(levels - level, len(MARKS) - 1)]
    tiles = length // LANES
    return [0] + [tiles * mark // 32 * LANES for mark in marks] + [length]


def merge_order(levels, bounds):
    if levels == len(MARKS):
        return ORDER
    length = bounds[0][-1]
    made = [0] * levels
    order = []
    while len(order) < sum(len(bound) - 1 for bound in bounds[1:]):
        ready = []
        for level in range(levels):
            chunk = made[level]
            if chunk < len(bounds[level + 1]) - 1:
                stop = min(bounds[level + 1][chunk + 1] + LANES, length)
                needed = len(pieces_of(bounds[level], 0, stop))
                if level == 0 or needed <= made[level - 1]:
                    ready.append((level + chunk, level, chunk))
        _, level, chunk = min(ready)
        made[level] += 1
        order.append((level, chunk))
    return order


def from_partner(value, bit):
    mask = 1 << bit
    pairs = [(source, source ^ mask) for source in range(lax.axis_size("pulse"))]
    return lax.ppermute(value, "pulse", pairs)


def on_device(beams_in, ukern, rkern, angles, taps, shifts, half_table):
    beams, length = beams_in.shape[1:]
    utaps, rtaps = ukern.shape[1], rkern.shape[1]
    window = beams // 2 + utaps // 2
    levels = half_table.shape[0]
    sizes = (beams, window, rtaps, length)
    bounds = [[0, length]]
    bounds += [chunk_bounds(level, levels, length) for level in range(1, levels + 1)]
    mix, codes = mixing(ukern, rkern, angles, taps, shifts, half_table)
    owns = [[beams_in]] + [[None] * (len(bound) - 1) for bound in bounds[1:]]
    fars = [[from_partner(beams_in, 0)]] + [[None] * (len(bound) - 1) for bound in bounds[1:]]
    before = mix
    for level, chunk in merge_order(levels, bounds):
        start, stop = bounds[level + 1][chunk], bounds[level + 1][chunk + 1]
        done = merge(
            level, levels, codes, mix, owns[level], fars[level], bounds[level],
            start, stop, sizes, before,
        )
        before = owns[level + 1][chunk] = done[0]
        if level < levels - 1:
            fars[level + 1][chunk] = from_partner(done[1], level + 1)
    edges = bounds[levels]
    made = [part[:, :, :high - low] for part, low, high in zip(owns[levels], edges, edges[1:])]
    return jnp.concatenate(made, axis=2)


def solution(mesh):
    in_specs = (
        P(None, ("scene", "pulse"), None),
        P(),
        P(),
        P(),
        P(None, ("scene", "pulse")),
        P(),
        P(),
    )
    out_specs = P(None, ("scene", "pulse"), None)
    return jax.shard_map(
        on_device, mesh=mesh, in_specs=in_specs, out_specs=out_specs, check_vma=False
    )
```
